32 devices in a mesh: parts: 2 (over x), row: 8 (over z, y), col: 2 (over core).
Axes of the slice: x: 2, y: 2, z: 4, core: 2. Of those that a mesh axis runs over, the one named last changes fastest.
Arguments:
- density_real: float32 [32, 3, 128, 128], P(('row', 'col')), may hold values from -4 to 4, as said below
- density_imag: float32 [32, 3, 128, 128], P(('row', 'col')), may hold values from -4 to 4, as said below
- hamiltonian: float32 [32, 3, 128, 128], P(('row', 'col')), may hold values from -0.30618622 to 0.30618622, as said below
- dipole: float32 [64, 3, 128, 128], P(('parts', 'row', 'col')), parts along dimension 0, may hold values from -0.15309311 to 0.15309311, as said below
- field: float32 [2], P('parts'), parts along dimension 0, may hold values from 0.5 to 1.5
- pattern: int32 [6, 32, 3], P(None, ('row', 'col')), may hold values from 0 to 1, as said below
Outputs:
- final_real: float32 [64, 3, 128, 128], P(('parts', 'row', 'col')), parts along dimension 0
- final_imag: float32 [64, 3, 128, 128], P(('parts', 'row', 'col')), parts along dimension 0
The draws below stay inside these ranges and needn't reach their ends.
There are 2 independent parts, one for each index of `parts`. The reference program is written for one: setup_inputs(seed, part) draws one part's arguments, and reference() takes and returns one part's arrays. A program takes and returns all parts, laid end to end along the dimension named above; an argument that names none is the same for every part. Nothing has to cross between parts.
Inputs may be any that keep to these rules, and one draw needn't show every extreme that they name: Blocks of the density's real part form a symmetric matrix: density_real[i, 1 + d] is the transpose of density_real[i + d mod 32, 1 - d] for d = 1 .. 1, and each density_real[i, 1] is symmetric. Blocks of the imaginary part form an antisymmetric matrix: density_imag[i, 1 + d] is minus the transpose of density_imag[i + d mod 32, 1 - d] for d = 1 .. 1, and each density_imag[i, 1] is antisymmetric. `hamiltonian`: symmetric in the same sense as density_real. `dipole`: symmetric in the same sense as density_real. pattern[t, i, 1] = 1 and pattern[t, i, 1 + d] = pattern[t, i + d mod 32, 1 - d] for d = 1 .. 1.
All inputs are finite; a program needn't handle non-finite values.
Results may differ from the reference program's by a relative error of at most 0.00022.
Values sent between devices are 32-bit elements; how exact they have to be, the bound alone decides.
No kernel may reach another device: no remote copies, remote signals or barrier semaphores. Data moves between devices by JAX's collectives and lax.ppermute only.
A program may use at most 64 MiB of HBM per device.

```python
import math
import jax
import jax.numpy as jnp
from jax import lax

BS = 128
BAND = 3
STEPS = 1
TERMS = 6
NB = 32


def fold_band(raw_tiles, sign_value):
    half_band = (BAND - 1) // 2
    lower_list = [raw_tiles[:, index] for index in range(half_band)]
    diagonal_tiles = (raw_tiles[:, half_band] + sign_value * jnp.swapaxes(raw_tiles[:, half_band], -1, -2)) / math.sqrt(2.0)
    upper_list = []
    for offset_up in range(1, half_band + 1):
        source = lower_list[half_band - offset_up]
        upper_list.append(sign_value * jnp.swapaxes(jnp.roll(source, -offset_up, axis=0), -1, -2))
    return jnp.stack(lower_list + [diagonal_tiles] + upper_list, axis=1)


def raw_normal(key, scale_value):
    return jax.random.truncated_normal(key, -4.0, 4.0, (NB, (BAND + 1) // 2, BS, BS), jnp.float32) * scale_value


def draw_density_real(key, part):
    key = jax.random.fold_in(key, 11)
    raw_tiles = raw_normal(key, 0.6)
    return fold_band(raw_tiles, 1.0)


def draw_density_imag(key, part):
    key = jax.random.fold_in(key, 12)
    raw_tiles = raw_normal(key, 0.6)
    return fold_band(raw_tiles, -1.0)


def draw_hamiltonian(key, part):
    key = jax.random.fold_in(key, 13)
    raw_tiles = raw_normal(key, (BAND * BS) ** (-0.5))
    return fold_band(raw_tiles, 1.0)


def draw_dipole(key, part):
    key = jax.random.fold_in(key, 14)
    raw_tiles = raw_normal(key, 0.5 * (BAND * BS) ** (-0.5))
    return fold_band(raw_tiles, 1.0)


def draw_pattern(key, part):
    key = jax.random.fold_in(key, 17)
    half_band = (BAND - 1) // 2
    kept = (jax.random.randint(key, (STEPS * TERMS, NB, half_band), 0, 4) < 3).astype(jnp.int32)
    lower_list = [kept[:, :, index] for index in range(half_band)]
    upper_list = []
    for offset_up in range(1, half_band + 1):
        upper_list.append(jnp.roll(lower_list[half_band - offset_up], -offset_up, axis=1))
    kept_middle = jnp.ones((STEPS * TERMS, NB), jnp.int32)
    return jnp.stack(lower_list + [kept_middle] + upper_list, axis=2)


def setup_inputs(seed: int = 0, part: int = 0) -> dict:
    streams_of = jax.random.split(jax.random.key(seed), 7)
    own_keys = jax.random.split(jax.random.fold_in(streams_of[6], part), 7)
    return {
        "density_real": draw_density_real(jax.random.fold_in(streams_of[6], 71), part),
        "density_imag": draw_density_imag(jax.random.fold_in(streams_of[6], 71), part),
        "hamiltonian": draw_hamiltonian(jax.random.fold_in(streams_of[6], 71), part),
        "dipole": draw_dipole(jax.random.fold_in(jax.random.fold_in(streams_of[6], part), 71), part),
        "field": jnp.clip(jax.random.uniform(own_keys[4], (STEPS,), jnp.float32, 0.5, 1.5), 0.5, 1.5),
        "pattern": draw_pattern(jax.random.fold_in(streams_of[6], 71), part),
    }


time_step = 0.5


def banded_product(left_band, right_band):
    half_band = (left_band.shape[1] - 1) // 2
    outputs = []
    for offset_out in range(-half_band, half_band + 1):
        accumulated = jnp.zeros_like(left_band[:, 0])
        for offset_mid in range(-half_band, half_band + 1):
            if abs(offset_out - offset_mid) <= half_band:
                shifted = jnp.roll(right_band, -offset_mid, axis=0)[:, offset_out - offset_mid + half_band]
                accumulated = accumulated + jnp.einsum("nab,nbc->nac", left_band[:, offset_mid + half_band], shifted, precision=lax.Precision.HIGHEST)
        outputs.append(accumulated)
    return jnp.stack(outputs, axis=1)


def reference(density_real, density_imag, hamiltonian, dipole, field, pattern):
    series_real = density_real
    series_imag = density_imag
    for step_index in range(STEPS):
        operator_now = hamiltonian + field[step_index] * dipole
        current_real = series_real
        current_imag = series_imag
        for order_index in range(TERMS):
            coefficient = time_step / (order_index + 1)
            keep_mask = pattern[step_index * TERMS + order_index].astype(jnp.float32)[:, :, None, None]
            comm_real = banded_product(operator_now, current_real) - banded_product(current_real, operator_now)
            comm_imag = banded_product(operator_now, current_imag) - banded_product(current_imag, operator_now)
            current_real = coefficient * keep_mask * comm_imag
            current_imag = -(coefficient * keep_mask * comm_real)
            series_real = series_real + current_real
            series_imag = series_imag + current_imag
    return series_real, series_imag
```

```python
import functools

import jax
import jax.numpy as jnp
from jax import lax
from jax.experimental import pallas as pl
from jax.experimental.pallas import tpu as pltpu
from jax.sharding import PartitionSpec as P

TERMS = 6
BS = 128
time_step = 0.5
RING = ("row", "col")
f32, bf16 = jnp.float32, jnp.bfloat16

ROWS = 6
SIGN_RE = (1.0, -1.0, -1.0, 1.0, 1.0, -1.0)
SIGN_IM = (-1.0, -1.0, 1.0, 1.0, -1.0, -1.0)
PAYLOAD_ROWS = 7 * BS + 8


def own_index(row, offset):
    core = lax.axis_index("col")
    return jnp.where(core == 0, row, 1 - row), jnp.where(core == 0, 1 + offset, 1 - offset)


def own(ref, row, offset):
    r, e = own_index(row, offset)
    return ref[r, e]


def slot(ref, index):
    return ref[index * BS : (index + 1) * BS, :]


class Band:
    def __init__(self, high, low):
        self.high, self.low = high, low

    def put(self, i, j, value):
        part = slice((j - i + 1) * BS, (j - i + 2) * BS)
        high = value.astype(bf16)
        self.high[i, :, part] = high
        self.low[i, :, part] = (value - high.astype(f32)).astype(bf16)

    def put_parts(self, i, j, high, low):
        part = slice((j - i + 1) * BS, (j - i + 2) * BS)
        self.high[i, :, part] = high
        self.low[i, :, part] = low

    def get_parts(self, i, j):
        part = slice((j - i + 1) * BS, (j - i + 2) * BS)
        return self.high[i, :, part], self.low[i, :, part]

    def left(self, i, first, last):
        part = slice((first - i + 1) * BS, (last - i + 2) * BS)
        high, low = self.high[i, :, part], self.low[i, :, part]
        return [high, high, low]

    def right(self, first, last, j):
        highs, lows = [], []
        for k in range(first, last + 1):
            part = slice((j - k + 1) * BS, (j - k + 2) * BS)
            highs.append(self.high[k, :, part])
            lows.append(self.low[k, :, part])
        return highs + lows + highs


def commute(h, hn, x, i, first, last, j):
    left = jnp.concatenate(h.left(i, first, last) + x.left(i, first, last), axis=1)
    right = jnp.concatenate(x.right(first, last, j) + hn.right(first, last, j), axis=0)
    return jnp.dot(left, right, preferred_element_type=f32)


def diagonal(h, hn, x, i, scale):
    return commute(h, hn, x, i, i - 1, i + 1, i) * scale


def edge(h, hn, x, i, scale):
    return (
        commute(h, hn, x, i, i, i + 1, i + 1) * scale,
        commute(h, hn, x, i + 1, i, i + 1, i) * scale,
    )


def put_h(h, hn, i, j, value):
    h.put(i, j, value)
    high, low = h.get_parts(i, j)
    hn.put_parts(i, j, -high, -low)


def coefficient(term):
    return time_step / (term + 1)


def own_scale(pattern, term, row, offset):
    r, e = own_index(row, offset)
    return pattern[term, r, e].astype(f32) * coefficient(term)


def pack_kernel(re, im, ham, dip, field, pattern, out):
    f = field[0]
    for index, (row, offset) in enumerate(((0, 0), (0, 1), (1, -1), (1, 0))):
        out[index * BS : (index + 1) * BS, :] = own(re, row, offset) + own(im, row, offset)
    for index, (row, offset) in enumerate(((0, 0), (0, 1), (1, 0))):
        out[(4 + index) * BS : (5 + index) * BS, :] = own(ham, row, offset) + f * own(dip, row, offset)
    for term in range(TERMS):
        out[7 * BS + term : 7 * BS + term + 1, :] = jnp.full((1, BS), own_scale(pattern, term, 0, 1), f32)


def place_h_inner(h, hn, ham, dip, f, near):
    def op(row, offset):
        return own(ham, row, offset) + f * own(dip, row, offset)

    put_h(h, hn, 2, 2, op(0, 0))
    put_h(h, hn, 3, 3, op(1, 0))
    put_h(h, hn, 2, 3, op(0, 1))
    put_h(h, hn, 3, 2, op(1, -1))
    below = op(0, -1)
    put_h(h, hn, 2, 1, below)
    put_h(h, hn, 1, 2, below.T)
    above = op(1, 1)
    put_h(h, hn, 3, 4, above)
    put_h(h, hn, 4, 3, above.T)
    put_h(h, hn, 4, 4, slot(near, 6))
    put_h(h, hn, 5, 5, slot(near, 4))
    put_h(h, hn, 5, 4, slot(near, 5))
    put_h(h, hn, 4, 5, slot(near, 5).T)


def inner_levels(h, hn, xs, base, near, pattern, record):
    def put(level, i, j, value):
        record(level, i, j, value)
        if level < 3:
            xs[level].put(i, j, value)

    def own_edge(level, i):
        term = base + level - 1
        up, down = edge(h, hn, xs[level - 1], i, own_scale(pattern, term, i - 2, 1))
        put(level, i, i + 1, up)
        put(level, i + 1, i, down)

    def own_diagonal(level, i):
        put(level, i, i, diagonal(h, hn, xs[level - 1], i, coefficient(base + level - 1)))

    own_edge(1, 2)
    own_diagonal(1, 3)
    own_edge(1, 3)
    own_diagonal(1, 4)
    row = 7 * BS + base
    up, down = edge(h, hn, xs[0], 4, near[row : row + 1, :])
    put(1, 4, 5, up)
    put(1, 5, 4, down)
    own_diagonal(1, 2)
    own_edge(2, 2)
    own_diagonal(2, 3)
    own_edge(2, 3)
    own_diagonal(2, 4)
    own_diagonal(3, 3)
    own_edge(3, 3)


KEPT_X = ((0, 2, 2), (0, 1, 2), (0, 2, 1), (1, 2, 2), (1, 2, 3), (1, 3, 2), (2, 2, 3), (2, 3, 2), (2, 3, 3))
KEPT_H = ((2, 2), (1, 2), (2, 1), (2, 3), (3, 2), (3, 3))
INNER_TERMS = (
    (1, 2, 2), (1, 3, 3), (1, 2, 3), (1, 3, 2), (1, 3, 4), (1, 4, 3),
    (2, 3, 3), (2, 2, 3), (2, 3, 2), (2, 3, 4), (2, 4, 3),
    (3, 3, 3), (3, 3, 4), (3, 4, 3),
)
OUTER_TERMS = (
    (1, 2, 1), (1, 1, 2), (2, 2, 1), (2, 1, 2), (2, 2, 2),
    (3, 2, 1), (3, 1, 2), (3, 2, 2), (3, 2, 3), (3, 3, 2),
)


def keep(kept, h, xs):
    for index, (level, i, j) in enumerate(KEPT_X):
        high, low = xs[level].get_parts(i, j)
        kept[index, 0], kept[index, 1] = high, low
    for index, (i, j) in enumerate(KEPT_H):
        high, low = h.get_parts(i, j)
        kept[len(KEPT_X) + index, 0], kept[len(KEPT_X) + index, 1] = high, low


def bands(scratch):
    h_high, h_low, hn_high, hn_low, x_high, x_low = scratch
    h, hn = Band(h_high, h_low), Band(hn_high, hn_low)
    xs = [Band(x_high.at[level], x_low.at[level]) for level in range(3)]
    return h, hn, xs


def band_scratch():
    one = pltpu.VMEM((ROWS, BS, 3 * BS), bf16)
    three = pltpu.VMEM((3, ROWS, BS, 3 * BS), bf16)
    return [one, one, one, one, three, three]


def inner_first(re, im, ham, dip, near, field, pattern, kept, terms, *scratch):
    h, hn, xs = bands(scratch)
    place_h_inner(h, hn, ham, dip, field[0], near)
    x0 = xs[0]
    for (i, j), (row, offset) in (((2, 2), (0, 0)), ((3, 3), (1, 0)), ((2, 3), (0, 1)), ((3, 2), (1, -1))):
        x0.put(i, j, own(re, row, offset) + own(im, row, offset))
    x0.put(2, 1, own(re, 0, -1) + own(im, 0, -1))
    x0.put(1, 2, (own(re, 0, -1) - own(im, 0, -1)).T)
    x0.put(3, 4, own(re, 1, 1) + own(im, 1, 1))
    x0.put(4, 3, (own(re, 1, 1) - own(im, 1, 1)).T)
    for (i, j), index in (((4, 4), 3), ((5, 5), 0), ((4, 5), 2), ((5, 4), 1)):
        x0.put(i, j, slot(near, index))

    def record(level, i, j, value):
        if (level, i, j) in INNER_TERMS:
            terms[INNER_TERMS.index((level, i, j))] = value

    inner_levels(h, hn, xs, 0, near, pattern, record)
    keep(kept, h, xs)


def outer_levels(h, hn, xs, base, far, far_scales, kept, pattern, record):
    for index, (level, i, j) in enumerate(KEPT_X):
        xs[level].put_parts(i, j, kept[index, 0], kept[index, 1])
    for index, (i, j) in enumerate(KEPT_H):
        high, low = kept[len(KEPT_X) + index, 0], kept[len(KEPT_X) + index, 1]
        h.put_parts(i, j, high, low)
        hn.put_parts(i, j, -high, -low)
    put_h(h, hn, 1, 1, slot(far_scales, 4))
    put_h(h, hn, 0, 0, slot(far_scales, 6))
    put_h(h, hn, 1, 0, slot(far_scales, 5))
    put_h(h, hn, 0, 1, slot(far_scales, 5).T)
    for (i, j), index in (((1, 1), 0), ((0, 0), 3), ((1, 0), 1), ((0, 1), 2)):
        xs[0].put(i, j, slot(far, index))

    def put(level, i, j, value):
        record(level, i, j, value)
        if level < 3:
            xs[level].put(i, j, value)

    def do_edge(level, i, scale):
        up, down = edge(h, hn, xs[level - 1], i, scale)
        put(level, i, i + 1, up)
        put(level, i + 1, i, down)

    def do_diagonal(level, i):
        put(level, i, i, diagonal(h, hn, xs[level - 1], i, coefficient(base + level - 1)))

    row = 7 * BS + base
    cross = [own_scale(pattern, base + n, 0, -1) for n in range(3)]
    do_edge(1, 0, far_scales[row : row + 1, :])
    do_diagonal(1, 1)
    do_edge(1, 1, cross[0])
    do_diagonal(2, 1)
    do_edge(2, 1, cross[1])
    do_diagonal(2, 2)
    do_edge(3, 1, cross[2])
    do_diagonal(3, 2)
    do_edge(3, 2, own_scale(pattern, base + 2, 0, 1))


def outer_first(far, kept, inner_terms, pattern, state, terms, *scratch):
    h, hn, xs = bands(scratch)

    def record(level, i, j, value):
        if (level, i, j) in OUTER_TERMS:
            terms[OUTER_TERMS.index((level, i, j))] = value
        if level == 3 and (i, j) in ((2, 2), (2, 3), (3, 2)):
            index = ((2, 2), (2, 3), (3, 2)).index((i, j))
            state[index * BS : (index + 1) * BS, :] = value

    outer_levels(h, hn, xs, 0, far, far, kept, pattern, record)
    state[3 * BS : 4 * BS, :] = inner_terms[INNER_TERMS.index((3, 3, 3))]


def weighted(terms_of, signs):
    total = None
    for sign, value in zip(signs, terms_of):
        total = (value if sign > 0 else -value) if total is None else (total + value if sign > 0 else total - value)
    return total


def parts_of(values, i, j, levels, base):
    re_signs = [SIGN_RE[base + level - 1] for level in levels]
    im_signs = [SIGN_IM[base + level - 1] for level in levels]
    here = [values[(level, i, j)] for level in levels]
    there = here if i == j else [values[(level, j, i)] for level in levels]
    real = 0.5 * (weighted(here, re_signs) + weighted(there, re_signs).T)
    imag = 0.5 * (weighted(here, im_signs) - weighted(there, im_signs).T)
    return real, imag


def inner_second(
    re, im, ham, dip, near, state, near_state, terms_a, terms_b, field, pattern, kept, out_re, out_im, *scratch
):
    h, hn, xs = bands(scratch)
    place_h_inner(h, hn, ham, dip, field[0], near)
    x0 = xs[0]
    for (i, j), index in (((2, 2), 0), ((2, 3), 1), ((3, 2), 2), ((3, 3), 3)):
        x0.put(i, j, slot(state, index))
    for (i, j), index in (((4, 4), 3), ((5, 5), 0), ((4, 5), 2), ((5, 4), 1)):
        x0.put(i, j, slot(near_state, index))
    for i, j in ((3, 4), (4, 3)):
        x0.put(i, j, terms_a[INNER_TERMS.index((3, i, j))])
    for i, j in ((2, 1), (1, 2)):
        x0.put(i, j, terms_b[OUTER_TERMS.index((3, i, j))])

    values = {}

    def record(level, i, j, value):
        values[(level, i, j)] = value

    inner_levels(h, hn, xs, 3, near, pattern, record)
    keep(kept, h, xs)

    first = {}
    for index, key in enumerate(INNER_TERMS):
        first[key] = terms_a[index]
    for index, key in enumerate(OUTER_TERMS):
        first[key] = terms_b[index]

    def finish(row, offset, i, j, levels):
        r, e = own_index(row, offset)
        real, imag = parts_of(first, i, j, (1, 2, 3), 0)
        real, imag = re[r, e] + real, im[r, e] + imag
        if levels:
            more_real, more_imag = parts_of(values, i, j, levels, 3)
            real, imag = real + more_real, imag + more_imag
        out_re[r, e], out_im[r, e] = real, imag

    finish(0, -1, 2, 1, ())
    finish(0, 0, 2, 2, (1,))
    finish(0, 1, 2, 3, (1, 2))
    finish(1, -1, 3, 2, (1, 2))
    finish(1, 0, 3, 3, (1, 2, 3))
    finish(1, 1, 3, 4, (1, 2, 3))


def outer_second(far, far_state, kept, base_re, base_im, pattern, out_re, out_im, *scratch):
    h, hn, xs = bands(scratch)
    values = {}

    def record(level, i, j, value):
        values[(level, i, j)] = value

    outer_levels(h, hn, xs, 3, far_state, far, kept, pattern, record)

    def finish(row, offset, i, j, levels):
        r, e = own_index(row, offset)
        if levels:
            real, imag = parts_of(values, i, j, levels, 3)
            out_re[r, e], out_im[r, e] = base_re[r, e] + real, base_im[r, e] + imag
        else:
            out_re[r, e], out_im[r, e] = base_re[r, e], base_im[r, e]

    finish(0, -1, 2, 1, (1, 2, 3))
    finish(0, 0, 2, 2, (2, 3))
    finish(0, 1, 2, 3, (3,))
    finish(1, -1, 3, 2, (3,))
    finish(1, 0, 3, 3, ())
    finish(1, 1, 3, 4, ())


VECTOR = pl.BlockSpec(memory_space=pltpu.VMEM)
SCALAR = pl.BlockSpec(memory_space=pltpu.SMEM)


def call(kernel, specs, outs, scratch, flops):
    many = isinstance(outs, tuple)
    return pl.pallas_call(
        kernel,
        out_shape=outs,
        in_specs=specs,
        out_specs=(VECTOR,) * len(outs) if many else VECTOR,
        scratch_shapes=scratch,
        compiler_params=pltpu.CompilerParams(vmem_limit_bytes=32 * 2**20),
        cost_estimate=pl.CostEstimate(flops=flops, bytes_accessed=4 * 2**20, transcendentals=0),
    )


def body(density_real, density_imag, hamiltonian, dipole, field, pattern):
    count = lax.axis_size(RING)
    pair = [(i, i ^ 1) for i in range(count)]
    cross = [(i, (i + 1) % count if i % 2 else (i - 1) % count) for i in range(count)]
    shape = jax.ShapeDtypeStruct
    kept_shape = shape((len(KEPT_X) + len(KEPT_H), 2, BS, BS), bf16)
    block_shape = shape(density_real.shape, f32)

    packed = call(pack_kernel, [VECTOR] * 4 + [SCALAR] * 2, shape((PAYLOAD_ROWS, BS), f32), [], 10**6)(
        density_real, density_imag, hamiltonian, dipole, field, pattern
    )
    far = lax.ppermute(packed, RING, cross)
    near = lax.ppermute(packed, RING, pair)
    kept, terms_a = call(
        inner_first,
        [VECTOR] * 5 + [SCALAR] * 2,
        (kept_shape, shape((len(INNER_TERMS), BS, BS), f32)),
        band_scratch(),
        2 * 10**9,
    )(density_real, density_imag, hamiltonian, dipole, near, field, pattern)
    state, terms_b = call(
        outer_first,
        [VECTOR] * 3 + [SCALAR],
        (shape((4 * BS, BS), f32), shape((len(OUTER_TERMS), BS, BS), f32)),
        band_scratch(),
        2 * 10**9,
    )(far, kept, terms_a, pattern)
    far_state = lax.ppermute(state, RING, cross)
    near_state = lax.ppermute(state, RING, pair)
    kept, base_re, base_im = call(
        inner_second,
        [VECTOR] * 9 + [SCALAR] * 2,
        (kept_shape, block_shape, block_shape),
        band_scratch(),
        2 * 10**9,
    )(
        density_real, density_imag, hamiltonian, dipole, near, state, near_state, terms_a, terms_b, field, pattern
    )
    return call(
        outer_second,
        [VECTOR] * 5 + [SCALAR],
        (block_shape, block_shape),
        band_scratch(),
        2 * 10**9,
    )(far, far_state, kept, base_re, base_im, pattern)


def solution(mesh):
    in_specs = (
        P(("row", "col"), None, None, None),
        P(("row", "col"), None, None, None),
        P(("row", "col"), None, None, None),
        P(("parts", "row", "col"), None, None, None),
        P("parts"),
        P(None, ("row", "col"), None),
    )
    out_specs = (
        P(("parts", "row", "col"), None, None, None),
        P(("parts", "row", "col"), None, None, None),
    )
    return jax.shard_map(body, mesh=mesh, in_specs=in_specs, out_specs=out_specs, check_vma=False)
```

```python
import functools

import jax
import jax.numpy as jnp
from jax import lax
from jax.experimental import pallas as pl
from jax.experimental.pallas import tpu as pltpu
from jax.sharding import PartitionSpec as P

TERMS = 6
BS = 128
time_step = 0.5
RING = ("row", "col")
f32, bf16 = jnp.float32, jnp.bfloat16

ROWS = 6
SIGN_RE = (1.0, -1.0, -1.0, 1.0, 1.0, -1.0)
SIGN_IM = (-1.0, -1.0, 1.0, 1.0, -1.0, -1.0)
PAYLOAD_ROWS = 7 * BS + 8


def own_index(row, offset):
    core = lax.axis_index("col")
    return jnp.where(core == 0, row, 1 - row), jnp.where(core == 0, 1 + offset, 1 - offset)


def own(ref, row, offset):
    r, e = own_index(row, offset)
    return ref[r, e]


def slot(ref, index):
    return ref[index * BS : (index + 1) * BS, :]


class Band:
    def __init__(self, high, low):
        self.high, self.low = high, low

    def put(self, i, j, value):
        part = slice((j - i + 1) * BS, (j - i + 2) * BS)
        high = value.astype(bf16)
        self.high[i, :, part] = high
        self.low[i, :, part] = (value - high.astype(f32)).astype(bf16)

    def put_parts(self, i, j, high, low):
        part = slice((j - i + 1) * BS, (j - i + 2) * BS)
        self.high[i, :, part] = high
        self.low[i, :, part] = low

    def get_parts(self, i, j):
        part = slice((j - i + 1) * BS, (j - i + 2) * BS)
        return self.high[i, :, part], self.low[i, :, part]

    def left(self, i, first, last):
        part = slice((first - i + 1) * BS, (last - i + 2) * BS)
        high, low = self.high[i, :, part], self.low[i, :, part]
        return [high, high, low]

    def right(self, first, last, j, j_last):
        highs, lows = [], []
        for k in range(first, last + 1):
            part = slice((j - k + 1) * BS, (j_last - k + 2) * BS)
            highs.append(self.high[k, :, part])
            lows.append(self.low[k, :, part])
        return highs + lows + highs


def piece(h, hn, x, rows, mids, cols):
    left = jnp.concatenate(
        [jnp.concatenate(h.left(i, *mids) + x.left(i, *mids), axis=1) for i in range(rows[0], rows[1] + 1)], axis=0
    )
    right = jnp.concatenate(x.right(*mids, *cols) + hn.right(*mids, *cols), axis=0)
    return jnp.dot(left, right, preferred_element_type=f32)


def one_side(a, b, row, mids, col):
    left = jnp.concatenate(a.left(row, *mids), axis=1)
    right = jnp.concatenate(b.right(*mids, col, col), axis=0)
    return jnp.dot(left, right, preferred_element_type=f32)


def corners(tile):
    return tile[:BS, :BS], tile[:BS, BS:], tile[BS:, :BS], tile[BS:, BS:]


def put_h(h, hn, i, j, value):
    h.put(i, j, value)
    high, low = h.get_parts(i, j)
    hn.put_parts(i, j, -high, -low)


def put_h_parts(h, hn, i, j, high, low):
    h.put_parts(i, j, high, low)
    hn.put_parts(i, j, -high, -low)


def coefficient(term):
    return time_step / (term + 1)


def own_scale(pattern, term, row, offset):
    r, e = own_index(row, offset)
    return pattern[e, r, term].astype(f32) * coefficient(term)


INNER_H = ((2, 2), (3, 3), (2, 3), (3, 2), (2, 1), (1, 2), (3, 4), (4, 3), (4, 4), (5, 5), (5, 4), (4, 5))
KEPT_X = ((0, 1, 2), (0, 2, 1), (1, 2, 2))
KEPT_H = ((1, 2), (2, 1), (2, 2), (2, 3), (3, 2))
SUMS = ((1, 1, 1), (1, 1, 2), (1, 2, 1), (2, 2, 2), (3, 2, 2), (3, 2, 3), (3, 3, 2))
OUTER_TERMS = ((1, 2, 1), (1, 1, 2), (2, 2, 1), (2, 1, 2), (3, 2, 1), (3, 1, 2), (2, 2, 2))
STATE = ((2, 2), (2, 3), (3, 2), (3, 3))


def pack_kernel(re, im, ham, dip, field, pattern, out, dens, oper, sems):
    copies = []
    for a, ref in enumerate((re, im)):
        for r in range(2):
            copies.append(pltpu.make_async_copy(ref.at[r, pl.ds(1 - r, 2)], dens.at[a, r], sems.at[len(copies)]))
    for a, ref in enumerate((ham, dip)):
        for n, (row, offset) in enumerate(((0, 0), (0, 1), (1, 0))):
            r, e = own_index(row, offset)
            copies.append(pltpu.make_async_copy(ref.at[r, e], oper.at[a, n], sems.at[len(copies)]))
    for copy in copies:
        copy.start()
    for term in range(TERMS):
        out[7 * BS + term : 7 * BS + term + 1, :] = jnp.full((1, BS), own_scale(pattern, term, 0, 1), f32)
    for copy in copies[:4]:
        copy.wait()
    for index, (row, offset) in enumerate(((0, 0), (0, 1), (1, -1), (1, 0))):
        r, e = own_index(row, offset)
        out[index * BS : (index + 1) * BS, :] = dens[0, r, e - 1 + r] + dens[1, r, e - 1 + r]
    for copy in copies[4:]:
        copy.wait()
    for n in range(3):
        out[(4 + n) * BS : (5 + n) * BS, :] = oper[0, n] + field[0] * oper[1, n]


def inner_levels(h, hn, xs, base, near, pattern, sums, record):
    def put(level, i, j, value):
        record(level, i, j, value)
        if level < 3:
            xs[level].put(i, j, value)

    def own_edge(level, i, up, down, scale=None):
        scale = own_scale(pattern, base + level - 1, i - 2, 1) if scale is None else scale
        put(level, i, i + 1, up * scale)
        put(level, i + 1, i, down * scale)

    def own_diagonal(level, i, total):
        put(level, i, i, total * coefficient(base + level - 1))

    def tile(level, i):
        return corners(piece(h, hn, xs[level - 1], (i, i + 1), (i, i + 1), (i, i + 1)))

    def part(level, i, k, j):
        return piece(h, hn, xs[level - 1], (i, i), (k, k), (j, j))

    def keep(level, i, j, value):
        sums[SUMS.index((level, i, j))] = value

    t2, t3, t4 = tile(1, 2), tile(1, 3), tile(1, 4)
    own_edge(1, 2, t2[1], t2[2])
    own_edge(1, 3, t3[1], t3[2])
    own_diagonal(1, 3, t2[3] + t3[0] - part(1, 3, 3, 3))
    own_diagonal(1, 4, t3[3] + t4[0] - part(1, 4, 4, 4))
    row = 7 * BS + base
    own_edge(1, 4, t4[1], t4[2], near[row : row + 1, :])
    own_diagonal(1, 2, part(1, 2, 1, 2) + t2[0])
    t2, t3 = tile(2, 2), tile(2, 3)
    own_edge(2, 2, t2[1], t2[2])
    own_diagonal(2, 3, t2[3] + t3[0] - part(2, 3, 3, 3))
    own_edge(2, 3, t3[1], t3[2])
    own_diagonal(2, 4, t3[3] + part(2, 4, 5, 4))
    t3 = tile(3, 3)
    own_edge(3, 3, t3[1], t3[2])
    own_diagonal(3, 3, t3[0] + part(3, 3, 2, 3))
    keep(1, 1, 1, part(1, 1, 2, 1))
    keep(1, 1, 2, part(1, 1, 2, 2))
    keep(1, 2, 1, part(1, 2, 2, 1))
    keep(2, 2, 2, part(2, 2, 3, 2))
    keep(3, 2, 2, part(3, 2, 3, 2))
    x2 = xs[2]
    keep(3, 2, 3, one_side(h, x2, 2, (2, 3), 3) + one_side(x2, hn, 2, (3, 3), 3))
    keep(3, 3, 2, one_side(h, x2, 3, (3, 3), 2) + one_side(x2, hn, 3, (2, 3), 2))


def keep_parts(kept, h, xs):
    for index, (level, i, j) in enumerate(KEPT_X):
        kept[index, 0], kept[index, 1] = xs[level].get_parts(i, j)
    for index, (i, j) in enumerate(KEPT_H):
        kept[len(KEPT_X) + index, 0], kept[len(KEPT_X) + index, 1] = h.get_parts(i, j)


def bands(scratch):
    h_high, h_low, hn_high, hn_low, x_high, x_low = scratch
    h, hn = Band(h_high, h_low), Band(hn_high, hn_low)
    xs = [Band(x_high.at[level], x_low.at[level]) for level in range(3)]
    return h, hn, xs


def band_scratch():
    one = pltpu.VMEM((ROWS, BS, 3 * BS), bf16)
    three = pltpu.VMEM((3, ROWS, BS, 3 * BS), bf16)
    return [one, one, one, one, three, three]


def weighted(terms_of, signs):
    total = None
    for sign, value in zip(signs, terms_of):
        total = (value if sign > 0 else -value) if total is None else (total + value if sign > 0 else total - value)
    return total


def parts_of(values, i, j, terms):
    re_signs, im_signs = [SIGN_RE[term] for term in terms], [SIGN_IM[term] for term in terms]
    here = [values[(term, i, j)] for term in terms]
    there = here if i == j else [values[(term, j, i)] for term in terms]
    real = 0.5 * (weighted(here, re_signs) + weighted(there, re_signs).T)
    imag = 0.5 * (weighted(here, im_signs) - weighted(there, im_signs).T)
    return real, imag


OWN = (((0, -1), (2, 1)), ((0, 0), (2, 2)), ((0, 1), (2, 3)), ((1, -1), (3, 2)), ((1, 0), (3, 3)), ((1, 1), (3, 4)))
INNER_DONE = {(2, 1): (), (2, 2): (1,), (2, 3): (1, 2), (3, 2): (1, 2), (3, 3): (1, 2, 3), (3, 4): (1, 2, 3)}
OUTER_DONE = {(2, 1): (1, 2, 3), (2, 2): (2, 3), (2, 3): (3,), (3, 2): (3,)}


def inner_first(
    re, im, ham, dip, near, field, pattern, kept, sums, h_kept, base, state, re_in, im_in, ham_in, dip_in, sems, *scratch
):
    copies = [
        pltpu.make_async_copy(source, target, sems.at[n])
        for n, (source, target) in enumerate(((ham, ham_in), (dip, dip_in), (re, re_in), (im, im_in)))
    ]
    for copy in copies:
        copy.start()
    h, hn, xs = bands(scratch)
    x0 = xs[0]
    put_h(h, hn, 4, 4, slot(near, 6))
    put_h(h, hn, 5, 5, slot(near, 4))
    put_h(h, hn, 5, 4, slot(near, 5))
    put_h(h, hn, 4, 5, slot(near, 5).T)
    for (i, j), index in (((4, 4), 3), ((5, 5), 0), ((4, 5), 2), ((5, 4), 1)):
        x0.put(i, j, slot(near, index))
    for copy in copies:
        copy.wait()
    for (row, offset), (i, j) in OWN:
        value = own(ham_in, row, offset) + field[0] * own(dip_in, row, offset)
        put_h(h, hn, i, j, value)
        if (j, i) in ((1, 2), (4, 3)):
            put_h(h, hn, j, i, value.T)
        real, imag = own(re_in, row, offset), own(im_in, row, offset)
        x0.put(i, j, real + imag)
        if (j, i) in ((1, 2), (4, 3)):
            x0.put(j, i, (real - imag).T)

    values = {}

    def record(level, i, j, value):
        values[(level - 1, i, j)] = value
        if level == 3:
            if (i, j) == (3, 3):
                state[0] = value
            if (i, j) == (3, 4):
                state[1] = value
            if (i, j) == (4, 3):
                state[2] = value

    inner_levels(h, hn, xs, 0, near, pattern, sums, record)
    keep_parts(kept, h, xs)
    for index, (i, j) in enumerate(INNER_H):
        h_kept[index, 0], h_kept[index, 1] = h.get_parts(i, j)
    for index, ((row, offset), (i, j)) in enumerate(OWN):
        real, imag = own(re_in, row, offset), own(im_in, row, offset)
        terms = [level - 1 for level in INNER_DONE[(i, j)]]
        if terms:
            more_real, more_imag = parts_of(values, i, j, terms)
            real, imag = real + more_real, imag + more_imag
        base[index, 0], base[index, 1] = real, imag


def outer_levels(h, hn, xs, base, far, far_payload, kept, sums, pattern, record):
    for index, (level, i, j) in enumerate(KEPT_X):
        xs[level].put_parts(i, j, kept[index, 0], kept[index, 1])
    for index, (i, j) in enumerate(KEPT_H):
        put_h_parts(h, hn, i, j, kept[len(KEPT_X) + index, 0], kept[len(KEPT_X) + index, 1])
    put_h(h, hn, 1, 1, slot(far_payload, 4))
    put_h(h, hn, 0, 0, slot(far_payload, 6))
    put_h(h, hn, 1, 0, slot(far_payload, 5))
    put_h(h, hn, 0, 1, slot(far_payload, 5).T)
    for (i, j), index in (((1, 1), 0), ((0, 0), 3), ((1, 0), 1), ((0, 1), 2)):
        xs[0].put(i, j, slot(far, index))

    def put(level, i, j, value):
        record(level, i, j, value)
        if level < 3:
            xs[level].put(i, j, value)

    def part(level, i, k, j):
        return piece(h, hn, xs[level - 1], (i, i), (k, k), (j, j))

    def tile(level, i):
        return corners(piece(h, hn, xs[level - 1], (i, i + 1), (i, i + 1), (i, i + 1)))

    def known(level, i, j):
        return sums[SUMS.index((level, i, j))]

    row = 7 * BS + base
    cross = [own_scale(pattern, base + n, 0, -1) for n in range(3)]
    c = [coefficient(base + n) for n in range(3)]
    t0 = tile(1, 0)
    scale = far_payload[row : row + 1, :]
    put(1, 0, 1, t0[1] * scale)
    put(1, 1, 0, t0[2] * scale)
    put(1, 1, 1, (t0[3] + known(1, 1, 1)) * c[0])
    put(1, 1, 2, (part(1, 1, 1, 2) + known(1, 1, 2)) * cross[0])
    put(1, 2, 1, (part(1, 2, 1, 1) + known(1, 2, 1)) * cross[0])
    t1 = tile(2, 1)
    put(2, 1, 1, (part(2, 1, 0, 1) + t1[0]) * c[1])
    put(2, 1, 2, t1[1] * cross[1])
    put(2, 2, 1, t1[2] * cross[1])
    put(2, 2, 2, (t1[3] + known(2, 2, 2)) * c[1])
    t1 = tile(3, 1)
    put(3, 1, 2, t1[1] * cross[2])
    put(3, 2, 1, t1[2] * cross[2])
    put(3, 2, 2, (t1[3] + known(3, 2, 2)) * c[2])
    scale = own_scale(pattern, base + 2, 0, 1)
    put(3, 2, 3, (one_side(xs[2], hn, 2, (2, 2), 3) + known(3, 2, 3)) * scale)
    put(3, 3, 2, (one_side(h, xs[2], 3, (2, 2), 2) + known(3, 3, 2)) * scale)


def outer_first(far, kept, sums, inner_state, pattern, state, terms, *scratch):
    h, hn, xs = bands(scratch)

    def record(level, i, j, value):
        if (level, i, j) in OUTER_TERMS:
            terms[OUTER_TERMS.index((level, i, j))] = value
        if level == 3 and (i, j) in STATE:
            index = STATE.index((i, j))
            state[index * BS : (index + 1) * BS, :] = value

    outer_levels(h, hn, xs, 0, far, far, kept, sums, pattern, record)
    state[3 * BS : 4 * BS, :] = inner_state[0]


def inner_second(
    near, state, near_state, inner_state, terms, h_kept, base, pattern,
    kept, sums, base_out, out_re, out_im, stage, sems, *scratch
):
    h, hn, xs = bands(scratch)
    x0 = xs[0]
    for index, (i, j) in enumerate(INNER_H):
        put_h_parts(h, hn, i, j, h_kept[index, 0], h_kept[index, 1])
    for index, (i, j) in enumerate(STATE):
        x0.put(i, j, slot(state, index))
    for (i, j), index in (((4, 4), 3), ((5, 5), 0), ((4, 5), 2), ((5, 4), 1)):
        x0.put(i, j, slot(near_state, index))
    x0.put(3, 4, inner_state[1])
    x0.put(4, 3, inner_state[2])
    for i, j in ((2, 1), (1, 2)):
        x0.put(i, j, terms[OUTER_TERMS.index((3, i, j))])

    values = {(level - 1, i, j): (terms, index) for index, (level, i, j) in enumerate(OUTER_TERMS)}
    values = {key: ref[index] for key, (ref, index) in values.items()}
    for index, (i, j) in enumerate(STATE):
        values[(2, i, j)] = slot(state, index)

    def record(level, i, j, value):
        values[(level + 2, i, j)] = value

    inner_levels(h, hn, xs, 3, near, pattern, sums, record)
    keep_parts(kept, h, xs)
    for index, ((row, offset), (i, j)) in enumerate(OWN):
        real, imag = base[index, 0], base[index, 1]
        terms_here = [level - 1 for level in OUTER_DONE.get((i, j), ())] + [level + 2 for level in INNER_DONE[(i, j)]]
        more_real, more_imag = parts_of(values, i, j, terms_here)
        real, imag = real + more_real, imag + more_imag
        if index < 4:
            base_out[index, 0], base_out[index, 1] = real, imag
        else:
            stage[index - 4, 0], stage[index - 4, 1] = real, imag
    copies = []
    for n, (row, offset) in enumerate(((1, 0), (1, 1))):
        r, e = own_index(row, offset)
        for a, out in enumerate((out_re, out_im)):
            copies.append(pltpu.make_async_copy(stage.at[n, a], out.at[r, e], sems.at[len(copies)]))
    for copy in copies:
        copy.start()
    for copy in copies:
        copy.wait()


def outer_second(
    far, far_state, kept, sums, base, in_re, in_im, pattern, out_re, out_im, stage, sems, *scratch
):
    h, hn, xs = bands(scratch)
    values = {}

    def record(level, i, j, value):
        values[(level + 2, i, j)] = value

    outer_levels(h, hn, xs, 3, far_state, far, kept, sums, pattern, record)
    copies = []
    for index, ((row, offset), (i, j)) in enumerate(OWN[:4]):
        real, imag = parts_of(values, i, j, [level + 2 for level in OUTER_DONE[(i, j)]])
        stage[index, 0], stage[index, 1] = base[index, 0] + real, base[index, 1] + imag
        r, e = own_index(row, offset)
        for a, out in enumerate((out_re, out_im)):
            copies.append(pltpu.make_async_copy(stage.at[index, a], out.at[r, e], sems.at[len(copies)]))
            copies[-1].start()
    for copy in copies:
        copy.wait()


VECTOR = pl.BlockSpec(memory_space=pltpu.VMEM)
SCALAR = pl.BlockSpec(memory_space=pltpu.SMEM)
BIG = pl.BlockSpec(memory_space=pltpu.HBM)


def call(kernel, ins, outs, scratch, flops, aliases=None):
    return pl.pallas_call(
        kernel,
        out_shape=[shape for shape, _ in outs],
        in_specs=ins,
        out_specs=[spec for _, spec in outs],
        scratch_shapes=scratch,
        input_output_aliases=aliases or {},
        compiler_params=pltpu.CompilerParams(vmem_limit_bytes=32 * 2**20),
        cost_estimate=pl.CostEstimate(flops=flops, bytes_accessed=4 * 2**20, transcendentals=0),
    )


def blocks(*lead, dtype=f32):
    return jax.ShapeDtypeStruct((*lead, BS, BS), dtype)


def body(density_real, density_imag, hamiltonian, dipole, field, pattern):
    count = lax.axis_size(RING)
    pair = [(i, i ^ 1) for i in range(count)]
    cross = [(i, (i + 1) % count if i % 2 else (i - 1) % count) for i in range(count)]
    pattern = jnp.transpose(pattern, (2, 1, 0))
    whole = density_real.shape
    arrays = [
        pltpu.with_memory_space_constraint(x, pltpu.HBM) for x in (density_real, density_imag, hamiltonian, dipole)
    ]
    dma = pltpu.SemaphoreType.DMA
    kept_out = (blocks(len(KEPT_X) + len(KEPT_H), 2, dtype=bf16), VECTOR)
    sums_out = (blocks(len(SUMS)), VECTOR)

    (packed,) = call(
        pack_kernel,
        [BIG] * 4 + [SCALAR] * 2,
        [(jax.ShapeDtypeStruct((PAYLOAD_ROWS, BS), f32), VECTOR)],
        [pltpu.VMEM((2, 2, 2, BS, BS), f32), pltpu.VMEM((2, 3, BS, BS), f32), dma((10,))],
        10**6,
    )(*arrays, field, pattern)
    far = lax.ppermute(packed, RING, cross)
    near = lax.ppermute(packed, RING, pair)
    kept, sums, h_kept, base, inner_state = call(
        inner_first,
        [BIG] * 4 + [VECTOR] + [SCALAR] * 2,
        [
            kept_out,
            sums_out,
            (blocks(len(INNER_H), 2, dtype=bf16), VECTOR),
            (blocks(len(OWN), 2), VECTOR),
            (blocks(3), VECTOR),
        ],
        [pltpu.VMEM(whole, f32)] * 4 + [dma((4,))] + band_scratch(),
        2 * 10**9,
    )(*arrays, near, field, pattern)
    state, terms = call(
        outer_first,
        [VECTOR] * 4 + [SCALAR],
        [(jax.ShapeDtypeStruct((4 * BS, BS), f32), VECTOR), (blocks(len(OUTER_TERMS)), VECTOR)],
        band_scratch(),
        2 * 10**9,
    )(far, kept, sums, inner_state, pattern)
    far_state = lax.ppermute(state, RING, cross)
    near_state = lax.ppermute(state, RING, pair)
    out = (jax.ShapeDtypeStruct(whole, f32), BIG)
    kept, sums, base, out_re, out_im = call(
        inner_second,
        [VECTOR] * 7 + [SCALAR],
        [kept_out, sums_out, (blocks(4, 2), VECTOR), out, out],
        [pltpu.VMEM((2, 2, BS, BS), f32), dma((4,))] + band_scratch(),
        2 * 10**9,
    )(near, state, near_state, inner_state, terms, h_kept, base, pattern)
    return tuple(
        call(
            outer_second,
            [VECTOR] * 5 + [BIG] * 2 + [SCALAR],
            [out, out],
            [pltpu.VMEM((4, 2, BS, BS), f32), dma((8,))] + band_scratch(),
            2 * 10**9,
            {5: 0, 6: 1},
        )(far, far_state, kept, sums, base, out_re, out_im, pattern)
    )


def solution(mesh):
    in_specs = (
        P(("row", "col"), None, None, None),
        P(("row", "col"), None, None, None),
        P(("row", "col"), None, None, None),
        P(("parts", "row", "col"), None, None, None),
        P("parts"),
        P(None, ("row", "col"), None),
    )
    out_specs = (
        P(("parts", "row", "col"), None, None, None),
        P(("parts", "row", "col"), None, None, None),
    )
    return jax.shard_map(body, mesh=mesh, in_specs=in_specs, out_specs=out_specs, check_vma=False)
```

```python
import functools

import jax
import jax.numpy as jnp
from jax import lax
from jax.experimental import pallas as pl
from jax.experimental.pallas import tpu as pltpu
from jax.sharding import PartitionSpec as P

TERMS = 6
BS = 128
time_step = 0.5
RING = ("row", "col")
f32, bf16 = jnp.float32, jnp.bfloat16

ROWS = 6
SIGN_RE = (1.0, -1.0, -1.0, 1.0, 1.0, -1.0)
SIGN_IM = (-1.0, -1.0, 1.0, 1.0, -1.0, -1.0)
FIRST_ROWS = 6 * BS + 8
SECOND_ROWS = 4 * BS
MORE = 8
TABLE_ROWS = 32
TABLE_FIELD = 24


def own_index(row, offset):
    core = lax.axis_index("col")
    return jnp.where(core == 0, row, 1 - row), jnp.where(core == 0, 1 + offset, 1 - offset)


def own(ref, row, offset):
    r, e = own_index(row, offset)
    return ref[r, e]


def slot(ref, index):
    return ref[index * BS : (index + 1) * BS, :]


def line(ref, index):
    return ref[index : index + 1, :]


class Band:
    def __init__(self, ref, negated=False):
        self.high, self.low = ref.at[0], ref.at[1]
        self.minus = Band(ref.at[pl.ds(2, 2)]) if negated else None

    def put(self, i, j, value):
        part = slice((j - i + 1) * BS, (j - i + 2) * BS)
        high = value.astype(bf16)
        low = (value - high.astype(f32)).astype(bf16)
        self.high[i, :, part] = high
        self.low[i, :, part] = low
        if self.minus is not None:
            self.minus.high[i, :, part] = -high
            self.minus.low[i, :, part] = -low

    def left(self, i, first, last):
        part = slice((first - i + 1) * BS, (last - i + 2) * BS)
        high, low = self.high[i, :, part], self.low[i, :, part]
        return [high, high, low]

    def right(self, first, last, j, j_last):
        highs, lows = [], []
        for k in range(first, last + 1):
            part = slice((j - k + 1) * BS, (j_last - k + 2) * BS)
            highs.append(self.high[k, :, part])
            lows.append(self.low[k, :, part])
        return highs + lows + highs


def piece(h, x, rows, mids, cols):
    right = jnp.concatenate(x.right(*mids, *cols) + h.minus.right(*mids, *cols), axis=0)
    return [
        jnp.dot(
            jnp.concatenate(h.left(i, *mids) + x.left(i, *mids), axis=1), right, preferred_element_type=f32
        )
        for i in rows
    ]


def one_side(a, b, row, mids, col):
    left = jnp.concatenate(a.left(row, *mids), axis=1)
    right = jnp.concatenate(b.right(*mids, col, col), axis=0)
    return jnp.dot(left, right, preferred_element_type=f32)


def tile(h, x, i):
    upper, lower = piece(h, x, (i, i + 1), (i, i + 1), (i, i + 1))
    return upper[:, :BS], upper[:, BS:], lower[:, :BS], lower[:, BS:]


def part(h, x, i, k, j):
    return piece(h, x, (i,), (k, k), (j, j))[0]


def coefficient(term):
    return time_step / (term + 1)


SUMS = ((1, 1, 1), (1, 1, 2), (1, 2, 1), (2, 2, 2), (3, 2, 2), (3, 2, 3), (3, 3, 2))
OUTER_TERMS = ((1, 2, 1), (1, 1, 2), (2, 2, 1), (2, 1, 2), (3, 2, 1), (3, 1, 2), (2, 2, 2))
STATE = ((2, 2), (2, 3), (3, 2), (3, 3))
INNER_STATE = ((3, 3), (3, 4), (4, 3))
OWN = (((0, -1), (2, 1)), ((0, 0), (2, 2)), ((0, 1), (2, 3)), ((1, -1), (3, 2)), ((1, 0), (3, 3)), ((1, 1), (3, 4)))
DONE_A = {(2, 2): (1,), (2, 3): (1,), (3, 2): (1,)}
DONE_B = {(2, 3): (2,), (3, 2): (2,), (3, 3): (1, 2, 3), (3, 4): (1, 2, 3)}
DONE_OUTER = {(2, 1): (1, 2, 3), (2, 2): (2, 3), (2, 3): (3,), (3, 2): (3,)}
NEAR_X = (((4, 4), 3), ((5, 5), 0), ((4, 5), 2), ((5, 4), 1))
FAR_X = (((1, 1), 0), ((0, 0), 3), ((1, 0), 1), ((0, 1), 2))


def weighted(terms_of, signs):
    total = None
    for sign, value in zip(signs, terms_of):
        total = (value if sign > 0 else -value) if total is None else (total + value if sign > 0 else total - value)
    return total


def parts_of(values, i, j, terms):
    re_signs, im_signs = [SIGN_RE[term] for term in terms], [SIGN_IM[term] for term in terms]
    here = [values[(term, i, j)] for term in terms]
    there = here if i == j else [values[(term, j, i)] for term in terms]
    real = 0.5 * (weighted(here, re_signs) + weighted(there, re_signs).T)
    imag = 0.5 * (weighted(here, im_signs) - weighted(there, im_signs).T)
    return real, imag


def add_terms(base, values, done, phase):
    for index, (_, (i, j)) in enumerate(OWN):
        terms = [level - 1 + 3 * phase for level in done.get((i, j), ())]
        if terms:
            real, imag = parts_of(values, i, j, terms)
            base[index, 0] = base[index, 0] + real
            base[index, 1] = base[index, 1] + imag


def triangle(test):
    rows = lax.broadcasted_iota(jnp.int32, (BS, BS), 0)
    cols = lax.broadcasted_iota(jnp.int32, (BS, BS), 1)
    return test(rows, cols)


def unpack_h(payload):
    both = slot(payload, 4)
    turned = both.T
    first = jnp.where(triangle(lambda r, c: r <= c), both, turned)
    second = jnp.where(triangle(lambda r, c: r > c), both, turned)
    second = jnp.where(triangle(lambda r, c: r == c), line(payload, 6 * BS + 6), second)
    return first, second, slot(payload, 5)


def pack_kernel(re, im, ham, dip, pattern_in, field, far, near, table, dens, oper, pattern, sems):
    copies = [pltpu.make_async_copy(pattern_in, pattern, sems.at[0])]
    for a, ref in enumerate((re, im)):
        for r in range(2):
            copies.append(pltpu.make_async_copy(ref.at[r, pl.ds(1 - r, 2)], dens.at[a, r], sems.at[len(copies)]))
    for a, ref in enumerate((ham, dip)):
        for n, (row, offset) in enumerate(((0, 0), (0, 1), (1, 0))):
            r, e = own_index(row, offset)
            copies.append(pltpu.make_async_copy(ref.at[r, e], oper.at[a, n], sems.at[len(copies)]))
    for copy in copies:
        copy.start()
    for copy in copies[:5]:
        copy.wait()

    def put(first, value):
        far[first : first + value.shape[0], :] = value
        near[first : first + value.shape[0], :] = value

    for index, (row, offset) in enumerate(((0, 0), (0, 1), (1, -1), (1, 0))):
        r, e = own_index(row, offset)
        put(index * BS, dens[0, r, e - 1 + r] + dens[1, r, e - 1 + r])
    f = field[0]
    for n, (row, offset) in enumerate(((0, -1), (0, 1), (1, 1))):
        r, e = own_index(row, offset)
        for term in range(TERMS):
            value = jnp.full((1, BS), pattern[e, r, term].astype(f32) * coefficient(term), f32)
            table[8 * n + term : 8 * n + term + 1, :] = value
            if n == 1:
                put(6 * BS + term, value)
    table[TABLE_FIELD : TABLE_FIELD + 1, :] = jnp.full((1, BS), f, f32)
    for copy in copies[5:]:
        copy.wait()
    first, between, second = [oper[0, n] + f * oper[1, n] for n in range(3)]
    put(4 * BS, jnp.where(triangle(lambda r, c: r <= c), first, second))
    put(5 * BS, between)
    diagonal = jnp.where(triangle(lambda r, c: r == c), second, 0.0)
    put(6 * BS + 6, jnp.sum(diagonal, axis=0, keepdims=True))


def views(h_ref, x_ref):
    return Band(h_ref, True), [Band(x_ref.at[level]) for level in range(3)]


def inner_a(h, xs, phase, table, base, sums, carry, values):
    term = 3 * phase
    t2 = tile(h, xs[0], 2)
    scale = line(table, 8 + term)
    first = {
        (2, 3): t2[1] * scale,
        (3, 2): t2[2] * scale,
        (2, 2): (part(h, xs[0], 2, 1, 2) + t2[0]) * coefficient(term),
    }
    carry[...] = t2[3]
    for (i, j), value in first.items():
        xs[1].put(i, j, value)
        values[(term, i, j)] = value
    sums[0] = part(h, xs[0], 1, 2, 1)
    sums[1] = part(h, xs[0], 1, 2, 2)
    sums[2] = part(h, xs[0], 2, 2, 1)
    add_terms(base, values, DONE_A, phase)


def inner_a_first(re, im, ham, dip, table, h_ref, x_ref, base, sums, carry, re_in, im_in, ham_in, dip_in, sems):
    copies = [
        pltpu.make_async_copy(source, target, sems.at[n])
        for n, (source, target) in enumerate(((ham, ham_in), (dip, dip_in), (re, re_in), (im, im_in)))
    ]
    for copy in copies:
        copy.start()
    h, xs = views(h_ref, x_ref)
    for copy in copies:
        copy.wait()
    f = line(table, TABLE_FIELD)
    for index, ((row, offset), (i, j)) in enumerate(OWN):
        value = own(ham_in, row, offset) + f * own(dip_in, row, offset)
        h.put(i, j, value)
        real, imag = own(re_in, row, offset), own(im_in, row, offset)
        xs[0].put(i, j, real + imag)
        if j in (1, 4):
            h.put(j, i, value.T)
            xs[0].put(j, i, (real - imag).T)
        base[index, 0], base[index, 1] = real, imag
    inner_a(h, xs, 0, table, base, sums, carry, {})


def inner_b(h, xs, phase, near_scale, table, base, sums, carry, values):
    term = 3 * phase
    c = [coefficient(term + n) for n in range(3)]
    own_edge = [line(table, 8 + term + n) for n in range(3)]
    near_edge = [line(table, 16 + term + n) for n in range(3)]

    def put(level, i, j, value):
        values[(term + level - 1, i, j)] = value
        if level < 3:
            xs[level].put(i, j, value)

    x0, x1, x2 = xs
    t3, t4 = tile(h, x0, 3), tile(h, x0, 4)
    put(1, 3, 4, t3[1] * near_edge[0])
    put(1, 4, 3, t3[2] * near_edge[0])
    put(1, 3, 3, (carry[...] + t3[0] - part(h, x0, 3, 3, 3)) * c[0])
    put(1, 4, 4, (t3[3] + t4[0] - part(h, x0, 4, 4, 4)) * c[0])
    put(1, 4, 5, t4[1] * near_scale)
    put(1, 5, 4, t4[2] * near_scale)
    t2, t3 = tile(h, x1, 2), tile(h, x1, 3)
    put(2, 2, 3, t2[1] * own_edge[1])
    put(2, 3, 2, t2[2] * own_edge[1])
    put(2, 3, 3, (t2[3] + t3[0] - part(h, x1, 3, 3, 3)) * c[1])
    put(2, 3, 4, t3[1] * near_edge[1])
    put(2, 4, 3, t3[2] * near_edge[1])
    put(2, 4, 4, (t3[3] + part(h, x1, 4, 5, 4)) * c[1])
    sums[3] = part(h, x1, 2, 3, 2)
    t3 = tile(h, x2, 3)
    put(3, 3, 4, t3[1] * near_edge[2])
    put(3, 4, 3, t3[2] * near_edge[2])
    put(3, 3, 3, (t3[0] + part(h, x2, 3, 2, 3)) * c[2])
    sums[4] = part(h, x2, 2, 3, 2)
    sums[5] = one_side(h, x2, 2, (2, 3), 3) + one_side(x2, h.minus, 2, (3, 3), 3)
    sums[6] = one_side(h, x2, 3, (3, 3), 2) + one_side(x2, h.minus, 3, (2, 3), 2)
    add_terms(base, values, DONE_B, phase)


def inner_b_first(near, table, carry, h_in, x_in, base_in, sums_in, h_ref, x_ref, base, sums, state):
    h, xs = views(h_ref, x_ref)
    inside, outside, between = second_first(near)
    h.put(4, 4, inside)
    h.put(5, 5, outside)
    h.put(5, 4, between)
    h.put(4, 5, between.T)
    for (i, j), index in NEAR_X:
        xs[0].put(i, j, slot(near, index))
    values = {}
    inner_b(h, xs, 0, line(near, 6 * BS), table, base, sums, carry, values)
    for index, (i, j) in enumerate(INNER_STATE):
        state[index] = values[(2, i, j)]


def second_first(payload):
    first, second, between = unpack_h(payload)
    return second, first, between


def outer(h, xs, phase, far_scale, table, sums, record):
    term = 3 * phase
    c = [coefficient(term + n) for n in range(3)]
    cross = [line(table, term + n) for n in range(3)]

    def put(level, i, j, value):
        record(level, i, j, value)
        if level < 3:
            xs[level].put(i, j, value)

    def known(level, i, j):
        return sums[SUMS.index((level, i, j))]

    x0, x1, x2 = xs
    t0 = tile(h, x0, 0)
    put(1, 1, 1, (t0[3] + known(1, 1, 1)) * c[0])
    put(1, 1, 2, (part(h, x0, 1, 1, 2) + known(1, 1, 2)) * cross[0])
    put(1, 2, 1, (part(h, x0, 2, 1, 1) + known(1, 2, 1)) * cross[0])
    put(1, 0, 1, t0[1] * far_scale)
    put(1, 1, 0, t0[2] * far_scale)
    t1 = tile(h, x1, 1)
    put(2, 1, 1, (part(h, x1, 1, 0, 1) + t1[0]) * c[1])
    put(2, 1, 2, t1[1] * cross[1])
    put(2, 2, 1, t1[2] * cross[1])
    put(2, 2, 2, (t1[3] + known(2, 2, 2)) * c[1])
    t1 = tile(h, x2, 1)
    scale = line(table, 8 + term + 2)
    put(3, 2, 3, (one_side(x2, h.minus, 2, (2, 2), 3) + known(3, 2, 3)) * scale)
    put(3, 3, 2, (one_side(h, x2, 3, (2, 2), 2) + known(3, 3, 2)) * scale)
    put(3, 1, 2, t1[1] * cross[2])
    put(3, 2, 1, t1[2] * cross[2])
    put(3, 2, 2, (t1[3] + known(3, 2, 2)) * c[2])


def outer_first(far, table, sums, inner_state, h_in, x_in, h_ref, x_ref, state, state_near, terms):
    h, xs = views(h_ref, x_ref)
    inside, outside, between = unpack_h(far)
    h.put(1, 1, inside)
    h.put(0, 0, outside)
    h.put(1, 0, between)
    h.put(0, 1, between.T)
    for (i, j), index in FAR_X:
        xs[0].put(i, j, slot(far, index))

    def put(index, value):
        state[index * BS : (index + 1) * BS, :] = value
        state_near[index * BS : (index + 1) * BS, :] = value

    def record(level, i, j, value):
        if (level, i, j) in OUTER_TERMS:
            terms[OUTER_TERMS.index((level, i, j))] = value
        if level == 3 and (i, j) in STATE:
            put(STATE.index((i, j)), value)

    put(3, inner_state[0])
    outer(h, xs, 0, line(far, 6 * BS), table, sums, record)


def inner_a_second(state, inner_state, terms, table, h_ref, x_in, base_in, x_ref, base, sums, carry):
    h, xs = views(h_ref, x_ref)
    values = {(level - 1, i, j): terms[index] for index, (level, i, j) in enumerate(OUTER_TERMS)}
    for index, (i, j) in enumerate(STATE):
        values[(2, i, j)] = slot(state, index)
    for index, (i, j) in enumerate(INNER_STATE):
        values[(2, i, j)] = inner_state[index]
    for i, j in STATE + INNER_STATE[1:] + ((1, 2), (2, 1)):
        xs[0].put(i, j, values[(2, i, j)])
    add_terms(base, values, DONE_OUTER, 0)
    inner_a(h, xs, 1, table, base, sums, carry, {})


def inner_b_second(
    near_state, near, table, carry, h_ref, x_in, base_in, sums_in, x_ref, base, sums, out_re, out_im, sems
):
    h, xs = views(h_ref, x_ref)
    for (i, j), index in NEAR_X:
        xs[0].put(i, j, slot(near_state, index))
    inner_b(h, xs, 1, line(near, 6 * BS + 3), table, base, sums, carry, {})
    copies = []
    for index, ((row, offset), _) in tuple(enumerate(OWN))[4:]:
        r, e = own_index(row, offset)
        for a, out in enumerate((out_re, out_im)):
            copies.append(pltpu.make_async_copy(base.at[index, a], out.at[r, e], sems.at[len(copies)]))
    for copy in copies:
        copy.start()
    for copy in copies:
        copy.wait()


def outer_second(
    far_state, far, table, sums, base, h_ref, x_in, in_re, in_im, x_ref, out_re, out_im, stage, sems
):
    h, xs = views(h_ref, x_ref)
    for (i, j), index in FAR_X:
        xs[0].put(i, j, slot(far_state, index))
    values = {}

    def record(level, i, j, value):
        values[(level + 2, i, j)] = value

    outer(h, xs, 1, line(far, 6 * BS + 3), table, sums, record)
    copies = []
    for index in (2, 3, 0, 1):
        (row, offset), (i, j) = OWN[index]
        real, imag = parts_of(values, i, j, [level + 2 for level in DONE_OUTER[(i, j)]])
        stage[index, 0], stage[index, 1] = base[index, 0] + real, base[index, 1] + imag
        r, e = own_index(row, offset)
        for a, out in enumerate((out_re, out_im)):
            copies.append(pltpu.make_async_copy(stage.at[index, a], out.at[r, e], sems.at[len(copies)]))
            copies[-1].start()
    for copy in copies:
        copy.wait()


VECTOR = pl.BlockSpec(memory_space=pltpu.VMEM)
SCALAR = pl.BlockSpec(memory_space=pltpu.SMEM)
BIG = pl.BlockSpec(memory_space=pltpu.HBM)


def call(kernel, ins, outs, scratch=(), aliases=None):
    return pl.pallas_call(
        kernel,
        out_shape=[shape for shape, _ in outs],
        in_specs=ins,
        out_specs=[spec for _, spec in outs],
        scratch_shapes=list(scratch),
        input_output_aliases=aliases or {},
        compiler_params=pltpu.CompilerParams(vmem_limit_bytes=24 * 2**20),
        cost_estimate=pl.CostEstimate(flops=0, bytes_accessed=0, transcendentals=0),
    )


def vector(*shape, dtype=f32):
    return jax.ShapeDtypeStruct(shape, dtype), VECTOR


def body(density_real, density_imag, hamiltonian, dipole, field, pattern):
    count = lax.axis_size(RING)
    pair = [(i, i ^ 1) for i in range(count)]
    cross = [(i, (i + 1) % count if i % 2 else (i - 1) % count) for i in range(count)]
    pattern = jnp.transpose(pattern, (2, 1, 0))
    whole = density_real.shape
    inputs = [
        pltpu.with_memory_space_constraint(x, pltpu.HBM)
        for x in (density_real, density_imag, hamiltonian, dipole, pattern)
    ]
    dma = pltpu.SemaphoreType.DMA
    h_out, x_out = vector(4, ROWS, BS, 3 * BS, dtype=bf16), vector(3, 2, ROWS, BS, 3 * BS, dtype=bf16)
    base_out, sums_out, carry_out = vector(len(OWN), 2, BS, BS), vector(len(SUMS), BS, BS), vector(BS, BS)
    table_out = vector(TABLE_ROWS, BS)
    out = (jax.ShapeDtypeStruct(whole, f32), BIG)

    far_pack, near_pack, table = call(
        pack_kernel,
        [BIG] * 5 + [SCALAR],
        [vector(FIRST_ROWS + MORE, BS), vector(FIRST_ROWS, BS), table_out],
        [
            pltpu.VMEM((2, 2, 2, BS, BS), f32),
            pltpu.VMEM((2, 3, BS, BS), f32),
            pltpu.SMEM(pattern.shape, jnp.int32),
            dma((11,)),
        ],
    )(*inputs, field)
    far = lax.ppermute(far_pack, RING, cross)
    near = lax.ppermute(near_pack, RING, pair)
    h, x, base, sums, carry = call(
        inner_a_first,
        [BIG] * 4 + [VECTOR],
        [h_out, x_out, base_out, sums_out, carry_out],
        [pltpu.VMEM(whole, f32)] * 4 + [dma((4,))],
    )(*inputs[:4], table)
    h, x, base, sums, inner_state = call(
        inner_b_first,
        [VECTOR] * 7,
        [h_out, x_out, base_out, sums_out, vector(len(INNER_STATE), BS, BS)],
        aliases={3: 0, 4: 1, 5: 2, 6: 3},
    )(near, table, carry, h, x, base, sums)
    h, x, state, state_near, terms = call(
        outer_first,
        [VECTOR] * 6,
        [
            h_out,
            x_out,
            vector(SECOND_ROWS + MORE, BS),
            vector(SECOND_ROWS, BS),
            vector(len(OUTER_TERMS), BS, BS),
        ],
        aliases={4: 0, 5: 1},
    )(far, table, sums, inner_state, h, x)
    far_state = lax.ppermute(state, RING, cross)
    near_state = lax.ppermute(state_near, RING, pair)
    x, base, sums, carry = call(
        inner_a_second,
        [VECTOR] * 7,
        [x_out, base_out, sums_out, carry_out],
        aliases={5: 0, 6: 1},
    )(state, inner_state, terms, table, h, x, base)
    x, base, sums, out_re, out_im = call(
        inner_b_second,
        [VECTOR] * 8,
        [x_out, base_out, sums_out, out, out],
        [dma((4,))],
        aliases={5: 0, 6: 1, 7: 2},
    )(near_state, near, table, carry, h, x, base, sums)
    _, out_re, out_im = call(
        outer_second,
        [VECTOR] * 7 + [BIG] * 2,
        [x_out, out, out],
        [pltpu.VMEM((4, 2, BS, BS), f32), dma((8,))],
        aliases={6: 0, 7: 1, 8: 2},
    )(far_state, far, table, sums, base, h, x, out_re, out_im)
    return out_re, out_im


def solution(mesh):
    in_specs = (
        P(("row", "col"), None, None, None),
        P(("row", "col"), None, None, None),
        P(("row", "col"), None, None, None),
        P(("parts", "row", "col"), None, None, None),
        P("parts"),
        P(None, ("row", "col"), None),
    )
    out_specs = (
        P(("parts", "row", "col"), None, None, None),
        P(("parts", "row", "col"), None, None, None),
    )
    return jax.shard_map(body, mesh=mesh, in_specs=in_specs, out_specs=out_specs, check_vma=False)
```

```python
import functools

import jax
import jax.numpy as jnp
from jax import lax
from jax.experimental import pallas as pl
from jax.experimental.pallas import tpu as pltpu
from jax.sharding import PartitionSpec as P

TERMS = 6
BS = 128
time_step = 0.5
RING = ("row", "col")
f32, bf16 = jnp.float32, jnp.bfloat16

ROWS = 6
SIGN_RE = (1.0, -1.0, -1.0, 1.0, 1.0, -1.0)
SIGN_IM = (-1.0, -1.0, 1.0, 1.0, -1.0, -1.0)
FIRST_ROWS = 4 * BS
SECOND_ROWS = 3 * BS
MORE = 8
TABLE_ROWS = 24


def own_index(row, offset):
    core = lax.axis_index("col")
    return jnp.where(core == 0, row, 1 - row), jnp.where(core == 0, 1 + offset, 1 - offset)


def own(ref, row, offset):
    r, e = own_index(row, offset)
    return ref[r, e]


def slot(ref, index):
    return ref[index * BS : (index + 1) * BS, :]


def line(ref, index):
    return ref[index : index + 1, :]


class Band:
    def __init__(self, ref, negated=False):
        self.high, self.low = ref.at[0], ref.at[1]
        self.minus = Band(ref.at[pl.ds(2, 2)]) if negated else None

    def put(self, i, j, value):
        part = slice((j - i + 1) * BS, (j - i + 2) * BS)
        high = value.astype(bf16)
        low = (value - high.astype(f32)).astype(bf16)
        self.high[i, :, part] = high
        self.low[i, :, part] = low
        if self.minus is not None:
            self.minus.high[i, :, part] = -high
            self.minus.low[i, :, part] = -low

    def left(self, i, first, last):
        part = slice((first - i + 1) * BS, (last - i + 2) * BS)
        high, low = self.high[i, :, part], self.low[i, :, part]
        return [high, high, low]

    def right(self, first, last, j, j_last):
        highs, lows = [], []
        for k in range(first, last + 1):
            part = slice((j - k + 1) * BS, (j_last - k + 2) * BS)
            highs.append(self.high[k, :, part])
            lows.append(self.low[k, :, part])
        return highs + lows + highs


def piece(h, x, rows, mids, cols):
    right = jnp.concatenate(x.right(*mids, *cols) + h.minus.right(*mids, *cols), axis=0)
    return [
        jnp.dot(
            jnp.concatenate(h.left(i, *mids) + x.left(i, *mids), axis=1), right, preferred_element_type=f32
        )
        for i in rows
    ]


def one_side(a, b, row, mids, col):
    left = jnp.concatenate(a.left(row, *mids), axis=1)
    right = jnp.concatenate(b.right(*mids, col, col), axis=0)
    return jnp.dot(left, right, preferred_element_type=f32)


def tile(h, x, i):
    upper, lower = piece(h, x, (i, i + 1), (i, i + 1), (i, i + 1))
    return upper[:, :BS], upper[:, BS:], lower[:, :BS], lower[:, BS:]


def part(h, x, i, k, j):
    return piece(h, x, (i,), (k, k), (j, j))[0]


def coefficient(term):
    return time_step / (term + 1)


SUMS = ((1, 2, 1), (1, 1, 2), (1, 3, 4), (1, 4, 3), (2, 2, 2), (2, 3, 3), (3, 2, 2), (3, 3, 3), (3, 2, 3), (3, 3, 2))
OWN = (((0, -1), (2, 1)), ((0, 0), (2, 2)), ((0, 1), (2, 3)), ((1, -1), (3, 2)), ((1, 0), (3, 3)), ((1, 1), (3, 4)))
EARLY = ((1, 2, 2), (1, 3, 3), (1, 2, 3), (1, 3, 2))
LATE = ((1, 2, 1), (1, 1, 2), (2, 2, 1), (2, 1, 2), (3, 2, 1), (3, 1, 2), (2, 2, 2), (3, 2, 2), (3, 2, 3), (3, 3, 2))
DONE_EARLY = {(2, 2): (1,), (2, 3): (1, 2), (3, 2): (1, 2), (3, 3): (1,)}
DONE_NEAR = {(3, 3): (2, 3), (3, 4): (1, 2, 3)}
DONE_FAR = {(2, 1): (1, 2, 3), (2, 2): (2, 3), (2, 3): (3,), (3, 2): (3,)}


def weighted(terms_of, signs):
    total = None
    for sign, value in zip(signs, terms_of):
        total = (value if sign > 0 else -value) if total is None else (total + value if sign > 0 else total - value)
    return total


def parts_of(values, i, j, terms):
    re_signs, im_signs = [SIGN_RE[term] for term in terms], [SIGN_IM[term] for term in terms]
    here = [values[(term, i, j)] for term in terms]
    there = here if i == j else [values[(term, j, i)] for term in terms]
    real = 0.5 * (weighted(here, re_signs) + weighted(there, re_signs).T)
    imag = 0.5 * (weighted(here, im_signs) - weighted(there, im_signs).T)
    return real, imag


def add_terms(base, values, done, phase):
    for index, (_, (i, j)) in enumerate(OWN):
        terms = [level - 1 + 3 * phase for level in done.get((i, j), ())]
        if terms:
            real, imag = parts_of(values, i, j, terms)
            base[index, 0] = base[index, 0] + real
            base[index, 1] = base[index, 1] + imag


def views(h_ref, x_ref):
    return Band(h_ref, True), [Band(x_ref.at[level]) for level in range(3)]


def before_send(h, xs, phase, table, sums, early, far, near):
    x0, x1, _ = xs
    term = 3 * phase
    t = tile(h, x0, 2)
    scale = line(table, 6 + term)
    inner = {
        (2, 2): (t[0] + part(h, x0, 2, 1, 2)) * coefficient(term),
        (3, 3): (t[3] + part(h, x0, 3, 4, 3)) * coefficient(term),
        (2, 3): t[1] * scale,
        (3, 2): t[2] * scale,
    }
    for (i, j), value in inner.items():
        x1.put(i, j, value)
    far[BS : 2 * BS, :] = inner[(2, 2)]
    near[BS : 2 * BS, :] = inner[(3, 3)]
    for index, (_, i, j) in enumerate(EARLY):
        early[index] = inner[(i, j)]
    for out, i, k in ((far, 2, 3), (near, 3, 2)):
        value = part(h, x1, i, k, i)
        out[2 * BS : 3 * BS, :] = value
        sums[SUMS.index((2, i, i))] = value


def own_first(
    re, im, ham, dip, pattern_in, field,
    far, near, table, h_ref, x_ref, sums, early, re_in, im_in,
    ham_in, dip_in, pattern, sems,
):
    copies = [
        pltpu.make_async_copy(source, target, sems.at[n])
        for n, (source, target) in enumerate(
            ((pattern_in, pattern), (ham, ham_in), (dip, dip_in), (re, re_in), (im, im_in))
        )
    ]
    for copy in copies:
        copy.start()
    copies[0].wait()
    for n, (row, offset) in enumerate(((0, -1), (0, 1), (1, 1))):
        r, e = own_index(row, offset)
        for term in range(TERMS):
            table[6 * n + term : 6 * n + term + 1, :] = jnp.full(
                (1, BS), pattern[e, r, term].astype(f32) * coefficient(term), f32
            )
    h, xs = views(h_ref, x_ref)
    for copy in copies[1:3]:
        copy.wait()
    for (row, offset), (i, j) in OWN:
        value = own(ham_in, row, offset) + field[0] * own(dip_in, row, offset)
        h.put(i, j, value)
        if j in (1, 4):
            h.put(j, i, value.T)
        if i == j:
            (far if i == 2 else near)[3 * BS : 4 * BS, :] = value
    for copy in copies[3:]:
        copy.wait()
    for (row, offset), (i, j) in OWN:
        real, imag = own(re_in, row, offset), own(im_in, row, offset)
        xs[0].put(i, j, real + imag)
        if j in (1, 4):
            xs[0].put(j, i, (real - imag).T)
        if i == j:
            (far if i == 2 else near)[0:BS, :] = real + imag
    before_send(h, xs, 0, table, sums, early, far, near)


def own_rest(h, xs, phase, table, early, base, sums):
    x0, x1, x2 = xs
    term = 3 * phase
    values = {(term, i, j): early[index] for index, (_, i, j) in enumerate(EARLY)}
    t = tile(h, x1, 2)
    scale = line(table, 6 + term + 1)
    for (i, j), value in (((2, 3), t[1] * scale), ((3, 2), t[2] * scale)):
        x2.put(i, j, value)
        values[(term + 1, i, j)] = value
    for a, b in ((3, 4), (2, 1)):
        sums[SUMS.index((1, a, b))] = part(h, x0, a, a, b)
        sums[SUMS.index((1, b, a))] = part(h, x0, b, a, a)
    sums[SUMS.index((3, 2, 2))] = part(h, x2, 2, 3, 2)
    sums[SUMS.index((3, 3, 3))] = part(h, x2, 3, 2, 3)
    add_terms(base, values, DONE_EARLY, phase)


def side(h, xs, a, b, payload, phase, scales, sums, record):
    x0, x1, x2 = xs
    c = [coefficient(3 * phase + n) for n in range(3)]
    low = min(a, b)
    at_a, at_b = (0, 3) if a == low else (3, 0)
    up, down = (low, low + 1), (low + 1, low)

    def known(level, i, j):
        return sums[SUMS.index((level, i, j))]

    def put(level, i, j, value):
        record(level, i, j, value)
        if level < 3:
            xs[level].put(i, j, value)

    x0.put(b, b, slot(payload, 0))
    x1.put(b, b, slot(payload, 1))
    put(1, a, b, (part(h, x0, a, b, b) + known(1, a, b)) * scales[0])
    put(1, b, a, (part(h, x0, b, b, a) + known(1, b, a)) * scales[0])
    t = tile(h, x1, low)
    put(2, a, a, (t[at_a] + known(2, a, a)) * c[1])
    put(2, b, b, (t[at_b] + slot(payload, 2)) * c[1])
    put(2, *up, t[1] * scales[1])
    put(2, *down, t[2] * scales[1])
    t = tile(h, x2, low)
    put(3, *up, t[1] * scales[2])
    put(3, *down, t[2] * scales[2])
    put(3, a, a, (t[at_a] + known(3, a, a)) * c[2])


def near_side(h, xs, near, phase, table, base, sums):
    term = 3 * phase
    values = {}

    def record(level, i, j, value):
        values[(term + level - 1, i, j)] = value

    scales = [line(table, 12 + term + n) for n in range(3)]
    side(h, xs, 3, 4, near, phase, scales, sums, record)
    x2 = xs[2]
    sums[SUMS.index((3, 2, 3))] = one_side(h, x2, 2, (2, 3), 3) + one_side(x2, h.minus, 2, (3, 3), 3)
    sums[SUMS.index((3, 3, 2))] = one_side(h, x2, 3, (3, 3), 2) + one_side(x2, h.minus, 3, (2, 3), 2)
    add_terms(base, values, DONE_NEAR, phase)
    return values


def far_side(h, xs, far, phase, table, sums, record):
    term = 3 * phase
    scales = [line(table, term + n) for n in range(3)]
    side(h, xs, 2, 1, far, phase, scales, sums, record)
    x2 = xs[2]
    scale = line(table, 6 + term + 2)
    record(3, 2, 3, (one_side(x2, h.minus, 2, (2, 2), 3) + sums[SUMS.index((3, 2, 3))]) * scale)
    record(3, 3, 2, (one_side(h, x2, 3, (2, 2), 2) + sums[SUMS.index((3, 3, 2))]) * scale)


def rest_first(re_in, im_in, table, early, h_ref, x_in, sums_in, x_ref, sums, base):
    h, xs = views(h_ref, x_ref)
    for index, ((row, offset), _) in enumerate(OWN):
        base[index, 0], base[index, 1] = own(re_in, row, offset), own(im_in, row, offset)
    own_rest(h, xs, 0, table, early, base, sums)


def near_first(near, table, h_in, x_in, sums_in, base_in, h_ref, x_ref, sums, base, inner_state):
    h, xs = views(h_ref, x_ref)
    h.put(4, 4, slot(near, 3))
    values = near_side(h, xs, near, 0, table, base, sums)
    for i, j in ((3, 3), (3, 4), (4, 3)):
        xs[0].put(i, j, values[(2, i, j)])
    inner_state[...] = values[(2, 3, 3)]


def far_first(far, table, inner_state, h_in, x_in, sums_in, h_ref, x_ref, sums, late, early, far_next, near_next):
    h, xs = views(h_ref, x_ref)
    h.put(1, 1, slot(far, 3))
    state = {}

    def record(level, i, j, value):
        if (level, i, j) in LATE:
            late[LATE.index((level, i, j))] = value
        if level == 3:
            state[(i, j)] = value

    far_side(h, xs, far, 0, table, sums, record)
    for (i, j), value in state.items():
        xs[0].put(i, j, value)
    far_next[0:BS, :] = state[(2, 2)]
    near_next[0:BS, :] = inner_state[...]
    before_send(h, xs, 1, table, sums, early, far_next, near_next)


def rest_second(late, early, table, h_ref, x_in, sums_in, base_in, x_ref, sums, base):
    h, xs = views(h_ref, x_ref)
    values = {(level - 1, i, j): late[index] for index, (level, i, j) in enumerate(LATE)}
    add_terms(base, values, DONE_FAR, 0)
    own_rest(h, xs, 1, table, early, base, sums)


def near_second(near, table, h_ref, x_in, sums_in, base_in, x_ref, sums, base, out_re, out_im, sems):
    h, xs = views(h_ref, x_ref)
    near_side(h, xs, near, 1, table, base, sums)
    copies = []
    for index, ((row, offset), _) in tuple(enumerate(OWN))[4:]:
        r, e = own_index(row, offset)
        for a, out in enumerate((out_re, out_im)):
            copies.append(pltpu.make_async_copy(base.at[index, a], out.at[r, e], sems.at[len(copies)]))
    for copy in copies:
        copy.start()
    for copy in copies:
        copy.wait()


def far_second(far, table, sums, base, h_ref, x_in, in_re, in_im, x_ref, out_re, out_im, stage, sems):
    h, xs = views(h_ref, x_ref)
    values = {}

    def record(level, i, j, value):
        values[(level + 2, i, j)] = value

    far_side(h, xs, far, 1, table, sums, record)
    copies = []
    for index in (2, 3, 0, 1):
        (row, offset), (i, j) = OWN[index]
        real, imag = parts_of(values, i, j, [level + 2 for level in DONE_FAR[(i, j)]])
        stage[index, 0], stage[index, 1] = base[index, 0] + real, base[index, 1] + imag
        r, e = own_index(row, offset)
        for a, out in enumerate((out_re, out_im)):
            copies.append(pltpu.make_async_copy(stage.at[index, a], out.at[r, e], sems.at[len(copies)]))
            copies[-1].start()
    for copy in copies:
        copy.wait()


VECTOR = pl.BlockSpec(memory_space=pltpu.VMEM)
SCALAR = pl.BlockSpec(memory_space=pltpu.SMEM)
BIG = pl.BlockSpec(memory_space=pltpu.HBM)


def call(kernel, ins, outs, scratch=(), aliases=None):
    return pl.pallas_call(
        kernel,
        out_shape=[shape for shape, _ in outs],
        in_specs=ins,
        out_specs=[spec for _, spec in outs],
        scratch_shapes=list(scratch),
        input_output_aliases=aliases or {},
        compiler_params=pltpu.CompilerParams(vmem_limit_bytes=24 * 2**20),
        cost_estimate=pl.CostEstimate(flops=0, bytes_accessed=0, transcendentals=0),
    )


def vector(*shape, dtype=f32):
    return jax.ShapeDtypeStruct(shape, dtype), VECTOR


def body(density_real, density_imag, hamiltonian, dipole, field, pattern):
    count = lax.axis_size(RING)
    pair = [(i, i ^ 1) for i in range(count)]
    cross = [(i, (i + 1) % count if i % 2 else (i - 1) % count) for i in range(count)]
    pattern = jnp.transpose(pattern, (2, 1, 0))
    whole = density_real.shape
    inputs = [
        pltpu.with_memory_space_constraint(x, pltpu.HBM)
        for x in (density_real, density_imag, hamiltonian, dipole, pattern)
    ]
    dma = pltpu.SemaphoreType.DMA
    h_out, x_out = vector(4, ROWS, BS, 3 * BS, dtype=bf16), vector(3, 2, ROWS, BS, 3 * BS, dtype=bf16)
    base_out, sums_out = vector(len(OWN), 2, BS, BS), vector(len(SUMS), BS, BS)
    early_out, late_out = vector(len(EARLY), BS, BS), vector(len(LATE), BS, BS)
    out = (jax.ShapeDtypeStruct(whole, f32), BIG)

    far, near, table, h, x, sums, early, re_in, im_in = call(
        own_first,
        [BIG] * 5 + [SCALAR],
        [
            vector(FIRST_ROWS + MORE, BS),
            vector(FIRST_ROWS, BS),
            vector(TABLE_ROWS, BS),
            h_out,
            x_out,
            sums_out,
            early_out,
            vector(*whole),
            vector(*whole),
        ],
        [pltpu.VMEM(whole, f32)] * 2 + [pltpu.SMEM(pattern.shape, jnp.int32), dma((5,))],
    )(*inputs, field)
    far = lax.ppermute(far, RING, cross)
    near = lax.ppermute(near, RING, pair)
    x, sums, base = call(
        rest_first,
        [VECTOR] * 7,
        [x_out, sums_out, base_out],
        aliases={5: 0, 6: 1},
    )(re_in, im_in, table, early, h, x, sums)
    h, x, sums, base, inner_state = call(
        near_first,
        [VECTOR] * 6,
        [h_out, x_out, sums_out, base_out, vector(BS, BS)],
        aliases={2: 0, 3: 1, 4: 2, 5: 3},
    )(near, table, h, x, sums, base)
    h, x, sums, late, early, far, near = call(
        far_first,
        [VECTOR] * 6,
        [
            h_out,
            x_out,
            sums_out,
            late_out,
            early_out,
            vector(SECOND_ROWS + MORE, BS),
            vector(SECOND_ROWS, BS),
        ],
        aliases={3: 0, 4: 1, 5: 2},
    )(far, table, inner_state, h, x, sums)
    far = lax.ppermute(far, RING, cross)
    near = lax.ppermute(near, RING, pair)
    x, sums, base = call(
        rest_second,
        [VECTOR] * 7,
        [x_out, sums_out, base_out],
        aliases={4: 0, 5: 1, 6: 2},
    )(late, early, table, h, x, sums, base)
    x, sums, base, out_re, out_im = call(
        near_second,
        [VECTOR] * 6,
        [x_out, sums_out, base_out, out, out],
        [dma((4,))],
        aliases={3: 0, 4: 1, 5: 2},
    )(near, table, h, x, sums, base)
    _, out_re, out_im = call(
        far_second,
        [VECTOR] * 6 + [BIG] * 2,
        [x_out, out, out],
        [pltpu.VMEM((4, 2, BS, BS), f32), dma((8,))],
        aliases={5: 0, 6: 1, 7: 2},
    )(far, table, sums, base, h, x, out_re, out_im)
    return out_re, out_im


def solution(mesh):
    in_specs = (
        P(("row", "col"), None, None, None),
        P(("row", "col"), None, None, None),
        P(("row", "col"), None, None, None),
        P(("parts", "row", "col"), None, None, None),
        P("parts"),
        P(None, ("row", "col"), None),
    )
    out_specs = (
        P(("parts", "row", "col"), None, None, None),
        P(("parts", "row", "col"), None, None, None),
    )
    return jax.shard_map(body, mesh=mesh, in_specs=in_specs, out_specs=out_specs, check_vma=False)
```

```python
import functools

import jax
import jax.numpy as jnp
from jax import lax
from jax.experimental import pallas as pl
from jax.experimental.pallas import tpu as pltpu
from jax.sharding import PartitionSpec as P

TERMS = 6
BS = 128
time_step = 0.5
RING = ("row", "col")
f32, bf16 = jnp.float32, jnp.bfloat16

ROWS = 6
SIGN_RE = (1.0, -1.0, -1.0, 1.0, 1.0, -1.0)
SIGN_IM = (-1.0, -1.0, 1.0, 1.0, -1.0, -1.0)
FIRST_ROWS = 4 * BS
SECOND_ROWS = 3 * BS
MORE = 8
TABLE_ROWS = 24


def own_index(row, offset):
    core = lax.axis_index("col")
    return jnp.where(core == 0, row, 1 - row), jnp.where(core == 0, 1 + offset, 1 - offset)


def own(ref, row, offset):
    r, e = own_index(row, offset)
    return ref[r, e]


def slot(ref, index):
    return ref[index * BS : (index + 1) * BS, :]


def line(ref, index):
    return ref[index : index + 1, :]


class Band:
    def __init__(self, ref, negated=False):
        self.high, self.low = ref.at[0], ref.at[1]
        self.minus = Band(ref.at[pl.ds(2, 2)]) if negated else None

    def put(self, i, j, value):
        part = slice((j - i + 1) * BS, (j - i + 2) * BS)
        high = value.astype(bf16)
        low = (value - high.astype(f32)).astype(bf16)
        self.high[i, :, part] = high
        self.low[i, :, part] = low
        if self.minus is not None:
            self.minus.high[i, :, part] = -high
            self.minus.low[i, :, part] = -low

    def left(self, i, first, last):
        part = slice((first - i + 1) * BS, (last - i + 2) * BS)
        high, low = self.high[i, :, part], self.low[i, :, part]
        return [high, high, low]

    def right(self, first, last, j, j_last):
        highs, lows = [], []
        for k in range(first, last + 1):
            part = slice((j - k + 1) * BS, (j_last - k + 2) * BS)
            highs.append(self.high[k, :, part])
            lows.append(self.low[k, :, part])
        return highs + lows + highs


def piece(h, x, rows, mids, cols):
    after_h = jnp.concatenate(x.right(*mids, *cols), axis=0)
    after_x = jnp.concatenate(h.minus.right(*mids, *cols), axis=0)

    def product(left, right):
        return jnp.dot(jnp.concatenate(left, axis=1), right, preferred_element_type=f32)

    return [product(h.left(i, *mids), after_h) + product(x.left(i, *mids), after_x) for i in rows]


def one_side(a, b, row, mids, col):
    left = jnp.concatenate(a.left(row, *mids), axis=1)
    right = jnp.concatenate(b.right(*mids, col, col), axis=0)
    return jnp.dot(left, right, preferred_element_type=f32)


def tile(h, x, i):
    upper, lower = piece(h, x, (i, i + 1), (i, i + 1), (i, i + 1))
    return upper[:, :BS], upper[:, BS:], lower[:, :BS], lower[:, BS:]


def part(h, x, i, k, j):
    return piece(h, x, (i,), (k, k), (j, j))[0]


def coefficient(term):
    return time_step / (term + 1)


SUMS = ((1, 2, 1), (1, 1, 2), (1, 3, 4), (1, 4, 3), (2, 2, 2), (2, 3, 3), (3, 2, 2), (3, 3, 3), (3, 2, 3), (3, 3, 2))
OWN = (((0, -1), (2, 1)), ((0, 0), (2, 2)), ((0, 1), (2, 3)), ((1, -1), (3, 2)), ((1, 0), (3, 3)), ((1, 1), (3, 4)))
EARLY = ((1, 2, 2), (1, 3, 3), (1, 2, 3), (1, 3, 2))
LATE = ((1, 2, 1), (1, 1, 2), (2, 2, 1), (2, 1, 2), (3, 2, 1), (3, 1, 2), (2, 2, 2), (3, 2, 2), (3, 2, 3), (3, 3, 2))
DONE_EARLY = {(2, 2): (1,), (2, 3): (1, 2), (3, 2): (1, 2), (3, 3): (1,)}
DONE_NEAR = {(3, 3): (2, 3), (3, 4): (1, 2, 3)}
DONE_FAR = {(2, 1): (1, 2, 3), (2, 2): (2, 3), (2, 3): (3,), (3, 2): (3,)}


def weighted(terms_of, signs):
    total = None
    for sign, value in zip(signs, terms_of):
        total = (value if sign > 0 else -value) if total is None else (total + value if sign > 0 else total - value)
    return total


def parts_of(values, i, j, terms):
    re_signs, im_signs = [SIGN_RE[term] for term in terms], [SIGN_IM[term] for term in terms]
    here = [values[(term, i, j)] for term in terms]
    there = here if i == j else [values[(term, j, i)] for term in terms]
    real = 0.5 * (weighted(here, re_signs) + weighted(there, re_signs).T)
    imag = 0.5 * (weighted(here, im_signs) - weighted(there, im_signs).T)
    return real, imag


def add_terms(base, values, done, phase):
    for index, (_, (i, j)) in enumerate(OWN):
        terms = [level - 1 + 3 * phase for level in done.get((i, j), ())]
        if terms:
            real, imag = parts_of(values, i, j, terms)
            base[index, 0] = base[index, 0] + real
            base[index, 1] = base[index, 1] + imag


def views(h_ref, x_ref):
    return Band(h_ref, True), [Band(x_ref.at[level]) for level in range(3)]


def before_send(h, xs, phase, table, sums, early, far, near):
    x0, x1, _ = xs
    term = 3 * phase
    t = tile(h, x0, 2)
    scale = line(table, 6 + term)
    inner = {
        (2, 2): (t[0] + part(h, x0, 2, 1, 2)) * coefficient(term),
        (3, 3): (t[3] + part(h, x0, 3, 4, 3)) * coefficient(term),
        (2, 3): t[1] * scale,
        (3, 2): t[2] * scale,
    }
    for (i, j), value in inner.items():
        x1.put(i, j, value)
    far[BS : 2 * BS, :] = inner[(2, 2)]
    near[BS : 2 * BS, :] = inner[(3, 3)]
    for index, (_, i, j) in enumerate(EARLY):
        early[index] = inner[(i, j)]
    for out, i, k in ((far, 2, 3), (near, 3, 2)):
        value = part(h, x1, i, k, i)
        out[2 * BS : 3 * BS, :] = value
        sums[SUMS.index((2, i, i))] = value


def own_first(
    re, im, ham, dip, pattern_in, field,
    far, near, table, h_ref, x_ref, sums, early, re_in, im_in,
    ham_in, dip_in, pattern, sems,
):
    copies = [
        pltpu.make_async_copy(source, target, sems.at[n])
        for n, (source, target) in enumerate(
            ((pattern_in, pattern), (ham, ham_in), (dip, dip_in), (re, re_in), (im, im_in))
        )
    ]
    for copy in copies:
        copy.start()
    copies[0].wait()
    for n, (row, offset) in enumerate(((0, -1), (0, 1), (1, 1))):
        r, e = own_index(row, offset)
        for term in range(TERMS):
            table[6 * n + term : 6 * n + term + 1, :] = jnp.full(
                (1, BS), pattern[e, r, term].astype(f32) * coefficient(term), f32
            )
    h, xs = views(h_ref, x_ref)
    for copy in copies[1:3]:
        copy.wait()
    for (row, offset), (i, j) in OWN:
        value = own(ham_in, row, offset) + field[0] * own(dip_in, row, offset)
        h.put(i, j, value)
        if j in (1, 4):
            h.put(j, i, value.T)
        if i == j:
            (far if i == 2 else near)[3 * BS : 4 * BS, :] = value
    for copy in copies[3:]:
        copy.wait()
    for (row, offset), (i, j) in OWN:
        real, imag = own(re_in, row, offset), own(im_in, row, offset)
        xs[0].put(i, j, real + imag)
        if j in (1, 4):
            xs[0].put(j, i, (real - imag).T)
        if i == j:
            (far if i == 2 else near)[0:BS, :] = real + imag
    before_send(h, xs, 0, table, sums, early, far, near)


def own_rest(h, xs, phase, table, early, base, sums):
    x0, x1, x2 = xs
    term = 3 * phase
    values = {(term, i, j): early[index] for index, (_, i, j) in enumerate(EARLY)}
    t = tile(h, x1, 2)
    scale = line(table, 6 + term + 1)
    for (i, j), value in (((2, 3), t[1] * scale), ((3, 2), t[2] * scale)):
        x2.put(i, j, value)
        values[(term + 1, i, j)] = value
    for a, b in ((3, 4), (2, 1)):
        sums[SUMS.index((1, a, b))] = part(h, x0, a, a, b)
        sums[SUMS.index((1, b, a))] = part(h, x0, b, a, a)
    sums[SUMS.index((3, 2, 2))] = part(h, x2, 2, 3, 2)
    sums[SUMS.index((3, 3, 3))] = part(h, x2, 3, 2, 3)
    add_terms(base, values, DONE_EARLY, phase)


def side(h, xs, a, b, payload, phase, scales, sums, record):
    x0, x1, x2 = xs
    c = [coefficient(3 * phase + n) for n in range(3)]
    low = min(a, b)
    at_a, at_b = (0, 3) if a == low else (3, 0)
    up, down = (low, low + 1), (low + 1, low)

    def known(level, i, j):
        return sums[SUMS.index((level, i, j))]

    def put(level, i, j, value):
        record(level, i, j, value)
        if level < 3:
            xs[level].put(i, j, value)

    x0.put(b, b, slot(payload, 0))
    x1.put(b, b, slot(payload, 1))
    put(1, a, b, (part(h, x0, a, b, b) + known(1, a, b)) * scales[0])
    put(1, b, a, (part(h, x0, b, b, a) + known(1, b, a)) * scales[0])
    t = tile(h, x1, low)
    put(2, a, a, (t[at_a] + known(2, a, a)) * c[1])
    put(2, b, b, (t[at_b] + slot(payload, 2)) * c[1])
    put(2, *up, t[1] * scales[1])
    put(2, *down, t[2] * scales[1])
    t = tile(h, x2, low)
    put(3, *up, t[1] * scales[2])
    put(3, *down, t[2] * scales[2])
    put(3, a, a, (t[at_a] + known(3, a, a)) * c[2])


def near_side(h, xs, near, phase, table, base, sums):
    term = 3 * phase
    values = {}

    def record(level, i, j, value):
        values[(term + level - 1, i, j)] = value

    scales = [line(table, 12 + term + n) for n in range(3)]
    side(h, xs, 3, 4, near, phase, scales, sums, record)
    x2 = xs[2]
    sums[SUMS.index((3, 2, 3))] = one_side(h, x2, 2, (2, 3), 3) + one_side(x2, h.minus, 2, (3, 3), 3)
    sums[SUMS.index((3, 3, 2))] = one_side(h, x2, 3, (3, 3), 2) + one_side(x2, h.minus, 3, (2, 3), 2)
    add_terms(base, values, DONE_NEAR, phase)
    return values


def far_side(h, xs, far, phase, table, sums, record):
    term = 3 * phase
    scales = [line(table, term + n) for n in range(3)]
    side(h, xs, 2, 1, far, phase, scales, sums, record)
    x2 = xs[2]
    scale = line(table, 6 + term + 2)
    record(3, 2, 3, (one_side(x2, h.minus, 2, (2, 2), 3) + sums[SUMS.index((3, 2, 3))]) * scale)
    record(3, 3, 2, (one_side(h, x2, 3, (2, 2), 2) + sums[SUMS.index((3, 3, 2))]) * scale)


def rest_first(re_in, im_in, table, early, h_ref, x_in, sums_in, x_ref, sums, base):
    h, xs = views(h_ref, x_ref)
    for index, ((row, offset), _) in enumerate(OWN):
        base[index, 0], base[index, 1] = own(re_in, row, offset), own(im_in, row, offset)
    own_rest(h, xs, 0, table, early, base, sums)


def near_first(near, table, h_in, x_in, sums_in, base_in, h_ref, x_ref, sums, base, inner_state):
    h, xs = views(h_ref, x_ref)
    h.put(4, 4, slot(near, 3))
    values = near_side(h, xs, near, 0, table, base, sums)
    for i, j in ((3, 3), (3, 4), (4, 3)):
        xs[0].put(i, j, values[(2, i, j)])
    inner_state[...] = values[(2, 3, 3)]


def far_first(far, table, inner_state, h_in, x_in, sums_in, h_ref, x_ref, sums, late, early, far_next, near_next):
    h, xs = views(h_ref, x_ref)
    h.put(1, 1, slot(far, 3))
    state = {}

    def record(level, i, j, value):
        if (level, i, j) in LATE:
            late[LATE.index((level, i, j))] = value
        if level == 3:
            state[(i, j)] = value

    far_side(h, xs, far, 0, table, sums, record)
    for (i, j), value in state.items():
        xs[0].put(i, j, value)
    far_next[0:BS, :] = state[(2, 2)]
    near_next[0:BS, :] = inner_state[...]
    before_send(h, xs, 1, table, sums, early, far_next, near_next)


def rest_second(late, early, table, h_ref, x_in, sums_in, base_in, x_ref, sums, base):
    h, xs = views(h_ref, x_ref)
    values = {(level - 1, i, j): late[index] for index, (level, i, j) in enumerate(LATE)}
    add_terms(base, values, DONE_FAR, 0)
    own_rest(h, xs, 1, table, early, base, sums)


def near_second(near, table, h_ref, x_in, sums_in, base_in, x_ref, sums, base):
    h, xs = views(h_ref, x_ref)
    near_side(h, xs, near, 1, table, base, sums)


def far_second(far, table, sums, base, h_ref, x_in, x_ref, out_re, out_im, stage, sems):
    h, xs = views(h_ref, x_ref)
    outs = (out_re, out_im)

    def start(index, source):
        row, offset = OWN[index][0]
        r, e = own_index(row, offset)
        for a, out in enumerate(outs):
            copies.append(pltpu.make_async_copy(source.at[index, a], out.at[r, e], sems.at[len(copies)]))
            copies[-1].start()

    copies = []
    for index in (4, 5):
        start(index, base)
    values = {}

    def record(level, i, j, value):
        values[(level + 2, i, j)] = value

    far_side(h, xs, far, 1, table, sums, record)
    for index in (2, 3, 0, 1):
        i, j = OWN[index][1]
        real, imag = parts_of(values, i, j, [level + 2 for level in DONE_FAR[(i, j)]])
        stage[index, 0], stage[index, 1] = base[index, 0] + real, base[index, 1] + imag
        start(index, stage)
    for copy in copies:
        copy.wait()


VECTOR = pl.BlockSpec(memory_space=pltpu.VMEM)
SCALAR = pl.BlockSpec(memory_space=pltpu.SMEM)
BIG = pl.BlockSpec(memory_space=pltpu.HBM)


def call(kernel, ins, outs, scratch=(), aliases=None):
    return pl.pallas_call(
        kernel,
        out_shape=[shape for shape, _ in outs],
        in_specs=ins,
        out_specs=[spec for _, spec in outs],
        scratch_shapes=list(scratch),
        input_output_aliases=aliases or {},
        compiler_params=pltpu.CompilerParams(vmem_limit_bytes=24 * 2**20),
        cost_estimate=pl.CostEstimate(flops=0, bytes_accessed=0, transcendentals=0),
    )


def vector(*shape, dtype=f32):
    return jax.ShapeDtypeStruct(shape, dtype), VECTOR


def body(density_real, density_imag, hamiltonian, dipole, field, pattern):
    count = lax.axis_size(RING)
    pair = [(i, i ^ 1) for i in range(count)]
    cross = [(i, (i + 1) % count if i % 2 else (i - 1) % count) for i in range(count)]
    pattern = jnp.transpose(pattern, (2, 1, 0))
    whole = density_real.shape
    inputs = [
        pltpu.with_memory_space_constraint(x, pltpu.HBM)
        for x in (density_real, density_imag, hamiltonian, dipole, pattern)
    ]
    dma = pltpu.SemaphoreType.DMA
    h_out, x_out = vector(4, ROWS, BS, 3 * BS, dtype=bf16), vector(3, 2, ROWS, BS, 3 * BS, dtype=bf16)
    base_out, sums_out = vector(len(OWN), 2, BS, BS), vector(len(SUMS), BS, BS)
    early_out, late_out = vector(len(EARLY), BS, BS), vector(len(LATE), BS, BS)
    out = (jax.ShapeDtypeStruct(whole, f32), BIG)

    far, near, table, h, x, sums, early, re_in, im_in = call(
        own_first,
        [BIG] * 5 + [SCALAR],
        [
            vector(FIRST_ROWS + MORE, BS),
            vector(FIRST_ROWS, BS),
            vector(TABLE_ROWS, BS),
            h_out,
            x_out,
            sums_out,
            early_out,
            vector(*whole),
            vector(*whole),
        ],
        [pltpu.VMEM(whole, f32)] * 2 + [pltpu.SMEM(pattern.shape, jnp.int32), dma((5,))],
    )(*inputs, field)
    far = lax.ppermute(far, RING, cross)
    near = lax.ppermute(near, RING, pair)
    x, sums, base = call(
        rest_first,
        [VECTOR] * 7,
        [x_out, sums_out, base_out],
        aliases={5: 0, 6: 1},
    )(re_in, im_in, table, early, h, x, sums)
    h, x, sums, base, inner_state = call(
        near_first,
        [VECTOR] * 6,
        [h_out, x_out, sums_out, base_out, vector(BS, BS)],
        aliases={2: 0, 3: 1, 4: 2, 5: 3},
    )(near, table, h, x, sums, base)
    h, x, sums, late, early, far, near = call(
        far_first,
        [VECTOR] * 6,
        [
            h_out,
            x_out,
            sums_out,
            late_out,
            early_out,
            vector(SECOND_ROWS + MORE, BS),
            vector(SECOND_ROWS, BS),
        ],
        aliases={3: 0, 4: 1, 5: 2},
    )(far, table, inner_state, h, x, sums)
    far = lax.ppermute(far, RING, cross)
    near = lax.ppermute(near, RING, pair)
    x, sums, base = call(
        rest_second,
        [VECTOR] * 7,
        [x_out, sums_out, base_out],
        aliases={4: 0, 5: 1, 6: 2},
    )(late, early, table, h, x, sums, base)
    x, sums, base = call(
        near_second,
        [VECTOR] * 6,
        [x_out, sums_out, base_out],
        aliases={3: 0, 4: 1, 5: 2},
    )(near, table, h, x, sums, base)
    _, out_re, out_im = call(
        far_second,
        [VECTOR] * 6,
        [x_out, out, out],
        [pltpu.VMEM((4, 2, BS, BS), f32), dma((12,))],
        aliases={5: 0},
    )(far, table, sums, base, h, x)
    return out_re, out_im


def solution(mesh):
    in_specs = (
        P(("row", "col"), None, None, None),
        P(("row", "col"), None, None, None),
        P(("row", "col"), None, None, None),
        P(("parts", "row", "col"), None, None, None),
        P("parts"),
        P(None, ("row", "col"), None),
    )
    out_specs = (
        P(("parts", "row", "col"), None, None, None),
        P(("parts", "row", "col"), None, None, None),
    )
    return jax.shard_map(body, mesh=mesh, in_specs=in_specs, out_specs=out_specs, check_vma=False)
```

```python
import functools

import jax
import jax.numpy as jnp
from jax import lax
from jax.experimental import pallas as pl
from jax.experimental.pallas import tpu as pltpu
from jax.sharding import PartitionSpec as P

TERMS = 6
BS = 128
time_step = 0.5
RING = ("row", "col")
f32, bf16 = jnp.float32, jnp.bfloat16

ROWS = 6
SIGN_RE = (1.0, -1.0, -1.0, 1.0, 1.0, -1.0)
SIGN_IM = (-1.0, -1.0, 1.0, 1.0, -1.0, -1.0)
FIRST_ROWS = 4 * BS
SECOND_ROWS = 3 * BS
MORE = 8
TABLE_ROWS = 24


def own_index(row, offset):
    core = lax.axis_index("col")
    return jnp.where(core == 0, row, 1 - row), jnp.where(core == 0, 1 + offset, 1 - offset)


def own(ref, row, offset):
    r, e = own_index(row, offset)
    return ref[r, e]


def slot(ref, index):
    return ref[index * BS : (index + 1) * BS, :]


def line(ref, index):
    return ref[index : index + 1, :]


class Band:
    def __init__(self, ref, negated=False):
        self.high, self.low = ref.at[0], ref.at[1]
        self.minus = Band(ref.at[pl.ds(2, 2)]) if negated else None

    def put(self, i, j, value):
        part = slice((j - i + 1) * BS, (j - i + 2) * BS)
        high = value.astype(bf16)
        low = (value - high.astype(f32)).astype(bf16)
        self.high[i, :, part] = high
        self.low[i, :, part] = low
        if self.minus is not None:
            self.minus.high[i, :, part] = -high
            self.minus.low[i, :, part] = -low

    def left(self, i, first, last):
        part = slice((first - i + 1) * BS, (last - i + 2) * BS)
        high, low = self.high[i, :, part], self.low[i, :, part]
        return [high, high, low]

    def right(self, first, last, j, j_last):
        highs, lows = [], []
        for k in range(first, last + 1):
            part = slice((j - k + 1) * BS, (j_last - k + 2) * BS)
            highs.append(self.high[k, :, part])
            lows.append(self.low[k, :, part])
        return highs + lows + highs


def piece(h, x, rows, mids, cols):
    after_h = jnp.concatenate(x.right(*mids, *cols), axis=0)
    after_x = jnp.concatenate(h.minus.right(*mids, *cols), axis=0)

    def product(left, right):
        return jnp.dot(jnp.concatenate(left, axis=1), right, preferred_element_type=f32)

    return [product(h.left(i, *mids), after_h) + product(x.left(i, *mids), after_x) for i in rows]


def one_side(a, b, row, mids, col):
    left = jnp.concatenate(a.left(row, *mids), axis=1)
    right = jnp.concatenate(b.right(*mids, col, col), axis=0)
    return jnp.dot(left, right, preferred_element_type=f32)


def tile(h, x, i):
    upper, lower = piece(h, x, (i, i + 1), (i, i + 1), (i, i + 1))
    return upper[:, :BS], upper[:, BS:], lower[:, :BS], lower[:, BS:]


def part(h, x, i, k, j):
    return piece(h, x, (i,), (k, k), (j, j))[0]


def coefficient(term):
    return time_step / (term + 1)


SUMS = ((1, 2, 1), (1, 1, 2), (1, 3, 4), (1, 4, 3), (2, 2, 2), (2, 3, 3), (3, 2, 2), (3, 3, 3), (3, 2, 3), (3, 3, 2))
OWN = (((0, -1), (2, 1)), ((0, 0), (2, 2)), ((0, 1), (2, 3)), ((1, -1), (3, 2)), ((1, 0), (3, 3)), ((1, 1), (3, 4)))
EARLY = ((1, 2, 2), (1, 3, 3), (1, 2, 3), (1, 3, 2))
LATE = ((1, 2, 1), (1, 1, 2), (2, 2, 1), (2, 1, 2), (3, 2, 1), (3, 1, 2), (2, 2, 2), (3, 2, 2), (3, 2, 3), (3, 3, 2))
DONE_EARLY = {(2, 2): (1,), (2, 3): (1, 2), (3, 2): (1, 2), (3, 3): (1,)}
DONE_NEAR = {(3, 3): (2, 3), (3, 4): (1, 2, 3)}
DONE_FAR = {(2, 1): (1, 2, 3), (2, 2): (2, 3), (2, 3): (3,), (3, 2): (3,)}


def weighted(terms_of, signs):
    total = None
    for sign, value in zip(signs, terms_of):
        total = (value if sign > 0 else -value) if total is None else (total + value if sign > 0 else total - value)
    return total


def parts_of(values, i, j, terms):
    re_signs, im_signs = [SIGN_RE[term] for term in terms], [SIGN_IM[term] for term in terms]
    here = [values[(term, i, j)] for term in terms]
    there = here if i == j else [values[(term, j, i)] for term in terms]
    real = 0.5 * (weighted(here, re_signs) + weighted(there, re_signs).T)
    imag = 0.5 * (weighted(here, im_signs) - weighted(there, im_signs).T)
    return real, imag


def add_terms(base, values, done, phase):
    for index, (_, (i, j)) in enumerate(OWN):
        terms = [level - 1 + 3 * phase for level in done.get((i, j), ())]
        if terms:
            real, imag = parts_of(values, i, j, terms)
            base[index, 0] = base[index, 0] + real
            base[index, 1] = base[index, 1] + imag


def views(h_ref, x_ref):
    return Band(h_ref, True), [Band(x_ref.at[level]) for level in range(3)]


def before_far(h, xs, phase, table, sums, early, far, carry):
    x0, x1, _ = xs
    term = 3 * phase
    t = tile(h, x0, 2)
    scale = line(table, 6 + term)
    inner = {
        (2, 2): (t[0] + part(h, x0, 2, 1, 2)) * coefficient(term),
        (2, 3): t[1] * scale,
        (3, 2): t[2] * scale,
    }
    for (i, j), value in inner.items():
        x1.put(i, j, value)
        early[EARLY.index((1, i, j))] = value
    carry[...] = t[3]
    far[BS : 2 * BS, :] = inner[(2, 2)]
    value = part(h, x1, 2, 3, 2)
    far[2 * BS : 3 * BS, :] = value
    sums[SUMS.index((2, 2, 2))] = value


def before_near(carry, h_ref, near_in, x_in, sums_in, early_in, near, x_ref, sums, early, *, phase):
    h, (x0, x1, _) = views(h_ref, x_ref)
    value = (carry[...] + part(h, x0, 3, 4, 3)) * coefficient(3 * phase)
    x1.put(3, 3, value)
    early[EARLY.index((1, 3, 3))] = value
    near[BS : 2 * BS, :] = value
    value = part(h, x1, 3, 2, 3)
    near[2 * BS : 3 * BS, :] = value
    sums[SUMS.index((2, 3, 3))] = value


def own_first(
    re, im, ham, dip, pattern_in, field,
    far, near, table, h_ref, x_ref, sums, early, carry, re_in, im_in,
    ham_in, dip_in, pattern, sems,
):
    copies = [
        pltpu.make_async_copy(source, target, sems.at[n])
        for n, (source, target) in enumerate(
            ((pattern_in, pattern), (ham, ham_in), (dip, dip_in), (re, re_in), (im, im_in))
        )
    ]
    for copy in copies:
        copy.start()
    copies[0].wait()
    for n, (row, offset) in enumerate(((0, -1), (0, 1), (1, 1))):
        r, e = own_index(row, offset)
        for term in range(TERMS):
            table[6 * n + term : 6 * n + term + 1, :] = jnp.full(
                (1, BS), pattern[e, r, term].astype(f32) * coefficient(term), f32
            )
    h, xs = views(h_ref, x_ref)
    for copy in copies[1:3]:
        copy.wait()
    for (row, offset), (i, j) in OWN:
        value = own(ham_in, row, offset) + field[0] * own(dip_in, row, offset)
        h.put(i, j, value)
        if j in (1, 4):
            h.put(j, i, value.T)
        if i == j:
            (far if i == 2 else near)[3 * BS : 4 * BS, :] = value
    for copy in copies[3:]:
        copy.wait()
    for (row, offset), (i, j) in OWN:
        real, imag = own(re_in, row, offset), own(im_in, row, offset)
        xs[0].put(i, j, real + imag)
        if j in (1, 4):
            xs[0].put(j, i, (real - imag).T)
        if i == j:
            (far if i == 2 else near)[0:BS, :] = real + imag
    before_far(h, xs, 0, table, sums, early, far, carry)


def own_rest(h, xs, phase, table, early, base, sums):
    x0, x1, x2 = xs
    term = 3 * phase
    values = {(term, i, j): early[index] for index, (_, i, j) in enumerate(EARLY)}
    t = tile(h, x1, 2)
    scale = line(table, 6 + term + 1)
    for (i, j), value in (((2, 3), t[1] * scale), ((3, 2), t[2] * scale)):
        x2.put(i, j, value)
        values[(term + 1, i, j)] = value
    for a, b in ((3, 4), (2, 1)):
        sums[SUMS.index((1, a, b))] = part(h, x0, a, a, b)
        sums[SUMS.index((1, b, a))] = part(h, x0, b, a, a)
    sums[SUMS.index((3, 2, 2))] = part(h, x2, 2, 3, 2)
    sums[SUMS.index((3, 3, 3))] = part(h, x2, 3, 2, 3)
    add_terms(base, values, DONE_EARLY, phase)


def side(h, xs, a, b, payload, phase, scales, sums, record):
    x0, x1, x2 = xs
    c = [coefficient(3 * phase + n) for n in range(3)]
    low = min(a, b)
    at_a, at_b = (0, 3) if a == low else (3, 0)
    up, down = (low, low + 1), (low + 1, low)

    def known(level, i, j):
        return sums[SUMS.index((level, i, j))]

    def put(level, i, j, value):
        record(level, i, j, value)
        if level < 3:
            xs[level].put(i, j, value)

    x0.put(b, b, slot(payload, 0))
    x1.put(b, b, slot(payload, 1))
    put(1, a, b, (part(h, x0, a, b, b) + known(1, a, b)) * scales[0])
    put(1, b, a, (part(h, x0, b, b, a) + known(1, b, a)) * scales[0])
    t = tile(h, x1, low)
    put(2, a, a, (t[at_a] + known(2, a, a)) * c[1])
    put(2, b, b, (t[at_b] + slot(payload, 2)) * c[1])
    put(2, *up, t[1] * scales[1])
    put(2, *down, t[2] * scales[1])

    def last():
        t = tile(h, x2, low)
        put(3, *up, t[1] * scales[2])
        put(3, *down, t[2] * scales[2])
        put(3, a, a, (t[at_a] + known(3, a, a)) * c[2])

    return last


def near_side(h, xs, near, phase, table, base, sums):
    term = 3 * phase
    values = {}

    def record(level, i, j, value):
        values[(term + level - 1, i, j)] = value

    scales = [line(table, 12 + term + n) for n in range(3)]
    side(h, xs, 3, 4, near, phase, scales, sums, record)()
    x2 = xs[2]
    sums[SUMS.index((3, 2, 3))] = one_side(h, x2, 2, (2, 3), 3) + one_side(x2, h.minus, 2, (3, 3), 3)
    sums[SUMS.index((3, 3, 2))] = one_side(h, x2, 3, (3, 3), 2) + one_side(x2, h.minus, 3, (2, 3), 2)
    add_terms(base, values, DONE_NEAR, phase)
    return values


def far_side(h, xs, far, phase, table, sums, record, between=lambda: None):
    term = 3 * phase
    scales = [line(table, term + n) for n in range(3)]
    last = side(h, xs, 2, 1, far, phase, scales, sums, record)
    x2 = xs[2]
    scale = line(table, 6 + term + 2)
    record(3, 2, 3, (one_side(x2, h.minus, 2, (2, 2), 3) + sums[SUMS.index((3, 2, 3))]) * scale)
    record(3, 3, 2, (one_side(h, x2, 3, (2, 2), 2) + sums[SUMS.index((3, 3, 2))]) * scale)
    between()
    last()


def rest_first(re_in, im_in, table, early, h_ref, x_in, sums_in, x_ref, sums, base):
    h, xs = views(h_ref, x_ref)
    for index, ((row, offset), _) in enumerate(OWN):
        base[index, 0], base[index, 1] = own(re_in, row, offset), own(im_in, row, offset)
    own_rest(h, xs, 0, table, early, base, sums)


def near_first(near, table, h_in, x_in, sums_in, base_in, h_ref, x_ref, sums, base, inner_state):
    h, xs = views(h_ref, x_ref)
    h.put(4, 4, slot(near, 3))
    values = near_side(h, xs, near, 0, table, base, sums)
    for i, j in ((3, 3), (3, 4), (4, 3)):
        xs[0].put(i, j, values[(2, i, j)])
    inner_state[...] = values[(2, 3, 3)]


def far_first(
    far, table, inner_state, h_in, x_in, sums_in, h_ref, x_ref, sums, late, early, far_next, near_next, carry
):
    h, xs = views(h_ref, x_ref)
    h.put(1, 1, slot(far, 3))
    state = {}

    def record(level, i, j, value):
        if (level, i, j) in LATE:
            late[LATE.index((level, i, j))] = value
        if level == 3:
            state[(i, j)] = value

    far_side(h, xs, far, 0, table, sums, record)
    for (i, j), value in state.items():
        xs[0].put(i, j, value)
    far_next[0:BS, :] = state[(2, 2)]
    near_next[0:BS, :] = inner_state[...]
    before_far(h, xs, 1, table, sums, early, far_next, carry)


def rest_second(late, early, table, h_ref, x_in, sums_in, base_in, x_ref, sums, base):
    h, xs = views(h_ref, x_ref)
    values = {(level - 1, i, j): late[index] for index, (level, i, j) in enumerate(LATE)}
    add_terms(base, values, DONE_FAR, 0)
    own_rest(h, xs, 1, table, early, base, sums)


def near_second(near, table, h_ref, x_in, sums_in, base_in, x_ref, sums, base):
    h, xs = views(h_ref, x_ref)
    near_side(h, xs, near, 1, table, base, sums)


def far_second(far, table, sums, base, h_ref, x_in, x_ref, out_re, out_im, stage, sems):
    h, xs = views(h_ref, x_ref)
    copies = []
    for index, ((row, offset), _) in enumerate(OWN):
        r, e = own_index(row, offset)
        source = stage if index < 4 else base
        for a, out in enumerate((out_re, out_im)):
            copies.append(pltpu.make_async_copy(source.at[index, a], out.at[r, e], sems.at[len(copies)]))

    def send(first):
        for copy in copies[2 * first : 2 * first + 4]:
            copy.start()

    def apart(first):
        pl.when(lax.axis_index("col") >= 0)(lambda: send(first))

    apart(4)
    values = {}

    def record(level, i, j, value):
        values[(level + 2, i, j)] = value

    def finish(index):
        i, j = OWN[index][1]
        real, imag = parts_of(values, i, j, [level + 2 for level in DONE_FAR[(i, j)]])
        stage[index, 0], stage[index, 1] = base[index, 0] + real, base[index, 1] + imag

    def between():
        finish(2)
        finish(3)
        apart(2)

    far_side(h, xs, far, 1, table, sums, record, between)
    finish(0)
    finish(1)
    send(0)
    for copy in copies:
        copy.wait()


VECTOR = pl.BlockSpec(memory_space=pltpu.VMEM)
SCALAR = pl.BlockSpec(memory_space=pltpu.SMEM)
BIG = pl.BlockSpec(memory_space=pltpu.HBM)


def call(kernel, ins, outs, scratch=(), aliases=None):
    return pl.pallas_call(
        kernel,
        out_shape=[shape for shape, _ in outs],
        in_specs=ins,
        out_specs=[spec for _, spec in outs],
        scratch_shapes=list(scratch),
        input_output_aliases=aliases or {},
        compiler_params=pltpu.CompilerParams(vmem_limit_bytes=24 * 2**20),
        cost_estimate=pl.CostEstimate(flops=0, bytes_accessed=0, transcendentals=0),
    )


def vector(*shape, dtype=f32):
    return jax.ShapeDtypeStruct(shape, dtype), VECTOR


def body(density_real, density_imag, hamiltonian, dipole, field, pattern):
    count = lax.axis_size(RING)
    pair = [(i, i ^ 1) for i in range(count)]
    cross = [(i, (i + 1) % count if i % 2 else (i - 1) % count) for i in range(count)]
    pattern = jnp.transpose(pattern, (2, 1, 0))
    whole = density_real.shape
    inputs = [
        pltpu.with_memory_space_constraint(x, pltpu.HBM)
        for x in (density_real, density_imag, hamiltonian, dipole, pattern)
    ]
    dma = pltpu.SemaphoreType.DMA
    h_out, x_out = vector(4, ROWS, BS, 3 * BS, dtype=bf16), vector(3, 2, ROWS, BS, 3 * BS, dtype=bf16)
    base_out, sums_out = vector(len(OWN), 2, BS, BS), vector(len(SUMS), BS, BS)
    carry_out, early_out, late_out = vector(BS, BS), vector(len(EARLY), BS, BS), vector(len(LATE), BS, BS)
    out = (jax.ShapeDtypeStruct(whole, f32), BIG)

    far, near, table, h, x, sums, early, carry, re_in, im_in = call(
        own_first,
        [BIG] * 5 + [SCALAR],
        [
            vector(FIRST_ROWS + MORE, BS),
            vector(FIRST_ROWS, BS),
            vector(TABLE_ROWS, BS),
            h_out,
            x_out,
            sums_out,
            early_out,
            carry_out,
            vector(*whole),
            vector(*whole),
        ],
        [pltpu.VMEM(whole, f32)] * 2 + [pltpu.SMEM(pattern.shape, jnp.int32), dma((5,))],
    )(*inputs, field)
    far = lax.ppermute(far, RING, cross)
    near, x, sums, early = call(
        functools.partial(before_near, phase=0),
        [VECTOR] * 6,
        [vector(FIRST_ROWS, BS), x_out, sums_out, early_out],
        aliases={2: 0, 3: 1, 4: 2, 5: 3},
    )(carry, h, near, x, sums, early)
    near = lax.ppermute(near, RING, pair)
    x, sums, base = call(
        rest_first,
        [VECTOR] * 7,
        [x_out, sums_out, base_out],
        aliases={5: 0, 6: 1},
    )(re_in, im_in, table, early, h, x, sums)
    h, x, sums, base, inner_state = call(
        near_first,
        [VECTOR] * 6,
        [h_out, x_out, sums_out, base_out, vector(BS, BS)],
        aliases={2: 0, 3: 1, 4: 2, 5: 3},
    )(near, table, h, x, sums, base)
    h, x, sums, late, early, far, near, carry = call(
        far_first,
        [VECTOR] * 6,
        [
            h_out,
            x_out,
            sums_out,
            late_out,
            early_out,
            vector(SECOND_ROWS + MORE, BS),
            vector(SECOND_ROWS, BS),
            carry_out,
        ],
        aliases={3: 0, 4: 1, 5: 2},
    )(far, table, inner_state, h, x, sums)
    far = lax.ppermute(far, RING, cross)
    near, x, sums, early = call(
        functools.partial(before_near, phase=1),
        [VECTOR] * 6,
        [vector(SECOND_ROWS, BS), x_out, sums_out, early_out],
        aliases={2: 0, 3: 1, 4: 2, 5: 3},
    )(carry, h, near, x, sums, early)
    near = lax.ppermute(near, RING, pair)
    x, sums, base = call(
        rest_second,
        [VECTOR] * 7,
        [x_out, sums_out, base_out],
        aliases={4: 0, 5: 1, 6: 2},
    )(late, early, table, h, x, sums, base)
    x, sums, base = call(
        near_second,
        [VECTOR] * 6,
        [x_out, sums_out, base_out],
        aliases={3: 0, 4: 1, 5: 2},
    )(near, table, h, x, sums, base)
    _, out_re, out_im = call(
        far_second,
        [VECTOR] * 6,
        [x_out, out, out],
        [pltpu.VMEM((4, 2, BS, BS), f32), dma((12,))],
        aliases={5: 0},
    )(far, table, sums, base, h, x)
    return out_re, out_im


def solution(mesh):
    in_specs = (
        P(("row", "col"), None, None, None),
        P(("row", "col"), None, None, None),
        P(("row", "col"), None, None, None),
        P(("parts", "row", "col"), None, None, None),
        P("parts"),
        P(None, ("row", "col"), None),
    )
    out_specs = (
        P(("parts", "row", "col"), None, None, None),
        P(("parts", "row", "col"), None, None, None),
    )
    return jax.shard_map(body, mesh=mesh, in_specs=in_specs, out_specs=out_specs, check_vma=False)
```

```python
import functools

import jax
import jax.numpy as jnp
from jax import lax
from jax.experimental import pallas as pl
from jax.experimental.pallas import tpu as pltpu
from jax.sharding import PartitionSpec as P

TERMS = 6
BS = 128
time_step = 0.5
RING = ("row", "col")
f32, bf16 = jnp.float32, jnp.bfloat16

ROWS = 6
SIGN_RE = (1.0, -1.0, -1.0, 1.0, 1.0, -1.0)
SIGN_IM = (-1.0, -1.0, 1.0, 1.0, -1.0, -1.0)
FIRST_ROWS = 3 * BS + BS // 2 + 8
SECOND_ROWS = 3 * BS
MORE = 8
TABLE_ROWS = 24


def own_index(row, offset):
    core = lax.axis_index("col")
    return jnp.where(core == 0, row, 1 - row), jnp.where(core == 0, 1 + offset, 1 - offset)


def own(ref, row, offset):
    r, e = own_index(row, offset)
    return ref[r, e]


def slot(ref, index):
    return ref[index * BS : (index + 1) * BS, :]


def line(ref, index):
    return ref[index : index + 1, :]


class Band:
    def __init__(self, ref, negated=False):
        self.high, self.low = ref.at[0], ref.at[1]
        self.minus = Band(ref.at[pl.ds(2, 2)]) if negated else None

    def put(self, i, j, value):
        part = slice((j - i + 1) * BS, (j - i + 2) * BS)
        high = value.astype(bf16)
        low = (value - high.astype(f32)).astype(bf16)
        self.high[i, :, part] = high
        self.low[i, :, part] = low
        if self.minus is not None:
            self.minus.high[i, :, part] = -high
            self.minus.low[i, :, part] = -low

    def left(self, i, first, last):
        part = slice((first - i + 1) * BS, (last - i + 2) * BS)
        high, low = self.high[i, :, part], self.low[i, :, part]
        return [high, high, low]

    def right(self, first, last, j, j_last):
        highs, lows = [], []
        for k in range(first, last + 1):
            part = slice((j - k + 1) * BS, (j_last - k + 2) * BS)
            highs.append(self.high[k, :, part])
            lows.append(self.low[k, :, part])
        return highs + lows + highs


def piece(h, x, rows, mids, cols):
    after_h = jnp.concatenate(x.right(*mids, *cols), axis=0)
    after_x = jnp.concatenate(h.minus.right(*mids, *cols), axis=0)

    def product(left, right):
        return jnp.dot(jnp.concatenate(left, axis=1), right, preferred_element_type=f32)

    return [product(h.left(i, *mids), after_h) + product(x.left(i, *mids), after_x) for i in rows]


def one_side(a, b, row, mids, col):
    left = jnp.concatenate(a.left(row, *mids), axis=1)
    right = jnp.concatenate(b.right(*mids, col, col), axis=0)
    return jnp.dot(left, right, preferred_element_type=f32)


def tile(h, x, i):
    upper, lower = piece(h, x, (i, i + 1), (i, i + 1), (i, i + 1))
    return upper[:, :BS], upper[:, BS:], lower[:, :BS], lower[:, BS:]


def part(h, x, i, k, j):
    return piece(h, x, (i,), (k, k), (j, j))[0]


def half_places():
    shape = (BS // 2, BS)
    return lax.broadcasted_iota(jnp.int32, shape, 0), lax.broadcasted_iota(jnp.int32, shape, 1)


def swap_halves(rows):
    return jnp.concatenate([rows[:, BS // 2 :], rows[:, : BS // 2]], axis=1)


def put_symmetric(payload, block):
    r, c = half_places()
    turned = swap_halves(block[BS // 2 :])
    first = 3 * BS
    payload[first : first + BS // 2, :] = jnp.where(c < r, turned, block[: BS // 2])
    payload[first + BS // 2 : first + BS // 2 + 1, :] = jnp.sum(jnp.where(c == r, turned, 0.0), axis=0, keepdims=True)


def get_symmetric(payload):
    r, c = half_places()
    first = 3 * BS
    rows = payload[first : first + BS // 2, :]
    turned = jnp.concatenate([rows, rows], axis=0).T
    upper = jnp.where(c < r, turned[: BS // 2], rows)
    quarter = jnp.where(c < r, rows, turned[: BS // 2])
    quarter = jnp.where(c == r, line(payload, first + BS // 2), quarter)
    lower = jnp.where(c < BS // 2, turned[BS // 2 :], swap_halves(quarter))
    return jnp.concatenate([upper, lower], axis=0)


def coefficient(term):
    return time_step / (term + 1)


SUMS = ((1, 2, 1), (1, 1, 2), (1, 3, 4), (1, 4, 3), (2, 2, 2), (2, 3, 3), (3, 2, 2), (3, 3, 3), (3, 2, 3), (3, 3, 2))
OWN = (((0, -1), (2, 1)), ((0, 0), (2, 2)), ((0, 1), (2, 3)), ((1, -1), (3, 2)), ((1, 0), (3, 3)), ((1, 1), (3, 4)))
EARLY = ((1, 2, 2), (1, 3, 3), (1, 2, 3), (1, 3, 2))
LATE = ((1, 2, 1), (1, 1, 2), (2, 2, 1), (2, 1, 2), (3, 2, 1), (3, 1, 2), (2, 2, 2), (3, 2, 2), (3, 2, 3), (3, 3, 2))
DONE_EARLY = {(2, 2): (1,), (2, 3): (1, 2), (3, 2): (1, 2), (3, 3): (1,)}
DONE_NEAR = {(3, 3): (2, 3), (3, 4): (1, 2, 3)}
DONE_FAR = {(2, 1): (1, 2, 3), (2, 2): (2, 3), (2, 3): (3,), (3, 2): (3,)}


def weighted(terms_of, signs):
    total = None
    for sign, value in zip(signs, terms_of):
        total = (value if sign > 0 else -value) if total is None else (total + value if sign > 0 else total - value)
    return total


def parts_of(values, i, j, terms):
    re_signs, im_signs = [SIGN_RE[term] for term in terms], [SIGN_IM[term] for term in terms]
    here = [values[(term, i, j)] for term in terms]
    there = here if i == j else [values[(term, j, i)] for term in terms]
    real = 0.5 * (weighted(here, re_signs) + weighted(there, re_signs).T)
    imag = 0.5 * (weighted(here, im_signs) - weighted(there, im_signs).T)
    return real, imag


def add_terms(base, values, done, phase):
    for index, (_, (i, j)) in enumerate(OWN):
        terms = [level - 1 + 3 * phase for level in done.get((i, j), ())]
        if terms:
            real, imag = parts_of(values, i, j, terms)
            base[index, 0] = base[index, 0] + real
            base[index, 1] = base[index, 1] + imag


def views(h_ref, x_ref):
    return Band(h_ref, True), [Band(x_ref.at[level]) for level in range(3)]


def before_far(h, xs, phase, table, sums, early, far, carry):
    x0, x1, _ = xs
    term = 3 * phase
    t = tile(h, x0, 2)
    scale = line(table, 6 + term)
    inner = {
        (2, 2): (t[0] + part(h, x0, 2, 1, 2)) * coefficient(term),
        (2, 3): t[1] * scale,
        (3, 2): t[2] * scale,
    }
    for (i, j), value in inner.items():
        x1.put(i, j, value)
        early[EARLY.index((1, i, j))] = value
    carry[...] = t[3]
    far[BS : 2 * BS, :] = inner[(2, 2)]
    value = part(h, x1, 2, 3, 2)
    far[2 * BS : 3 * BS, :] = value
    sums[SUMS.index((2, 2, 2))] = value


def before_near(carry, h_ref, near_in, x_in, sums_in, early_in, near, x_ref, sums, early, *, phase):
    h, (x0, x1, _) = views(h_ref, x_ref)
    value = (carry[...] + part(h, x0, 3, 4, 3)) * coefficient(3 * phase)
    x1.put(3, 3, value)
    early[EARLY.index((1, 3, 3))] = value
    near[BS : 2 * BS, :] = value
    value = part(h, x1, 3, 2, 3)
    near[2 * BS : 3 * BS, :] = value
    sums[SUMS.index((2, 3, 3))] = value


def own_first(
    re, im, ham, dip, pattern_in, field,
    far, near, table, h_ref, x_ref, sums, early, carry, re_in, im_in,
    ham_in, dip_in, pattern, sems,
):
    copies = [
        pltpu.make_async_copy(source, target, sems.at[n])
        for n, (source, target) in enumerate(
            ((pattern_in, pattern), (ham, ham_in), (dip, dip_in), (re, re_in), (im, im_in))
        )
    ]
    for copy in copies:
        copy.start()
    copies[0].wait()
    for n, (row, offset) in enumerate(((0, -1), (0, 1), (1, 1))):
        r, e = own_index(row, offset)
        for term in range(TERMS):
            table[6 * n + term : 6 * n + term + 1, :] = jnp.full(
                (1, BS), pattern[e, r, term].astype(f32) * coefficient(term), f32
            )
    h, xs = views(h_ref, x_ref)
    for copy in copies[1:3]:
        copy.wait()
    for (row, offset), (i, j) in OWN:
        value = own(ham_in, row, offset) + field[0] * own(dip_in, row, offset)
        h.put(i, j, value)
        if j in (1, 4):
            h.put(j, i, value.T)
        if i == j:
            put_symmetric(far if i == 2 else near, value)
    for copy in copies[3:]:
        copy.wait()
    for (row, offset), (i, j) in OWN:
        real, imag = own(re_in, row, offset), own(im_in, row, offset)
        xs[0].put(i, j, real + imag)
        if j in (1, 4):
            xs[0].put(j, i, (real - imag).T)
        if i == j:
            (far if i == 2 else near)[0:BS, :] = real + imag
    before_far(h, xs, 0, table, sums, early, far, carry)


def own_rest(h, xs, phase, table, early, base, sums):
    x0, x1, x2 = xs
    term = 3 * phase
    values = {(term, i, j): early[index] for index, (_, i, j) in enumerate(EARLY)}
    t = tile(h, x1, 2)
    scale = line(table, 6 + term + 1)
    for (i, j), value in (((2, 3), t[1] * scale), ((3, 2), t[2] * scale)):
        x2.put(i, j, value)
        values[(term + 1, i, j)] = value
    for a, b in ((3, 4), (2, 1)):
        sums[SUMS.index((1, a, b))] = part(h, x0, a, a, b)
        sums[SUMS.index((1, b, a))] = part(h, x0, b, a, a)
    sums[SUMS.index((3, 2, 2))] = part(h, x2, 2, 3, 2)
    sums[SUMS.index((3, 3, 3))] = part(h, x2, 3, 2, 3)
    add_terms(base, values, DONE_EARLY, phase)


def side(h, xs, a, b, payload, phase, scales, sums, record):
    x0, x1, x2 = xs
    c = [coefficient(3 * phase + n) for n in range(3)]
    low = min(a, b)
    at_a, at_b = (0, 3) if a == low else (3, 0)
    up, down = (low, low + 1), (low + 1, low)

    def known(level, i, j):
        return sums[SUMS.index((level, i, j))]

    def put(level, i, j, value):
        record(level, i, j, value)
        if level < 3:
            xs[level].put(i, j, value)

    x0.put(b, b, slot(payload, 0))
    x1.put(b, b, slot(payload, 1))
    put(1, a, b, (part(h, x0, a, b, b) + known(1, a, b)) * scales[0])
    put(1, b, a, (part(h, x0, b, b, a) + known(1, b, a)) * scales[0])
    t = tile(h, x1, low)
    put(2, a, a, (t[at_a] + known(2, a, a)) * c[1])
    put(2, b, b, (t[at_b] + slot(payload, 2)) * c[1])
    put(2, *up, t[1] * scales[1])
    put(2, *down, t[2] * scales[1])

    def last():
        row = piece(h, x2, (a,), (low, low + 1), (low, low + 1))[0]
        here, there = (row[:, :BS], row[:, BS:]) if a == low else (row[:, BS:], row[:, :BS])
        put(3, a, b, there * scales[2])
        put(3, a, a, (here + known(3, a, a)) * c[2])
        put(3, b, a, piece(h, x2, (b,), (low, low + 1), (a, a))[0] * scales[2])

    return last


def near_side(h, xs, near, phase, table, base, sums):
    term = 3 * phase
    values = {}

    def record(level, i, j, value):
        values[(term + level - 1, i, j)] = value

    scales = [line(table, 12 + term + n) for n in range(3)]
    side(h, xs, 3, 4, near, phase, scales, sums, record)()
    x2 = xs[2]
    sums[SUMS.index((3, 2, 3))] = one_side(h, x2, 2, (2, 3), 3) + one_side(x2, h.minus, 2, (3, 3), 3)
    sums[SUMS.index((3, 3, 2))] = one_side(h, x2, 3, (3, 3), 2) + one_side(x2, h.minus, 3, (2, 3), 2)
    add_terms(base, values, DONE_NEAR, phase)
    return values


def far_side(h, xs, far, phase, table, sums, record, between=lambda: None):
    term = 3 * phase
    scales = [line(table, term + n) for n in range(3)]
    last = side(h, xs, 2, 1, far, phase, scales, sums, record)
    x2 = xs[2]
    scale = line(table, 6 + term + 2)
    record(3, 2, 3, (one_side(x2, h.minus, 2, (2, 2), 3) + sums[SUMS.index((3, 2, 3))]) * scale)
    record(3, 3, 2, (one_side(h, x2, 3, (2, 2), 2) + sums[SUMS.index((3, 3, 2))]) * scale)
    between()
    last()


def rest_first(re_in, im_in, table, early, h_ref, x_in, sums_in, x_ref, sums, base):
    h, xs = views(h_ref, x_ref)
    for index, ((row, offset), _) in enumerate(OWN):
        base[index, 0], base[index, 1] = own(re_in, row, offset), own(im_in, row, offset)
    own_rest(h, xs, 0, table, early, base, sums)


def near_first(near, table, h_in, x_in, sums_in, base_in, h_ref, x_ref, sums, base, inner_state):
    h, xs = views(h_ref, x_ref)
    h.put(4, 4, get_symmetric(near))
    values = near_side(h, xs, near, 0, table, base, sums)
    for i, j in ((3, 3), (3, 4), (4, 3)):
        xs[0].put(i, j, values[(2, i, j)])
    inner_state[...] = values[(2, 3, 3)]


def far_first(
    far, table, inner_state, h_in, x_in, sums_in, h_ref, x_ref, sums, late, early, far_next, near_next, carry
):
    h, xs = views(h_ref, x_ref)
    h.put(1, 1, get_symmetric(far))
    state = {}

    def record(level, i, j, value):
        if (level, i, j) in LATE:
            late[LATE.index((level, i, j))] = value
        if level == 3:
            state[(i, j)] = value

    far_side(h, xs, far, 0, table, sums, record)
    for (i, j), value in state.items():
        xs[0].put(i, j, value)
    far_next[0:BS, :] = state[(2, 2)]
    near_next[0:BS, :] = inner_state[...]
    before_far(h, xs, 1, table, sums, early, far_next, carry)


def rest_second(late, early, table, h_ref, x_in, sums_in, base_in, x_ref, sums, base):
    h, xs = views(h_ref, x_ref)
    values = {(level - 1, i, j): late[index] for index, (level, i, j) in enumerate(LATE)}
    add_terms(base, values, DONE_FAR, 0)
    own_rest(h, xs, 1, table, early, base, sums)


def near_second(near, table, h_ref, x_in, sums_in, base_in, x_ref, sums, base):
    h, xs = views(h_ref, x_ref)
    near_side(h, xs, near, 1, table, base, sums)


def far_second(far, table, sums, base, h_ref, x_in, x_ref, out_re, out_im, stage, sems):
    h, xs = views(h_ref, x_ref)
    copies = []
    for index, ((row, offset), _) in enumerate(OWN):
        r, e = own_index(row, offset)
        source = stage if index < 4 else base
        for a, out in enumerate((out_re, out_im)):
            copies.append(pltpu.make_async_copy(source.at[index, a], out.at[r, e], sems.at[len(copies)]))

    def send(first):
        for copy in copies[2 * first : 2 * first + 4]:
            copy.start()

    def apart(first):
        pl.when(lax.axis_index("col") >= 0)(lambda: send(first))

    apart(4)
    values = {}

    def record(level, i, j, value):
        values[(level + 2, i, j)] = value

    def finish(index):
        i, j = OWN[index][1]
        real, imag = parts_of(values, i, j, [level + 2 for level in DONE_FAR[(i, j)]])
        stage[index, 0], stage[index, 1] = base[index, 0] + real, base[index, 1] + imag

    def between():
        finish(2)
        finish(3)
        apart(2)

    far_side(h, xs, far, 1, table, sums, record, between)
    finish(0)
    finish(1)
    send(0)
    for copy in copies:
        copy.wait()


VECTOR = pl.BlockSpec(memory_space=pltpu.VMEM)
SCALAR = pl.BlockSpec(memory_space=pltpu.SMEM)
BIG = pl.BlockSpec(memory_space=pltpu.HBM)


def call(kernel, ins, outs, scratch=(), aliases=None):
    return pl.pallas_call(
        kernel,
        out_shape=[shape for shape, _ in outs],
        in_specs=ins,
        out_specs=[spec for _, spec in outs],
        scratch_shapes=list(scratch),
        input_output_aliases=aliases or {},
        compiler_params=pltpu.CompilerParams(vmem_limit_bytes=24 * 2**20),
        cost_estimate=pl.CostEstimate(flops=0, bytes_accessed=0, transcendentals=0),
    )


def vector(*shape, dtype=f32):
    return jax.ShapeDtypeStruct(shape, dtype), VECTOR


def body(density_real, density_imag, hamiltonian, dipole, field, pattern):
    count = lax.axis_size(RING)
    pair = [(i, i ^ 1) for i in range(count)]
    cross = [(i, (i + 1) % count if i % 2 else (i - 1) % count) for i in range(count)]
    pattern = jnp.transpose(pattern, (2, 1, 0))
    whole = density_real.shape
    inputs = [
        pltpu.with_memory_space_constraint(x, pltpu.HBM)
        for x in (density_real, density_imag, hamiltonian, dipole, pattern)
    ]
    dma = pltpu.SemaphoreType.DMA
    h_out, x_out = vector(4, ROWS, BS, 3 * BS, dtype=bf16), vector(3, 2, ROWS, BS, 3 * BS, dtype=bf16)
    base_out, sums_out = vector(len(OWN), 2, BS, BS), vector(len(SUMS), BS, BS)
    carry_out, early_out, late_out = vector(BS, BS), vector(len(EARLY), BS, BS), vector(len(LATE), BS, BS)
    out = (jax.ShapeDtypeStruct(whole, f32), BIG)

    far, near, table, h, x, sums, early, carry, re_in, im_in = call(
        own_first,
        [BIG] * 5 + [SCALAR],
        [
            vector(FIRST_ROWS + MORE, BS),
            vector(FIRST_ROWS, BS),
            vector(TABLE_ROWS, BS),
            h_out,
            x_out,
            sums_out,
            early_out,
            carry_out,
            vector(*whole),
            vector(*whole),
        ],
        [pltpu.VMEM(whole, f32)] * 2 + [pltpu.SMEM(pattern.shape, jnp.int32), dma((5,))],
    )(*inputs, field)
    far = lax.ppermute(far, RING, cross)
    near, x, sums, early = call(
        functools.partial(before_near, phase=0),
        [VECTOR] * 6,
        [vector(FIRST_ROWS, BS), x_out, sums_out, early_out],
        aliases={2: 0, 3: 1, 4: 2, 5: 3},
    )(carry, h, near, x, sums, early)
    near = lax.ppermute(near, RING, pair)
    x, sums, base = call(
        rest_first,
        [VECTOR] * 7,
        [x_out, sums_out, base_out],
        aliases={5: 0, 6: 1},
    )(re_in, im_in, table, early, h, x, sums)
    h, x, sums, base, inner_state = call(
        near_first,
        [VECTOR] * 6,
        [h_out, x_out, sums_out, base_out, vector(BS, BS)],
        aliases={2: 0, 3: 1, 4: 2, 5: 3},
    )(near, table, h, x, sums, base)
    h, x, sums, late, early, far, near, carry = call(
        far_first,
        [VECTOR] * 6,
        [
            h_out,
            x_out,
            sums_out,
            late_out,
            early_out,
            vector(SECOND_ROWS + MORE, BS),
            vector(SECOND_ROWS, BS),
            carry_out,
        ],
        aliases={3: 0, 4: 1, 5: 2},
    )(far, table, inner_state, h, x, sums)
    far = lax.ppermute(far, RING, cross)
    near, x, sums, early = call(
        functools.partial(before_near, phase=1),
        [VECTOR] * 6,
        [vector(SECOND_ROWS, BS), x_out, sums_out, early_out],
        aliases={2: 0, 3: 1, 4: 2, 5: 3},
    )(carry, h, near, x, sums, early)
    near = lax.ppermute(near, RING, pair)
    x, sums, base = call(
        rest_second,
        [VECTOR] * 7,
        [x_out, sums_out, base_out],
        aliases={4: 0, 5: 1, 6: 2},
    )(late, early, table, h, x, sums, base)
    x, sums, base = call(
        near_second,
        [VECTOR] * 6,
        [x_out, sums_out, base_out],
        aliases={3: 0, 4: 1, 5: 2},
    )(near, table, h, x, sums, base)
    _, out_re, out_im = call(
        far_second,
        [VECTOR] * 6,
        [x_out, out, out],
        [pltpu.VMEM((4, 2, BS, BS), f32), dma((12,))],
        aliases={5: 0},
    )(far, table, sums, base, h, x)
    return out_re, out_im


def solution(mesh):
    in_specs = (
        P(("row", "col"), None, None, None),
        P(("row", "col"), None, None, None),
        P(("row", "col"), None, None, None),
        P(("parts", "row", "col"), None, None, None),
        P("parts"),
        P(None, ("row", "col"), None),
    )
    out_specs = (
        P(("parts", "row", "col"), None, None, None),
        P(("parts", "row", "col"), None, None, None),
    )
    return jax.shard_map(body, mesh=mesh, in_specs=in_specs, out_specs=out_specs, check_vma=False)
```

```python
import functools

import jax
import jax.numpy as jnp
from jax import lax
from jax.experimental import pallas as pl
from jax.experimental.pallas import tpu as pltpu
from jax.sharding import PartitionSpec as P

TERMS = 6
BS = 128
time_step = 0.5
RING = ("row", "col")
f32, bf16 = jnp.float32, jnp.bfloat16

ROWS = 6
SIGN_RE = (1.0, -1.0, -1.0, 1.0, 1.0, -1.0)
SIGN_IM = (-1.0, -1.0, 1.0, 1.0, -1.0, -1.0)
FIRST_ROWS = 3 * BS + BS // 2 + 8
SECOND_ROWS = 2 * BS
MORE = 8
PART_ROWS = SECOND_ROWS + 2 * MORE
FAR_PART_ROWS = SECOND_ROWS + 2 * MORE
TABLE_ROWS = 24


def own_index(row, offset):
    core = lax.axis_index("col")
    return jnp.where(core == 0, row, 1 - row), jnp.where(core == 0, 1 + offset, 1 - offset)


def own(ref, row, offset):
    r, e = own_index(row, offset)
    return ref[r, e]


def slot(ref, index):
    return ref[index * BS : (index + 1) * BS, :]


def line(ref, index):
    return ref[index : index + 1, :]


class Band:
    def __init__(self, ref, negated=False):
        self.high, self.low = ref.at[0], ref.at[1]
        self.minus = Band(ref.at[pl.ds(2, 2)]) if negated else None

    def put(self, i, j, value):
        part = slice((j - i + 1) * BS, (j - i + 2) * BS)
        high = value.astype(bf16)
        low = (value - high.astype(f32)).astype(bf16)
        self.high[i, :, part] = high
        self.low[i, :, part] = low
        if self.minus is not None:
            self.minus.high[i, :, part] = -high
            self.minus.low[i, :, part] = -low

    def left(self, i, first, last):
        part = slice((first - i + 1) * BS, (last - i + 2) * BS)
        high, low = self.high[i, :, part], self.low[i, :, part]
        return [high, high, low]

    def right(self, first, last, j, j_last):
        highs, lows = [], []
        for k in range(first, last + 1):
            part = slice((j - k + 1) * BS, (j_last - k + 2) * BS)
            highs.append(self.high[k, :, part])
            lows.append(self.low[k, :, part])
        return highs + lows + highs


def piece(h, x, rows, mids, cols):
    after_h = jnp.concatenate(x.right(*mids, *cols), axis=0)
    after_x = jnp.concatenate(h.minus.right(*mids, *cols), axis=0)

    def product(left, right):
        return jnp.dot(jnp.concatenate(left, axis=1), right, preferred_element_type=f32)

    return [product(h.left(i, *mids), after_h) + product(x.left(i, *mids), after_x) for i in rows]


def one_side(a, b, row, mids, col):
    left = jnp.concatenate(a.left(row, *mids), axis=1)
    right = jnp.concatenate(b.right(*mids, col, col), axis=0)
    return jnp.dot(left, right, preferred_element_type=f32)


def tile(h, x, i):
    upper, lower = piece(h, x, (i, i + 1), (i, i + 1), (i, i + 1))
    return upper[:, :BS], upper[:, BS:], lower[:, :BS], lower[:, BS:]


def part(h, x, i, k, j):
    return piece(h, x, (i,), (k, k), (j, j))[0]


def half_places():
    shape = (BS // 2, BS)
    return lax.broadcasted_iota(jnp.int32, shape, 0), lax.broadcasted_iota(jnp.int32, shape, 1)


def swap_halves(rows):
    return jnp.concatenate([rows[:, BS // 2 :], rows[:, : BS // 2]], axis=1)


def put_symmetric(payload, block):
    r, c = half_places()
    turned = swap_halves(block[BS // 2 :])
    first = 3 * BS
    payload[first : first + BS // 2, :] = jnp.where(c < r, turned, block[: BS // 2])
    payload[first + BS // 2 : first + BS // 2 + 1, :] = jnp.sum(jnp.where(c == r, turned, 0.0), axis=0, keepdims=True)


def get_symmetric(payload):
    r, c = half_places()
    first = 3 * BS
    rows = payload[first : first + BS // 2, :]
    turned = jnp.concatenate([rows, rows], axis=0).T
    upper = jnp.where(c < r, turned[: BS // 2], rows)
    quarter = jnp.where(c < r, rows, turned[: BS // 2])
    quarter = jnp.where(c == r, line(payload, first + BS // 2), quarter)
    lower = jnp.where(c < BS // 2, turned[BS // 2 :], swap_halves(quarter))
    return jnp.concatenate([upper, lower], axis=0)


def coefficient(term):
    return time_step / (term + 1)


SUMS = ((1, 2, 1), (1, 1, 2), (1, 3, 4), (1, 4, 3), (2, 2, 2), (2, 3, 3), (3, 2, 2), (3, 3, 3), (3, 2, 3), (3, 3, 2))
OWN = (((0, -1), (2, 1)), ((0, 0), (2, 2)), ((0, 1), (2, 3)), ((1, -1), (3, 2)), ((1, 0), (3, 3)), ((1, 1), (3, 4)))
EARLY = ((1, 2, 2), (1, 3, 3), (1, 2, 3), (1, 3, 2))
LATE = ((1, 2, 1), (1, 1, 2), (2, 2, 1), (2, 1, 2), (3, 2, 1), (3, 1, 2), (2, 2, 2), (3, 2, 2), (3, 2, 3), (3, 3, 2))
DONE_EARLY = {(2, 2): (1,), (2, 3): (1, 2), (3, 2): (1, 2), (3, 3): (1,)}
DONE_NEAR = {(3, 3): (2, 3), (3, 4): (1, 2, 3)}
DONE_FAR = {(2, 1): (1, 2, 3), (2, 2): (2, 3), (2, 3): (3,), (3, 2): (3,)}


def weighted(terms_of, signs):
    total = None
    for sign, value in zip(signs, terms_of):
        total = (value if sign > 0 else -value) if total is None else (total + value if sign > 0 else total - value)
    return total


def parts_of(values, i, j, terms):
    re_signs, im_signs = [SIGN_RE[term] for term in terms], [SIGN_IM[term] for term in terms]
    here = [values[(term, i, j)] for term in terms]
    there = here if i == j else [values[(term, j, i)] for term in terms]
    real = 0.5 * (weighted(here, re_signs) + weighted(there, re_signs).T)
    imag = 0.5 * (weighted(here, im_signs) - weighted(there, im_signs).T)
    return real, imag


def add_terms(base, values, done, phase):
    for index, (_, (i, j)) in enumerate(OWN):
        terms = [level - 1 + 3 * phase for level in done.get((i, j), ())]
        if terms:
            real, imag = parts_of(values, i, j, terms)
            base[index, 0] = base[index, 0] + real
            base[index, 1] = base[index, 1] + imag


def views(h_ref, x_ref):
    return Band(h_ref, True), [Band(x_ref.at[level]) for level in range(3)]


def before_far(h, xs, phase, table, sums, early, far, carry):
    x0, x1, _ = xs
    term = 3 * phase
    t = tile(h, x0, 2)
    scale = line(table, 6 + term)
    inner = {
        (2, 2): (t[0] + part(h, x0, 2, 1, 2)) * coefficient(term),
        (2, 3): t[1] * scale,
        (3, 2): t[2] * scale,
    }
    for (i, j), value in inner.items():
        x1.put(i, j, value)
        early[EARLY.index((1, i, j))] = value
    carry[...] = t[3]
    first = 1 - phase
    far[first * BS : (first + 1) * BS, :] = inner[(2, 2)]
    value = part(h, x1, 2, 3, 2)
    far[(first + 1) * BS : (first + 2) * BS, :] = value
    sums[SUMS.index((2, 2, 2))] = value


def before_near_first(carry, h_ref, near_in, x_in, sums_in, early_in, near, x_ref, sums, early):
    before_near(carry, h_ref, x_ref, sums, early, near, 0)


def before_near_second(carry, h_ref, x_in, sums_in, early_in, near, x_ref, sums, early):
    before_near(carry, h_ref, x_ref, sums, early, near, 1)


def before_near(carry, h_ref, x_ref, sums, early, near, phase):
    h, (x0, x1, _) = views(h_ref, x_ref)
    first = 1 - phase
    value = (carry[...] + part(h, x0, 3, 4, 3)) * coefficient(3 * phase)
    x1.put(3, 3, value)
    early[EARLY.index((1, 3, 3))] = value
    near[first * BS : (first + 1) * BS, :] = value
    value = part(h, x1, 3, 2, 3)
    near[(first + 1) * BS : (first + 2) * BS, :] = value
    sums[SUMS.index((2, 3, 3))] = value


def own_first(
    re, im, ham, dip, pattern_in, field,
    far, near, table, h_ref, x_ref, sums, early, carry, re_in, im_in,
    ham_in, dip_in, pattern, sems,
):
    copies = [
        pltpu.make_async_copy(source, target, sems.at[n])
        for n, (source, target) in enumerate(
            ((pattern_in, pattern), (ham, ham_in), (dip, dip_in), (re, re_in), (im, im_in))
        )
    ]
    for copy in copies:
        copy.start()
    copies[0].wait()
    for n, (row, offset) in enumerate(((0, -1), (0, 1), (1, 1))):
        r, e = own_index(row, offset)
        for term in range(TERMS):
            table[6 * n + term : 6 * n + term + 1, :] = jnp.full(
                (1, BS), pattern[e, r, term].astype(f32) * coefficient(term), f32
            )
    h, xs = views(h_ref, x_ref)
    for copy in copies[1:3]:
        copy.wait()
    for (row, offset), (i, j) in OWN:
        value = own(ham_in, row, offset) + field[0] * own(dip_in, row, offset)
        h.put(i, j, value)
        if j in (1, 4):
            h.put(j, i, value.T)
        if i == j:
            put_symmetric(far if i == 2 else near, value)
    for copy in copies[3:]:
        copy.wait()
    for (row, offset), (i, j) in OWN:
        real, imag = own(re_in, row, offset), own(im_in, row, offset)
        xs[0].put(i, j, real + imag)
        if j in (1, 4):
            xs[0].put(j, i, (real - imag).T)
        if i == j:
            (far if i == 2 else near)[0:BS, :] = real + imag
    before_far(h, xs, 0, table, sums, early, far, carry)


def own_rest(h, xs, phase, table, early, base, sums):
    x0, x1, x2 = xs
    term = 3 * phase
    values = {(term, i, j): early[index] for index, (_, i, j) in enumerate(EARLY)}
    t = tile(h, x1, 2)
    scale = line(table, 6 + term + 1)
    for (i, j), value in (((2, 3), t[1] * scale), ((3, 2), t[2] * scale)):
        x2.put(i, j, value)
        values[(term + 1, i, j)] = value
    for a, b in ((3, 4), (2, 1)):
        sums[SUMS.index((1, a, b))] = part(h, x0, a, a, b)
        sums[SUMS.index((1, b, a))] = part(h, x0, b, a, a)
    sums[SUMS.index((3, 2, 2))] = part(h, x2, 2, 3, 2)
    sums[SUMS.index((3, 3, 3))] = part(h, x2, 3, 2, 3)
    add_terms(base, values, DONE_EARLY, phase)


def side(h, xs, a, b, start, payload, phase, scales, sums, record):
    x0, x1, x2 = xs
    c = [coefficient(3 * phase + n) for n in range(3)]
    low = min(a, b)
    at_a, at_b = (0, 3) if a == low else (3, 0)
    up, down = (low, low + 1), (low + 1, low)

    def known(level, i, j):
        return sums[SUMS.index((level, i, j))]

    def put(level, i, j, value):
        record(level, i, j, value)
        if level < 3:
            xs[level].put(i, j, value)

    first = 1 - phase
    x0.put(b, b, start)
    x1.put(b, b, slot(payload, first))
    put(1, a, b, (part(h, x0, a, b, b) + known(1, a, b)) * scales[0])
    put(1, b, a, (part(h, x0, b, b, a) + known(1, b, a)) * scales[0])
    t = tile(h, x1, low)
    put(2, a, a, (t[at_a] + known(2, a, a)) * c[1])
    put(2, b, b, (t[at_b] + slot(payload, first + 1)) * c[1])
    put(2, *up, t[1] * scales[1])
    put(2, *down, t[2] * scales[1])

    def last():
        row = piece(h, x2, (a,), (low, low + 1), (low, low + 1))[0]
        here, there = (row[:, :BS], row[:, BS:]) if a == low else (row[:, BS:], row[:, :BS])
        put(3, a, b, there * scales[2])
        put(3, a, a, (here + known(3, a, a)) * c[2])
        if phase:
            put(3, b, a, piece(h, x2, (b,), (low, low + 1), (a, a))[0] * scales[2])
            return None
        row = piece(h, x2, (b,), (low, low + 1), (low, low + 1))[0]
        here, there = (row[:, :BS], row[:, BS:]) if b == low else (row[:, BS:], row[:, :BS])
        put(3, b, a, there * scales[2])
        return here

    return last


def near_side(h, xs, start, near, phase, table, base, sums):
    term = 3 * phase
    values = {}

    def record(level, i, j, value):
        values[(term + level - 1, i, j)] = value

    scales = [line(table, 12 + term + n) for n in range(3)]
    own_part = side(h, xs, 3, 4, start, near, phase, scales, sums, record)()
    x2 = xs[2]
    sums[SUMS.index((3, 2, 3))] = one_side(h, x2, 2, (2, 3), 3) + one_side(x2, h.minus, 2, (3, 3), 3)
    sums[SUMS.index((3, 3, 2))] = one_side(h, x2, 3, (3, 3), 2) + one_side(x2, h.minus, 3, (2, 3), 2)
    add_terms(base, values, DONE_NEAR, phase)
    return values, own_part


def far_side(h, xs, start, far, phase, table, sums, record, between=lambda: None):
    term = 3 * phase
    scales = [line(table, term + n) for n in range(3)]
    last = side(h, xs, 2, 1, start, far, phase, scales, sums, record)
    x2 = xs[2]
    scale = line(table, 6 + term + 2)
    record(3, 2, 3, (one_side(x2, h.minus, 2, (2, 2), 3) + sums[SUMS.index((3, 2, 3))]) * scale)
    record(3, 3, 2, (one_side(h, x2, 3, (2, 2), 2) + sums[SUMS.index((3, 3, 2))]) * scale)
    between()
    return last()


def rest_first(re_in, im_in, table, early, h_ref, x_in, sums_in, x_ref, sums, base):
    h, xs = views(h_ref, x_ref)
    for index, ((row, offset), _) in enumerate(OWN):
        base[index, 0], base[index, 1] = own(re_in, row, offset), own(im_in, row, offset)
    own_rest(h, xs, 0, table, early, base, sums)


def near_first(
    near, table, h_in, x_in, sums_in, base_in, h_ref, x_ref, sums, base, own_part, part_far, part_near
):
    h, xs = views(h_ref, x_ref)
    h.put(4, 4, get_symmetric(near))
    values, own_part[...] = near_side(h, xs, slot(near, 0), near, 0, table, base, sums)
    for i, j in ((3, 3), (3, 4), (4, 3)):
        xs[0].put(i, j, values[(2, i, j)])
    part_far[0:BS, :] = sums[SUMS.index((3, 2, 2))]
    part_far[BS:, :] = jnp.zeros((FAR_PART_ROWS - BS, BS), f32)
    part_near[0:BS, :] = sums[SUMS.index((3, 3, 3))]
    part_near[BS:, :] = jnp.zeros((PART_ROWS - BS, BS), f32)


def far_first(far, table, h_in, x_in, sums_in, h_ref, x_ref, sums, late, early, far_next, own_part, carry):
    h, xs = views(h_ref, x_ref)
    h.put(1, 1, get_symmetric(far))
    state = {}

    def record(level, i, j, value):
        if (level, i, j) in LATE:
            late[LATE.index((level, i, j))] = value
        if level == 3:
            state[(i, j)] = value

    own_part[...] = far_side(h, xs, slot(far, 0), far, 0, table, sums, record)
    for (i, j), value in state.items():
        xs[0].put(i, j, value)
    before_far(h, xs, 1, table, sums, early, far_next, carry)


def rest_second(late, early, table, h_ref, x_in, sums_in, base_in, x_ref, sums, base):
    h, xs = views(h_ref, x_ref)
    values = {(level - 1, i, j): late[index] for index, (level, i, j) in enumerate(LATE)}
    add_terms(base, values, DONE_FAR, 0)
    own_rest(h, xs, 1, table, early, base, sums)


def near_second(near, own_part, part_near, table, h_ref, x_in, sums_in, base_in, x_ref, sums, base):
    h, xs = views(h_ref, x_ref)
    start = (own_part[...] + part_near[0:BS, :]) * coefficient(2)
    near_side(h, xs, start, near, 1, table, base, sums)


def far_second(far, own_part, part_far, table, sums, base, h_ref, x_in, x_ref, out_re, out_im, stage, sems):
    h, xs = views(h_ref, x_ref)
    copies = []
    for index, ((row, offset), _) in enumerate(OWN):
        r, e = own_index(row, offset)
        source = stage if index < 4 else base
        for a, out in enumerate((out_re, out_im)):
            copies.append(pltpu.make_async_copy(source.at[index, a], out.at[r, e], sems.at[len(copies)]))

    def send(first):
        for copy in copies[2 * first : 2 * first + 4]:
            copy.start()

    def apart(first):
        pl.when(lax.axis_index("col") >= 0)(lambda: send(first))

    apart(4)
    values = {}

    def record(level, i, j, value):
        values[(level + 2, i, j)] = value

    def finish(index):
        i, j = OWN[index][1]
        real, imag = parts_of(values, i, j, [level + 2 for level in DONE_FAR[(i, j)]])
        stage[index, 0], stage[index, 1] = base[index, 0] + real, base[index, 1] + imag

    def between():
        finish(2)
        finish(3)
        apart(2)

    start = (own_part[...] + part_far[0:BS, :]) * coefficient(2)
    far_side(h, xs, start, far, 1, table, sums, record, between)
    finish(0)
    finish(1)
    send(0)
    for copy in copies:
        copy.wait()


VECTOR = pl.BlockSpec(memory_space=pltpu.VMEM)
SCALAR = pl.BlockSpec(memory_space=pltpu.SMEM)
BIG = pl.BlockSpec(memory_space=pltpu.HBM)


def call(kernel, ins, outs, scratch=(), aliases=None):
    return pl.pallas_call(
        kernel,
        out_shape=[shape for shape, _ in outs],
        in_specs=ins,
        out_specs=[spec for _, spec in outs],
        scratch_shapes=list(scratch),
        input_output_aliases=aliases or {},
        compiler_params=pltpu.CompilerParams(vmem_limit_bytes=24 * 2**20),
        cost_estimate=pl.CostEstimate(flops=0, bytes_accessed=0, transcendentals=0),
    )


def vector(*shape, dtype=f32):
    return jax.ShapeDtypeStruct(shape, dtype), VECTOR


def body(density_real, density_imag, hamiltonian, dipole, field, pattern):
    count = lax.axis_size(RING)
    pair = [(i, i ^ 1) for i in range(count)]
    cross = [(i, (i + 1) % count if i % 2 else (i - 1) % count) for i in range(count)]
    pattern = jnp.transpose(pattern, (2, 1, 0))
    whole = density_real.shape
    inputs = [
        pltpu.with_memory_space_constraint(x, pltpu.HBM)
        for x in (density_real, density_imag, hamiltonian, dipole, pattern)
    ]
    dma = pltpu.SemaphoreType.DMA
    h_out, x_out = vector(4, ROWS, BS, 3 * BS, dtype=bf16), vector(3, 2, ROWS, BS, 3 * BS, dtype=bf16)
    base_out, sums_out = vector(len(OWN), 2, BS, BS), vector(len(SUMS), BS, BS)
    carry_out, early_out, late_out = vector(BS, BS), vector(len(EARLY), BS, BS), vector(len(LATE), BS, BS)
    out = (jax.ShapeDtypeStruct(whole, f32), BIG)

    far, near, table, h, x, sums, early, carry, re_in, im_in = call(
        own_first,
        [BIG] * 5 + [SCALAR],
        [
            vector(FIRST_ROWS + 2 * MORE, BS),
            vector(FIRST_ROWS, BS),
            vector(TABLE_ROWS, BS),
            h_out,
            x_out,
            sums_out,
            early_out,
            carry_out,
            vector(*whole),
            vector(*whole),
        ],
        [pltpu.VMEM(whole, f32)] * 2 + [pltpu.SMEM(pattern.shape, jnp.int32), dma((5,))],
    )(*inputs, field)
    far = lax.ppermute(far, RING, cross)
    near, x, sums, early = call(
        before_near_first,
        [VECTOR] * 6,
        [vector(FIRST_ROWS, BS), x_out, sums_out, early_out],
        aliases={2: 0, 3: 1, 4: 2, 5: 3},
    )(carry, h, near, x, sums, early)
    near = lax.ppermute(near, RING, pair)
    x, sums, base = call(
        rest_first,
        [VECTOR] * 7,
        [x_out, sums_out, base_out],
        aliases={5: 0, 6: 1},
    )(re_in, im_in, table, early, h, x, sums)
    h, x, sums, base, own_near, part_far, part_near = call(
        near_first,
        [VECTOR] * 6,
        [h_out, x_out, sums_out, base_out, carry_out, vector(FAR_PART_ROWS, BS), vector(PART_ROWS, BS)],
        aliases={2: 0, 3: 1, 4: 2, 5: 3},
    )(near, table, h, x, sums, base)
    part_far = lax.ppermute(part_far, RING, cross)
    part_near = lax.ppermute(part_near, RING, pair)
    h, x, sums, late, early, far, own_far, carry = call(
        far_first,
        [VECTOR] * 5,
        [
            h_out,
            x_out,
            sums_out,
            late_out,
            early_out,
            vector(SECOND_ROWS + MORE, BS),
            carry_out,
            carry_out,
        ],
        aliases={2: 0, 3: 1, 4: 2},
    )(far, table, h, x, sums)
    far = lax.ppermute(far, RING, cross)
    near, x, sums, early = call(
        before_near_second,
        [VECTOR] * 5,
        [vector(SECOND_ROWS, BS), x_out, sums_out, early_out],
        aliases={2: 1, 3: 2, 4: 3},
    )(carry, h, x, sums, early)
    near = lax.ppermute(near, RING, pair)
    x, sums, base = call(
        rest_second,
        [VECTOR] * 7,
        [x_out, sums_out, base_out],
        aliases={4: 0, 5: 1, 6: 2},
    )(late, early, table, h, x, sums, base)
    x, sums, base = call(
        near_second,
        [VECTOR] * 8,
        [x_out, sums_out, base_out],
        aliases={5: 0, 6: 1, 7: 2},
    )(near, own_near, part_near, table, h, x, sums, base)
    _, out_re, out_im = call(
        far_second,
        [VECTOR] * 8,
        [x_out, out, out],
        [pltpu.VMEM((4, 2, BS, BS), f32), dma((12,))],
        aliases={7: 0},
    )(far, own_far, part_far, table, sums, base, h, x)
    return out_re, out_im


def solution(mesh):
    in_specs = (
        P(("row", "col"), None, None, None),
        P(("row", "col"), None, None, None),
        P(("row", "col"), None, None, None),
        P(("parts", "row", "col"), None, None, None),
        P("parts"),
        P(None, ("row", "col"), None),
    )
    out_specs = (
        P(("parts", "row", "col"), None, None, None),
        P(("parts", "row", "col"), None, None, None),
    )
    return jax.shard_map(body, mesh=mesh, in_specs=in_specs, out_specs=out_specs, check_vma=False)
```

```python
import functools

import jax
import jax.numpy as jnp
from jax import lax
from jax.experimental import pallas as pl
from jax.experimental.pallas import tpu as pltpu
from jax.sharding import PartitionSpec as P

TERMS = 6
BS = 128
time_step = 0.5
RING = ("row", "col")
f32, bf16 = jnp.float32, jnp.bfloat16

ROWS = 6
SIGN_RE = (1.0, -1.0, -1.0, 1.0, 1.0, -1.0)
SIGN_IM = (-1.0, -1.0, 1.0, 1.0, -1.0, -1.0)
FIRST_ROWS = 3 * BS + BS // 2 + 8
SECOND_ROWS = 2 * BS
MORE = 8
PART_ROWS = SECOND_ROWS + 2 * MORE
FAR_PART_ROWS = SECOND_ROWS + 2 * MORE
TABLE_ROWS = 32
TABLE_FIELD = 24


def own_index(row, offset):
    core = lax.axis_index("col")
    return jnp.where(core == 0, row, 1 - row), jnp.where(core == 0, 1 + offset, 1 - offset)


def own(ref, row, offset):
    r, e = own_index(row, offset)
    return ref[r, e]


def slot(ref, index):
    return ref[index * BS : (index + 1) * BS, :]


def line(ref, index):
    return ref[index : index + 1, :]


class Band:
    def __init__(self, ref, negated=False):
        self.high, self.low = ref.at[0], ref.at[1]
        self.minus = Band(ref.at[pl.ds(2, 2)]) if negated else None

    def put(self, i, j, value):
        part = slice((j - i + 1) * BS, (j - i + 2) * BS)
        high = value.astype(bf16)
        low = (value - high.astype(f32)).astype(bf16)
        self.high[i, :, part] = high
        self.low[i, :, part] = low
        if self.minus is not None:
            self.minus.high[i, :, part] = -high
            self.minus.low[i, :, part] = -low

    def left(self, i, first, last):
        part = slice((first - i + 1) * BS, (last - i + 2) * BS)
        high, low = self.high[i, :, part], self.low[i, :, part]
        return [high, high, low]

    def right(self, first, last, j, j_last):
        highs, lows = [], []
        for k in range(first, last + 1):
            part = slice((j - k + 1) * BS, (j_last - k + 2) * BS)
            highs.append(self.high[k, :, part])
            lows.append(self.low[k, :, part])
        return highs + lows + highs


def piece(h, x, rows, mids, cols):
    after_h = jnp.concatenate(x.right(*mids, *cols), axis=0)
    after_x = jnp.concatenate(h.minus.right(*mids, *cols), axis=0)

    def product(left, right):
        return jnp.dot(jnp.concatenate(left, axis=1), right, preferred_element_type=f32)

    return [product(h.left(i, *mids), after_h) + product(x.left(i, *mids), after_x) for i in rows]


def one_side(a, b, row, mids, col):
    left = jnp.concatenate(a.left(row, *mids), axis=1)
    right = jnp.concatenate(b.right(*mids, col, col), axis=0)
    return jnp.dot(left, right, preferred_element_type=f32)


def tile(h, x, i):
    upper, lower = piece(h, x, (i, i + 1), (i, i + 1), (i, i + 1))
    return upper[:, :BS], upper[:, BS:], lower[:, :BS], lower[:, BS:]


def part(h, x, i, k, j):
    return piece(h, x, (i,), (k, k), (j, j))[0]


def half_places():
    shape = (BS // 2, BS)
    return lax.broadcasted_iota(jnp.int32, shape, 0), lax.broadcasted_iota(jnp.int32, shape, 1)


def swap_halves(rows):
    return jnp.concatenate([rows[:, BS // 2 :], rows[:, : BS // 2]], axis=1)


def put_symmetric(payload, block):
    r, c = half_places()
    turned = swap_halves(block[BS // 2 :])
    first = 3 * BS
    payload[first : first + BS // 2, :] = jnp.where(c < r, turned, block[: BS // 2])
    payload[first + BS // 2 : first + BS // 2 + 1, :] = jnp.sum(jnp.where(c == r, turned, 0.0), axis=0, keepdims=True)


def get_symmetric(payload):
    r, c = half_places()
    first = 3 * BS
    rows = payload[first : first + BS // 2, :]
    turned = jnp.concatenate([rows, rows], axis=0).T
    upper = jnp.where(c < r, turned[: BS // 2], rows)
    quarter = jnp.where(c < r, rows, turned[: BS // 2])
    quarter = jnp.where(c == r, line(payload, first + BS // 2), quarter)
    lower = jnp.where(c < BS // 2, turned[BS // 2 :], swap_halves(quarter))
    return jnp.concatenate([upper, lower], axis=0)


def coefficient(term):
    return time_step / (term + 1)


SUMS = ((1, 2, 1), (1, 1, 2), (1, 3, 4), (1, 4, 3), (2, 2, 2), (2, 3, 3), (3, 2, 2), (3, 3, 3), (3, 2, 3), (3, 3, 2))
OWN = (((0, -1), (2, 1)), ((0, 0), (2, 2)), ((0, 1), (2, 3)), ((1, -1), (3, 2)), ((1, 0), (3, 3)), ((1, 1), (3, 4)))
EARLY = ((1, 2, 2), (1, 3, 3), (1, 2, 3), (1, 3, 2))
LATE = ((1, 2, 1), (1, 1, 2), (2, 2, 1), (2, 1, 2), (3, 2, 1), (3, 1, 2), (2, 2, 2), (3, 2, 2), (3, 2, 3), (3, 3, 2))
DONE_EARLY = {(2, 2): (1,), (2, 3): (1, 2), (3, 2): (1, 2), (3, 3): (1,)}
DONE_NEAR = {(3, 3): (2, 3), (3, 4): (1, 2, 3)}
DONE_FAR = {(2, 1): (1, 2, 3), (2, 2): (2, 3), (2, 3): (3,), (3, 2): (3,)}


def weighted(terms_of, signs):
    total = None
    for sign, value in zip(signs, terms_of):
        total = (value if sign > 0 else -value) if total is None else (total + value if sign > 0 else total - value)
    return total


def parts_of(values, i, j, terms):
    re_signs, im_signs = [SIGN_RE[term] for term in terms], [SIGN_IM[term] for term in terms]
    here = [values[(term, i, j)] for term in terms]
    there = here if i == j else [values[(term, j, i)] for term in terms]
    real = 0.5 * (weighted(here, re_signs) + weighted(there, re_signs).T)
    imag = 0.5 * (weighted(here, im_signs) - weighted(there, im_signs).T)
    return real, imag


def add_terms(base, values, done, phase):
    for index, (_, (i, j)) in enumerate(OWN):
        terms = [level - 1 + 3 * phase for level in done.get((i, j), ())]
        if terms:
            real, imag = parts_of(values, i, j, terms)
            base[index, 0] = base[index, 0] + real
            base[index, 1] = base[index, 1] + imag


def views(h_ref, x_ref):
    return Band(h_ref, True), [Band(x_ref.at[level]) for level in range(3)]


def before_far(h, xs, phase, table, sums, early, far, carry):
    x0, x1, _ = xs
    term = 3 * phase
    t = tile(h, x0, 2)
    scale = line(table, 6 + term)
    inner = {
        (2, 2): (t[0] + part(h, x0, 2, 1, 2)) * coefficient(term),
        (2, 3): t[1] * scale,
        (3, 2): t[2] * scale,
    }
    for (i, j), value in inner.items():
        x1.put(i, j, value)
        early[EARLY.index((1, i, j))] = value
    carry[...] = t[3]
    first = 1 - phase
    far[first * BS : (first + 1) * BS, :] = inner[(2, 2)]
    value = part(h, x1, 2, 3, 2)
    far[(first + 1) * BS : (first + 2) * BS, :] = value
    sums[SUMS.index((2, 2, 2))] = value


def before_near_first(
    carry, table, re_in, im_in, ham_in, dip_in, h_in, x_in, sums_in, early_in, h_ref, near, x_ref, sums, early
):
    h, xs = views(h_ref, x_ref)
    f = line(table, TABLE_FIELD)
    put_symmetric(near, own(ham_in, 1, 0) + f * own(dip_in, 1, 0))
    near[0:BS, :] = own(re_in, 1, 0) + own(im_in, 1, 0)
    value = own(ham_in, 1, 1) + f * own(dip_in, 1, 1)
    h.put(3, 4, value)
    h.put(4, 3, value.T)
    real, imag = own(re_in, 1, 1), own(im_in, 1, 1)
    xs[0].put(3, 4, real + imag)
    xs[0].put(4, 3, (real - imag).T)
    before_near(carry, h_ref, x_ref, sums, early, near, 0)


def before_near_second(carry, h_ref, x_in, sums_in, early_in, near, x_ref, sums, early):
    before_near(carry, h_ref, x_ref, sums, early, near, 1)


def before_near(carry, h_ref, x_ref, sums, early, near, phase):
    h, (x0, x1, _) = views(h_ref, x_ref)
    first = 1 - phase
    value = (carry[...] + part(h, x0, 3, 4, 3)) * coefficient(3 * phase)
    x1.put(3, 3, value)
    early[EARLY.index((1, 3, 3))] = value
    near[first * BS : (first + 1) * BS, :] = value
    value = part(h, x1, 3, 2, 3)
    near[(first + 1) * BS : (first + 2) * BS, :] = value
    sums[SUMS.index((2, 3, 3))] = value


def own_first(
    re, im, ham, dip, pattern_in, field,
    far, table, h_ref, x_ref, sums, early, carry, re_in, im_in, ham_in, dip_in,
    pattern, sems,
):
    copies = [
        pltpu.make_async_copy(source, target, sems.at[n])
        for n, (source, target) in enumerate(
            ((pattern_in, pattern), (ham, ham_in), (dip, dip_in), (re, re_in), (im, im_in))
        )
    ]
    for copy in copies:
        copy.start()
    copies[0].wait()
    for n, (row, offset) in enumerate(((0, -1), (0, 1), (1, 1))):
        r, e = own_index(row, offset)
        for term in range(TERMS):
            table[6 * n + term : 6 * n + term + 1, :] = jnp.full(
                (1, BS), pattern[e, r, term].astype(f32) * coefficient(term), f32
            )
    table[TABLE_FIELD : TABLE_FIELD + 1, :] = jnp.full((1, BS), field[0], f32)
    h, xs = views(h_ref, x_ref)
    for copy in copies[1:3]:
        copy.wait()
    for (row, offset), (i, j) in OWN[:5]:
        value = own(ham_in, row, offset) + field[0] * own(dip_in, row, offset)
        h.put(i, j, value)
        if j == 1:
            h.put(j, i, value.T)
        if (i, j) == (2, 2):
            put_symmetric(far, value)
    for copy in copies[3:]:
        copy.wait()
    for (row, offset), (i, j) in OWN[:5]:
        real, imag = own(re_in, row, offset), own(im_in, row, offset)
        xs[0].put(i, j, real + imag)
        if j == 1:
            xs[0].put(j, i, (real - imag).T)
        if (i, j) == (2, 2):
            far[0:BS, :] = real + imag
    before_far(h, xs, 0, table, sums, early, far, carry)


def own_rest(h, xs, phase, table, early, base, sums):
    x0, x1, x2 = xs
    term = 3 * phase
    values = {(term, i, j): early[index] for index, (_, i, j) in enumerate(EARLY)}
    t = tile(h, x1, 2)
    scale = line(table, 6 + term + 1)
    for (i, j), value in (((2, 3), t[1] * scale), ((3, 2), t[2] * scale)):
        x2.put(i, j, value)
        values[(term + 1, i, j)] = value
    for a, b in ((3, 4), (2, 1)):
        sums[SUMS.index((1, a, b))] = part(h, x0, a, a, b)
        sums[SUMS.index((1, b, a))] = part(h, x0, b, a, a)
    sums[SUMS.index((3, 2, 2))] = part(h, x2, 2, 3, 2)
    sums[SUMS.index((3, 3, 3))] = part(h, x2, 3, 2, 3)
    add_terms(base, values, DONE_EARLY, phase)


def side(h, xs, a, b, start, payload, phase, scales, sums, record):
    x0, x1, x2 = xs
    c = [coefficient(3 * phase + n) for n in range(3)]
    low = min(a, b)
    at_a, at_b = (0, 3) if a == low else (3, 0)
    up, down = (low, low + 1), (low + 1, low)

    def known(level, i, j):
        return sums[SUMS.index((level, i, j))]

    def put(level, i, j, value):
        record(level, i, j, value)
        if level < 3:
            xs[level].put(i, j, value)

    first = 1 - phase
    x0.put(b, b, start)
    x1.put(b, b, slot(payload, first))
    put(1, a, b, (part(h, x0, a, b, b) + known(1, a, b)) * scales[0])
    put(1, b, a, (part(h, x0, b, b, a) + known(1, b, a)) * scales[0])
    t = tile(h, x1, low)
    put(2, a, a, (t[at_a] + known(2, a, a)) * c[1])
    put(2, b, b, (t[at_b] + slot(payload, first + 1)) * c[1])
    put(2, *up, t[1] * scales[1])
    put(2, *down, t[2] * scales[1])

    def last():
        row = piece(h, x2, (a,), (low, low + 1), (low, low + 1))[0]
        here, there = (row[:, :BS], row[:, BS:]) if a == low else (row[:, BS:], row[:, :BS])
        put(3, a, b, there * scales[2])
        put(3, a, a, (here + known(3, a, a)) * c[2])
        if phase:
            put(3, b, a, piece(h, x2, (b,), (low, low + 1), (a, a))[0] * scales[2])
            return None
        row = piece(h, x2, (b,), (low, low + 1), (low, low + 1))[0]
        here, there = (row[:, :BS], row[:, BS:]) if b == low else (row[:, BS:], row[:, :BS])
        put(3, b, a, there * scales[2])
        return here

    return last


def near_side(h, xs, start, near, phase, table, base, sums):
    term = 3 * phase
    values = {}

    def record(level, i, j, value):
        values[(term + level - 1, i, j)] = value

    scales = [line(table, 12 + term + n) for n in range(3)]
    own_part = side(h, xs, 3, 4, start, near, phase, scales, sums, record)()
    x2 = xs[2]
    sums[SUMS.index((3, 2, 3))] = one_side(h, x2, 2, (2, 3), 3) + one_side(x2, h.minus, 2, (3, 3), 3)
    sums[SUMS.index((3, 3, 2))] = one_side(h, x2, 3, (3, 3), 2) + one_side(x2, h.minus, 3, (2, 3), 2)
    add_terms(base, values, DONE_NEAR, phase)
    return values, own_part


def far_side(h, xs, start, far, phase, table, sums, record, between=lambda: None):
    term = 3 * phase
    scales = [line(table, term + n) for n in range(3)]
    last = side(h, xs, 2, 1, start, far, phase, scales, sums, record)
    x2 = xs[2]
    scale = line(table, 6 + term + 2)
    record(3, 2, 3, (one_side(x2, h.minus, 2, (2, 2), 3) + sums[SUMS.index((3, 2, 3))]) * scale)
    record(3, 3, 2, (one_side(h, x2, 3, (2, 2), 2) + sums[SUMS.index((3, 3, 2))]) * scale)
    between()
    return last()


def rest_first(re_in, im_in, table, early, h_ref, x_in, sums_in, x_ref, sums, base):
    h, xs = views(h_ref, x_ref)
    for index, ((row, offset), _) in enumerate(OWN):
        base[index, 0], base[index, 1] = own(re_in, row, offset), own(im_in, row, offset)
    own_rest(h, xs, 0, table, early, base, sums)


def near_first(
    near, table, h_in, x_in, sums_in, base_in, h_ref, x_ref, sums, base, own_part, part_far, part_near
):
    h, xs = views(h_ref, x_ref)
    h.put(4, 4, get_symmetric(near))
    values, own_part[...] = near_side(h, xs, slot(near, 0), near, 0, table, base, sums)
    for i, j in ((3, 3), (3, 4), (4, 3)):
        xs[0].put(i, j, values[(2, i, j)])
    part_far[0:BS, :] = sums[SUMS.index((3, 2, 2))]
    part_far[BS:, :] = jnp.zeros((FAR_PART_ROWS - BS, BS), f32)
    part_near[0:BS, :] = sums[SUMS.index((3, 3, 3))]
    part_near[BS:, :] = jnp.zeros((PART_ROWS - BS, BS), f32)


def far_first(far, table, h_in, x_in, sums_in, h_ref, x_ref, sums, late, early, far_next, own_part, carry):
    h, xs = views(h_ref, x_ref)
    h.put(1, 1, get_symmetric(far))
    state = {}

    def record(level, i, j, value):
        if (level, i, j) in LATE:
            late[LATE.index((level, i, j))] = value
        if level == 3:
            state[(i, j)] = value

    own_part[...] = far_side(h, xs, slot(far, 0), far, 0, table, sums, record)
    for (i, j), value in state.items():
        xs[0].put(i, j, value)
    before_far(h, xs, 1, table, sums, early, far_next, carry)


def rest_second(late, early, table, h_ref, x_in, sums_in, base_in, x_ref, sums, base):
    h, xs = views(h_ref, x_ref)
    values = {(level - 1, i, j): late[index] for index, (level, i, j) in enumerate(LATE)}
    add_terms(base, values, DONE_FAR, 0)
    own_rest(h, xs, 1, table, early, base, sums)


def near_second(near, own_part, part_near, table, h_ref, x_in, sums_in, base_in, x_ref, sums, base):
    h, xs = views(h_ref, x_ref)
    start = (own_part[...] + part_near[0:BS, :]) * coefficient(2)
    near_side(h, xs, start, near, 1, table, base, sums)


def far_second(far, own_part, part_far, table, sums, base, h_ref, x_in, x_ref, out_re, out_im, stage, sems):
    h, xs = views(h_ref, x_ref)
    copies = []
    for index, ((row, offset), _) in enumerate(OWN):
        r, e = own_index(row, offset)
        source = stage if index < 4 else base
        for a, out in enumerate((out_re, out_im)):
            copies.append(pltpu.make_async_copy(source.at[index, a], out.at[r, e], sems.at[len(copies)]))

    def send(first):
        for copy in copies[2 * first : 2 * first + 4]:
            copy.start()

    def apart(first):
        pl.when(lax.axis_index("col") >= 0)(lambda: send(first))

    apart(4)
    values = {}

    def record(level, i, j, value):
        values[(level + 2, i, j)] = value

    def finish(index):
        i, j = OWN[index][1]
        real, imag = parts_of(values, i, j, [level + 2 for level in DONE_FAR[(i, j)]])
        stage[index, 0], stage[index, 1] = base[index, 0] + real, base[index, 1] + imag

    def between():
        finish(2)
        finish(3)
        apart(2)

    start = (own_part[...] + part_far[0:BS, :]) * coefficient(2)
    far_side(h, xs, start, far, 1, table, sums, record, between)
    finish(0)
    finish(1)
    send(0)
    for copy in copies:
        copy.wait()


VECTOR = pl.BlockSpec(memory_space=pltpu.VMEM)
SCALAR = pl.BlockSpec(memory_space=pltpu.SMEM)
BIG = pl.BlockSpec(memory_space=pltpu.HBM)


def call(kernel, ins, outs, scratch=(), aliases=None):
    return pl.pallas_call(
        kernel,
        out_shape=[shape for shape, _ in outs],
        in_specs=ins,
        out_specs=[spec for _, spec in outs],
        scratch_shapes=list(scratch),
        input_output_aliases=aliases or {},
        compiler_params=pltpu.CompilerParams(vmem_limit_bytes=24 * 2**20),
        cost_estimate=pl.CostEstimate(flops=0, bytes_accessed=0, transcendentals=0),
    )


def vector(*shape, dtype=f32):
    return jax.ShapeDtypeStruct(shape, dtype), VECTOR


def body(density_real, density_imag, hamiltonian, dipole, field, pattern):
    count = lax.axis_size(RING)
    pair = [(i, i ^ 1) for i in range(count)]
    cross = [(i, (i + 1) % count if i % 2 else (i - 1) % count) for i in range(count)]
    pattern = jnp.transpose(pattern, (2, 1, 0))
    whole = density_real.shape
    inputs = [
        pltpu.with_memory_space_constraint(x, pltpu.HBM)
        for x in (density_real, density_imag, hamiltonian, dipole, pattern)
    ]
    dma = pltpu.SemaphoreType.DMA
    h_out, x_out = vector(4, ROWS, BS, 3 * BS, dtype=bf16), vector(3, 2, ROWS, BS, 3 * BS, dtype=bf16)
    base_out, sums_out = vector(len(OWN), 2, BS, BS), vector(len(SUMS), BS, BS)
    carry_out, early_out, late_out = vector(BS, BS), vector(len(EARLY), BS, BS), vector(len(LATE), BS, BS)
    out = (jax.ShapeDtypeStruct(whole, f32), BIG)

    far, table, h, x, sums, early, carry, re_in, im_in, ham_in, dip_in = call(
        own_first,
        [BIG] * 5 + [SCALAR],
        [
            vector(FIRST_ROWS + 2 * MORE, BS),
            vector(TABLE_ROWS, BS),
            h_out,
            x_out,
            sums_out,
            early_out,
            carry_out,
        ]
        + [vector(*whole)] * 4,
        [pltpu.SMEM(pattern.shape, jnp.int32), dma((5,))],
    )(*inputs, field)
    far = lax.ppermute(far, RING, cross)
    h, near, x, sums, early = call(
        before_near_first,
        [VECTOR] * 10,
        [h_out, vector(FIRST_ROWS, BS), x_out, sums_out, early_out],
        aliases={6: 0, 7: 2, 8: 3, 9: 4},
    )(carry, table, re_in, im_in, ham_in, dip_in, h, x, sums, early)
    near = lax.ppermute(near, RING, pair)
    x, sums, base = call(
        rest_first,
        [VECTOR] * 7,
        [x_out, sums_out, base_out],
        aliases={5: 0, 6: 1},
    )(re_in, im_in, table, early, h, x, sums)
    h, x, sums, base, own_near, part_far, part_near = call(
        near_first,
        [VECTOR] * 6,
        [h_out, x_out, sums_out, base_out, carry_out, vector(FAR_PART_ROWS, BS), vector(PART_ROWS, BS)],
        aliases={2: 0, 3: 1, 4: 2, 5: 3},
    )(near, table, h, x, sums, base)
    part_far = lax.ppermute(part_far, RING, cross)
    part_near = lax.ppermute(part_near, RING, pair)
    h, x, sums, late, early, far, own_far, carry = call(
        far_first,
        [VECTOR] * 5,
        [
            h_out,
            x_out,
            sums_out,
            late_out,
            early_out,
            vector(SECOND_ROWS + MORE, BS),
            carry_out,
            carry_out,
        ],
        aliases={2: 0, 3: 1, 4: 2},
    )(far, table, h, x, sums)
    far = lax.ppermute(far, RING, cross)
    near, x, sums, early = call(
        before_near_second,
        [VECTOR] * 5,
        [vector(SECOND_ROWS, BS), x_out, sums_out, early_out],
        aliases={2: 1, 3: 2, 4: 3},
    )(carry, h, x, sums, early)
    near = lax.ppermute(near, RING, pair)
    x, sums, base = call(
        rest_second,
        [VECTOR] * 7,
        [x_out, sums_out, base_out],
        aliases={4: 0, 5: 1, 6: 2},
    )(late, early, table, h, x, sums, base)
    x, sums, base = call(
        near_second,
        [VECTOR] * 8,
        [x_out, sums_out, base_out],
        aliases={5: 0, 6: 1, 7: 2},
    )(near, own_near, part_near, table, h, x, sums, base)
    _, out_re, out_im = call(
        far_second,
        [VECTOR] * 8,
        [x_out, out, out],
        [pltpu.VMEM((4, 2, BS, BS), f32), dma((12,))],
        aliases={7: 0},
    )(far, own_far, part_far, table, sums, base, h, x)
    return out_re, out_im


def solution(mesh):
    in_specs = (
        P(("row", "col"), None, None, None),
        P(("row", "col"), None, None, None),
        P(("row", "col"), None, None, None),
        P(("parts", "row", "col"), None, None, None),
        P("parts"),
        P(None, ("row", "col"), None),
    )
    out_specs = (
        P(("parts", "row", "col"), None, None, None),
        P(("parts", "row", "col"), None, None, None),
    )
    return jax.shard_map(body, mesh=mesh, in_specs=in_specs, out_specs=out_specs, check_vma=False)
```

```python
import functools

import jax
import jax.numpy as jnp
from jax import lax
from jax.experimental import pallas as pl
from jax.experimental.pallas import tpu as pltpu
from jax.sharding import PartitionSpec as P

TERMS = 6
BS = 128
time_step = 0.5
RING = ("row", "col")
f32, bf16 = jnp.float32, jnp.bfloat16

ROWS = 6
SIGN_RE = (1.0, -1.0, -1.0, 1.0, 1.0, -1.0)
SIGN_IM = (-1.0, -1.0, 1.0, 1.0, -1.0, -1.0)
FIRST_ROWS = 3 * BS + BS // 2 + 8
SECOND_ROWS = 2 * BS
MORE = 8
PART_ROWS = SECOND_ROWS + 2 * MORE
FAR_PART_ROWS = SECOND_ROWS + 2 * MORE
TABLE_ROWS = 24


def own_index(row, offset):
    core = lax.axis_index("col")
    return jnp.where(core == 0, row, 1 - row), jnp.where(core == 0, 1 + offset, 1 - offset)


def own(ref, row, offset):
    r, e = own_index(row, offset)
    return ref[r, e]


def slot(ref, index):
    return ref[index * BS : (index + 1) * BS, :]


def line(ref, index):
    return ref[index : index + 1, :]


class Band:
    def __init__(self, ref, negated=False):
        self.high, self.low = ref.at[0], ref.at[1]
        self.minus = Band(ref.at[pl.ds(2, 2)]) if negated else None

    def put(self, i, j, value):
        part = slice((j - i + 1) * BS, (j - i + 2) * BS)
        high = value.astype(bf16)
        low = (value - high.astype(f32)).astype(bf16)
        self.high[i, :, part] = high
        self.low[i, :, part] = low
        if self.minus is not None:
            self.minus.high[i, :, part] = -high
            self.minus.low[i, :, part] = -low

    def left(self, i, first, last):
        part = slice((first - i + 1) * BS, (last - i + 2) * BS)
        high, low = self.high[i, :, part], self.low[i, :, part]
        return [high, high, low]

    def right(self, first, last, j, j_last):
        highs, lows = [], []
        for k in range(first, last + 1):
            part = slice((j - k + 1) * BS, (j_last - k + 2) * BS)
            highs.append(self.high[k, :, part])
            lows.append(self.low[k, :, part])
        return highs + lows + highs


def piece(h, x, rows, mids, cols):
    after_h = jnp.concatenate(x.right(*mids, *cols), axis=0)
    after_x = jnp.concatenate(h.minus.right(*mids, *cols), axis=0)

    def product(left, right):
        return jnp.dot(jnp.concatenate(left, axis=1), right, preferred_element_type=f32)

    return [product(h.left(i, *mids), after_h) + product(x.left(i, *mids), after_x) for i in rows]


def one_side(a, b, row, mids, col):
    left = jnp.concatenate(a.left(row, *mids), axis=1)
    right = jnp.concatenate(b.right(*mids, col, col), axis=0)
    return jnp.dot(left, right, preferred_element_type=f32)


def tile(h, x, i):
    upper, lower = piece(h, x, (i, i + 1), (i, i + 1), (i, i + 1))
    return upper[:, :BS], upper[:, BS:], lower[:, :BS], lower[:, BS:]


def part(h, x, i, k, j):
    return piece(h, x, (i,), (k, k), (j, j))[0]


def half_places():
    shape = (BS // 2, BS)
    return lax.broadcasted_iota(jnp.int32, shape, 0), lax.broadcasted_iota(jnp.int32, shape, 1)


def swap_halves(rows):
    return jnp.concatenate([rows[:, BS // 2 :], rows[:, : BS // 2]], axis=1)


def put_symmetric(payload, block):
    r, c = half_places()
    turned = swap_halves(block[BS // 2 :])
    first = 3 * BS
    payload[first : first + BS // 2, :] = jnp.where(c < r, turned, block[: BS // 2])
    payload[first + BS // 2 : first + BS // 2 + 1, :] = jnp.sum(jnp.where(c == r, turned, 0.0), axis=0, keepdims=True)


def get_symmetric(payload):
    r, c = half_places()
    first = 3 * BS
    rows = payload[first : first + BS // 2, :]
    turned = jnp.concatenate([rows, rows], axis=0).T
    upper = jnp.where(c < r, turned[: BS // 2], rows)
    quarter = jnp.where(c < r, rows, turned[: BS // 2])
    quarter = jnp.where(c == r, line(payload, first + BS // 2), quarter)
    lower = jnp.where(c < BS // 2, turned[BS // 2 :], swap_halves(quarter))
    return jnp.concatenate([upper, lower], axis=0)


def coefficient(term):
    return time_step / (term + 1)


SUMS = ((1, 2, 1), (1, 1, 2), (1, 3, 4), (1, 4, 3), (2, 2, 2), (2, 3, 3), (3, 2, 2), (3, 3, 3), (3, 2, 3), (3, 3, 2))
OWN = (((0, -1), (2, 1)), ((0, 0), (2, 2)), ((0, 1), (2, 3)), ((1, -1), (3, 2)), ((1, 0), (3, 3)), ((1, 1), (3, 4)))
EARLY = ((1, 2, 2), (1, 3, 3), (1, 2, 3), (1, 3, 2))
LATE = ((1, 2, 1), (1, 1, 2), (2, 2, 1), (2, 1, 2), (3, 2, 1), (3, 1, 2), (2, 2, 2), (3, 2, 2), (3, 2, 3), (3, 3, 2))
DONE_EARLY = {(2, 2): (1,), (2, 3): (1, 2), (3, 2): (1, 2), (3, 3): (1,)}
DONE_NEAR = {(3, 3): (2, 3), (3, 4): (1, 2, 3)}
DONE_FAR = {(2, 1): (1, 2, 3), (2, 2): (2, 3), (2, 3): (3,), (3, 2): (3,)}


def weighted(terms_of, signs):
    total = None
    for sign, value in zip(signs, terms_of):
        total = (value if sign > 0 else -value) if total is None else (total + value if sign > 0 else total - value)
    return total


def parts_of(values, i, j, terms):
    re_signs, im_signs = [SIGN_RE[term] for term in terms], [SIGN_IM[term] for term in terms]
    here = [values[(term, i, j)] for term in terms]
    there = here if i == j else [values[(term, j, i)] for term in terms]
    real = 0.5 * (weighted(here, re_signs) + weighted(there, re_signs).T)
    imag = 0.5 * (weighted(here, im_signs) - weighted(there, im_signs).T)
    return real, imag


def add_terms(base, values, done, phase):
    for index, (_, (i, j)) in enumerate(OWN):
        terms = [level - 1 + 3 * phase for level in done.get((i, j), ())]
        if terms:
            real, imag = parts_of(values, i, j, terms)
            base[index, 0] = base[index, 0] + real
            base[index, 1] = base[index, 1] + imag


def views(h_ref, x_ref):
    return Band(h_ref, True), [Band(x_ref.at[level]) for level in range(3)]


def before_far(h, xs, phase, table, sums, early, far, carry):
    x0, x1, _ = xs
    term = 3 * phase
    t = tile(h, x0, 2)
    scale = line(table, 6 + term)
    inner = {
        (2, 2): (t[0] + part(h, x0, 2, 1, 2)) * coefficient(term),
        (2, 3): t[1] * scale,
        (3, 2): t[2] * scale,
    }
    for (i, j), value in inner.items():
        x1.put(i, j, value)
        early[EARLY.index((1, i, j))] = value
    carry[...] = t[3]
    first = 1 - phase
    far[first * BS : (first + 1) * BS, :] = inner[(2, 2)]
    value = part(h, x1, 2, 3, 2)
    far[(first + 1) * BS : (first + 2) * BS, :] = value
    sums[SUMS.index((2, 2, 2))] = value


def before_near_first(carry, h_ref, near_in, x_in, sums_in, early_in, near, x_ref, sums, early):
    before_near(carry, h_ref, x_ref, sums, early, near, 0)


def before_near_second(carry, h_ref, x_in, sums_in, early_in, near, x_ref, sums, early):
    before_near(carry, h_ref, x_ref, sums, early, near, 1)


def before_near(carry, h_ref, x_ref, sums, early, near, phase):
    h, (x0, x1, _) = views(h_ref, x_ref)
    first = 1 - phase
    value = (carry[...] + part(h, x0, 3, 4, 3)) * coefficient(3 * phase)
    x1.put(3, 3, value)
    early[EARLY.index((1, 3, 3))] = value
    near[first * BS : (first + 1) * BS, :] = value
    value = part(h, x1, 3, 2, 3)
    near[(first + 1) * BS : (first + 2) * BS, :] = value
    sums[SUMS.index((2, 3, 3))] = value


def own_first(
    re, im, ham, dip, pattern_in, field,
    far, near, table, h_ref, x_ref, sums, early, carry, re_in, im_in,
    ham_in, dip_in, pattern, sems,
):
    copies = [
        pltpu.make_async_copy(source, target, sems.at[n])
        for n, (source, target) in enumerate(
            ((pattern_in, pattern), (ham, ham_in), (dip, dip_in), (re, re_in), (im, im_in))
        )
    ]
    for copy in copies:
        copy.start()
    copies[0].wait()
    for n, (row, offset) in enumerate(((0, -1), (0, 1), (1, 1))):
        r, e = own_index(row, offset)
        for term in range(TERMS):
            table[6 * n + term : 6 * n + term + 1, :] = jnp.full(
                (1, BS), pattern[e, r, term].astype(f32) * coefficient(term), f32
            )
    h, xs = views(h_ref, x_ref)
    for copy in copies[1:3]:
        copy.wait()
    for (row, offset), (i, j) in OWN:
        value = own(ham_in, row, offset) + field[0] * own(dip_in, row, offset)
        h.put(i, j, value)
        if j in (1, 4):
            h.put(j, i, value.T)
        if i == j:
            put_symmetric(far if i == 2 else near, value)
    for copy in copies[3:]:
        copy.wait()
    for (row, offset), (i, j) in OWN:
        real, imag = own(re_in, row, offset), own(im_in, row, offset)
        xs[0].put(i, j, real + imag)
        if j in (1, 4):
            xs[0].put(j, i, (real - imag).T)
        if i == j:
            (far if i == 2 else near)[0:BS, :] = real + imag
    before_far(h, xs, 0, table, sums, early, far, carry)


def own_rest(h, xs, phase, table, early, base, sums):
    x0, x1, x2 = xs
    term = 3 * phase
    values = {(term, i, j): early[index] for index, (_, i, j) in enumerate(EARLY)}
    t = tile(h, x1, 2)
    scale = line(table, 6 + term + 1)
    for (i, j), value in (((2, 3), t[1] * scale), ((3, 2), t[2] * scale)):
        x2.put(i, j, value)
        values[(term + 1, i, j)] = value
    for a, b in ((3, 4), (2, 1)):
        sums[SUMS.index((1, a, b))] = part(h, x0, a, a, b)
        sums[SUMS.index((1, b, a))] = part(h, x0, b, a, a)
    sums[SUMS.index((3, 2, 2))] = part(h, x2, 2, 3, 2)
    sums[SUMS.index((3, 3, 3))] = part(h, x2, 3, 2, 3)
    add_terms(base, values, DONE_EARLY, phase)


def side(h, xs, a, b, start, payload, phase, scales, sums, record, place=lambda: None):
    x0, x1, x2 = xs
    c = [coefficient(3 * phase + n) for n in range(3)]
    low = min(a, b)
    at_a, at_b = (0, 3) if a == low else (3, 0)
    up, down = (low, low + 1), (low + 1, low)

    def known(level, i, j):
        return sums[SUMS.index((level, i, j))]

    def put(level, i, j, value):
        record(level, i, j, value)
        if level < 3:
            xs[level].put(i, j, value)

    first = 1 - phase
    x0.put(b, b, start)
    x1.put(b, b, slot(payload, first))
    row, col = one_side(h, x0, a, (b, b), b), one_side(x0, h.minus, b, (b, b), a)
    place()
    put(1, a, b, (row + one_side(x0, h.minus, a, (b, b), b) + known(1, a, b)) * scales[0])
    put(1, b, a, (col + one_side(h, x0, b, (b, b), a) + known(1, b, a)) * scales[0])
    t = tile(h, x1, low)
    put(2, a, a, (t[at_a] + known(2, a, a)) * c[1])
    put(2, b, b, (t[at_b] + slot(payload, first + 1)) * c[1])
    put(2, *up, t[1] * scales[1])
    put(2, *down, t[2] * scales[1])

    def last():
        row = piece(h, x2, (a,), (low, low + 1), (low, low + 1))[0]
        here, there = (row[:, :BS], row[:, BS:]) if a == low else (row[:, BS:], row[:, :BS])
        put(3, a, b, there * scales[2])
        put(3, a, a, (here + known(3, a, a)) * c[2])
        if phase:
            put(3, b, a, piece(h, x2, (b,), (low, low + 1), (a, a))[0] * scales[2])
            return None
        row = piece(h, x2, (b,), (low, low + 1), (low, low + 1))[0]
        here, there = (row[:, :BS], row[:, BS:]) if b == low else (row[:, BS:], row[:, :BS])
        put(3, b, a, there * scales[2])
        return here

    return last


def near_side(h, xs, start, near, phase, table, base, sums):
    term = 3 * phase
    values = {}

    def record(level, i, j, value):
        values[(term + level - 1, i, j)] = value

    scales = [line(table, 12 + term + n) for n in range(3)]
    own_part = side(h, xs, 3, 4, start, near, phase, scales, sums, record)()
    x2 = xs[2]
    sums[SUMS.index((3, 2, 3))] = one_side(h, x2, 2, (2, 3), 3) + one_side(x2, h.minus, 2, (3, 3), 3)
    sums[SUMS.index((3, 3, 2))] = one_side(h, x2, 3, (3, 3), 2) + one_side(x2, h.minus, 3, (2, 3), 2)
    add_terms(base, values, DONE_NEAR, phase)
    return values, own_part


def far_side(h, xs, start, far, phase, table, sums, record, between=lambda: None, place=lambda: None):
    term = 3 * phase
    scales = [line(table, term + n) for n in range(3)]
    last = side(h, xs, 2, 1, start, far, phase, scales, sums, record, place)
    x2 = xs[2]
    scale = line(table, 6 + term + 2)
    record(3, 2, 3, (one_side(x2, h.minus, 2, (2, 2), 3) + sums[SUMS.index((3, 2, 3))]) * scale)
    record(3, 3, 2, (one_side(h, x2, 3, (2, 2), 2) + sums[SUMS.index((3, 3, 2))]) * scale)
    between()
    return last()


def rest_first(re_in, im_in, table, early, h_ref, x_in, sums_in, x_ref, sums, base):
    h, xs = views(h_ref, x_ref)
    for index, ((row, offset), _) in enumerate(OWN):
        base[index, 0], base[index, 1] = own(re_in, row, offset), own(im_in, row, offset)
    own_rest(h, xs, 0, table, early, base, sums)


def near_first(
    near, table, h_in, x_in, sums_in, base_in, h_ref, x_ref, sums, base, own_part, part_far, part_near
):
    h, xs = views(h_ref, x_ref)
    h.put(4, 4, get_symmetric(near))
    values, own_part[...] = near_side(h, xs, slot(near, 0), near, 0, table, base, sums)
    for i, j in ((3, 3), (3, 4), (4, 3)):
        xs[0].put(i, j, values[(2, i, j)])
    part_far[0:BS, :] = sums[SUMS.index((3, 2, 2))]
    part_far[BS:, :] = jnp.zeros((FAR_PART_ROWS - BS, BS), f32)
    part_near[0:BS, :] = sums[SUMS.index((3, 3, 3))]
    part_near[BS:, :] = jnp.zeros((PART_ROWS - BS, BS), f32)


def far_first(far, table, h_in, x_in, sums_in, h_ref, x_ref, sums, late, early, far_next, own_part, carry):
    h, xs = views(h_ref, x_ref)
    state = {}

    def record(level, i, j, value):
        if (level, i, j) in LATE:
            late[LATE.index((level, i, j))] = value
        if level == 3:
            state[(i, j)] = value

    own_part[...] = far_side(
        h, xs, slot(far, 0), far, 0, table, sums, record, place=lambda: h.put(1, 1, get_symmetric(far))
    )
    for (i, j), value in state.items():
        xs[0].put(i, j, value)
    before_far(h, xs, 1, table, sums, early, far_next, carry)


def rest_second(late, early, table, h_ref, x_in, sums_in, base_in, x_ref, sums, base):
    h, xs = views(h_ref, x_ref)
    values = {(level - 1, i, j): late[index] for index, (level, i, j) in enumerate(LATE)}
    add_terms(base, values, DONE_FAR, 0)
    own_rest(h, xs, 1, table, early, base, sums)


def near_second(near, own_part, part_near, table, h_ref, x_in, sums_in, base_in, x_ref, sums, base):
    h, xs = views(h_ref, x_ref)
    start = (own_part[...] + part_near[0:BS, :]) * coefficient(2)
    near_side(h, xs, start, near, 1, table, base, sums)


def far_second(far, own_part, part_far, table, sums, base, h_ref, x_in, x_ref, out_re, out_im, stage, sems):
    h, xs = views(h_ref, x_ref)
    copies = []
    for index, ((row, offset), _) in enumerate(OWN):
        r, e = own_index(row, offset)
        source = stage if index < 4 else base
        for a, out in enumerate((out_re, out_im)):
            copies.append(pltpu.make_async_copy(source.at[index, a], out.at[r, e], sems.at[len(copies)]))

    def send(first):
        for copy in copies[2 * first : 2 * first + 4]:
            copy.start()

    def apart(first):
        pl.when(lax.axis_index("col") >= 0)(lambda: send(first))

    apart(4)
    values = {}

    def record(level, i, j, value):
        values[(level + 2, i, j)] = value

    def finish(index):
        i, j = OWN[index][1]
        real, imag = parts_of(values, i, j, [level + 2 for level in DONE_FAR[(i, j)]])
        stage[index, 0], stage[index, 1] = base[index, 0] + real, base[index, 1] + imag

    def between():
        finish(2)
        finish(3)
        apart(2)

    start = (own_part[...] + part_far[0:BS, :]) * coefficient(2)
    far_side(h, xs, start, far, 1, table, sums, record, between)
    finish(0)
    finish(1)
    send(0)
    for copy in copies:
        copy.wait()


VECTOR = pl.BlockSpec(memory_space=pltpu.VMEM)
SCALAR = pl.BlockSpec(memory_space=pltpu.SMEM)
BIG = pl.BlockSpec(memory_space=pltpu.HBM)


def call(kernel, ins, outs, scratch=(), aliases=None):
    return pl.pallas_call(
        kernel,
        out_shape=[shape for shape, _ in outs],
        in_specs=ins,
        out_specs=[spec for _, spec in outs],
        scratch_shapes=list(scratch),
        input_output_aliases=aliases or {},
        compiler_params=pltpu.CompilerParams(vmem_limit_bytes=24 * 2**20),
        cost_estimate=pl.CostEstimate(flops=0, bytes_accessed=0, transcendentals=0),
    )


def vector(*shape, dtype=f32):
    return jax.ShapeDtypeStruct(shape, dtype), VECTOR


def body(density_real, density_imag, hamiltonian, dipole, field, pattern):
    count = lax.axis_size(RING)
    pair = [(i, i ^ 1) for i in range(count)]
    cross = [(i, (i + 1) % count if i % 2 else (i - 1) % count) for i in range(count)]
    pattern = jnp.transpose(pattern, (2, 1, 0))
    whole = density_real.shape
    inputs = [
        pltpu.with_memory_space_constraint(x, pltpu.HBM)
        for x in (density_real, density_imag, hamiltonian, dipole, pattern)
    ]
    dma = pltpu.SemaphoreType.DMA
    h_out, x_out = vector(4, ROWS, BS, 3 * BS, dtype=bf16), vector(3, 2, ROWS, BS, 3 * BS, dtype=bf16)
    base_out, sums_out = vector(len(OWN), 2, BS, BS), vector(len(SUMS), BS, BS)
    carry_out, early_out, late_out = vector(BS, BS), vector(len(EARLY), BS, BS), vector(len(LATE), BS, BS)
    out = (jax.ShapeDtypeStruct(whole, f32), BIG)

    far, near, table, h, x, sums, early, carry, re_in, im_in = call(
        own_first,
        [BIG] * 5 + [SCALAR],
        [
            vector(FIRST_ROWS + 2 * MORE, BS),
            vector(FIRST_ROWS, BS),
            vector(TABLE_ROWS, BS),
            h_out,
            x_out,
            sums_out,
            early_out,
            carry_out,
            vector(*whole),
            vector(*whole),
        ],
        [pltpu.VMEM(whole, f32)] * 2 + [pltpu.SMEM(pattern.shape, jnp.int32), dma((5,))],
    )(*inputs, field)
    far = lax.ppermute(far, RING, cross)
    near, x, sums, early = call(
        before_near_first,
        [VECTOR] * 6,
        [vector(FIRST_ROWS, BS), x_out, sums_out, early_out],
        aliases={2: 0, 3: 1, 4: 2, 5: 3},
    )(carry, h, near, x, sums, early)
    near = lax.ppermute(near, RING, pair)
    x, sums, base = call(
        rest_first,
        [VECTOR] * 7,
        [x_out, sums_out, base_out],
        aliases={5: 0, 6: 1},
    )(re_in, im_in, table, early, h, x, sums)
    h, x, sums, base, own_near, part_far, part_near = call(
        near_first,
        [VECTOR] * 6,
        [h_out, x_out, sums_out, base_out, carry_out, vector(FAR_PART_ROWS, BS), vector(PART_ROWS, BS)],
        aliases={2: 0, 3: 1, 4: 2, 5: 3},
    )(near, table, h, x, sums, base)
    part_far = lax.ppermute(part_far, RING, cross)
    part_near = lax.ppermute(part_near, RING, pair)
    h, x, sums, late, early, far, own_far, carry = call(
        far_first,
        [VECTOR] * 5,
        [
            h_out,
            x_out,
            sums_out,
            late_out,
            early_out,
            vector(SECOND_ROWS + MORE, BS),
            carry_out,
            carry_out,
        ],
        aliases={2: 0, 3: 1, 4: 2},
    )(far, table, h, x, sums)
    far = lax.ppermute(far, RING, cross)
    near, x, sums, early = call(
        before_near_second,
        [VECTOR] * 5,
        [vector(SECOND_ROWS, BS), x_out, sums_out, early_out],
        aliases={2: 1, 3: 2, 4: 3},
    )(carry, h, x, sums, early)
    near = lax.ppermute(near, RING, pair)
    x, sums, base = call(
        rest_second,
        [VECTOR] * 7,
        [x_out, sums_out, base_out],
        aliases={4: 0, 5: 1, 6: 2},
    )(late, early, table, h, x, sums, base)
    x, sums, base = call(
        near_second,
        [VECTOR] * 8,
        [x_out, sums_out, base_out],
        aliases={5: 0, 6: 1, 7: 2},
    )(near, own_near, part_near, table, h, x, sums, base)
    _, out_re, out_im = call(
        far_second,
        [VECTOR] * 8,
        [x_out, out, out],
        [pltpu.VMEM((4, 2, BS, BS), f32), dma((12,))],
        aliases={7: 0},
    )(far, own_far, part_far, table, sums, base, h, x)
    return out_re, out_im


def solution(mesh):
    in_specs = (
        P(("row", "col"), None, None, None),
        P(("row", "col"), None, None, None),
        P(("row", "col"), None, None, None),
        P(("parts", "row", "col"), None, None, None),
        P("parts"),
        P(None, ("row", "col"), None),
    )
    out_specs = (
        P(("parts", "row", "col"), None, None, None),
        P(("parts", "row", "col"), None, None, None),
    )
    return jax.shard_map(body, mesh=mesh, in_specs=in_specs, out_specs=out_specs, check_vma=False)
```

```python
import functools

import jax
import jax.numpy as jnp
from jax import lax
from jax.experimental import pallas as pl
from jax.experimental.pallas import tpu as pltpu
from jax.sharding import PartitionSpec as P

TERMS = 6
BS = 128
time_step = 0.5
RING = ("row", "col")
f32, bf16 = jnp.float32, jnp.bfloat16

ROWS = 6
SIGN_RE = (1.0, -1.0, -1.0, 1.0, 1.0, -1.0)
SIGN_IM = (-1.0, -1.0, 1.0, 1.0, -1.0, -1.0)
FIRST_ROWS = 3 * BS + BS // 2 + 8
SECOND_ROWS = 2 * BS
MORE = 1
PART_ROWS = SECOND_ROWS + 2
FAR_PART_ROWS = SECOND_ROWS + 2
TABLE_ROWS = 24


def own_index(row, offset):
    core = lax.axis_index("col")
    return jnp.where(core == 0, row, 1 - row), jnp.where(core == 0, 1 + offset, 1 - offset)


def own(ref, row, offset):
    r, e = own_index(row, offset)
    return ref[r, e]


def slot(ref, index):
    return ref[index * BS : (index + 1) * BS, :]


def line(ref, index):
    return ref[index : index + 1, :]


class Band:
    def __init__(self, ref, negated=False):
        self.high, self.low = ref.at[0], ref.at[1]
        self.minus = Band(ref.at[pl.ds(2, 2)]) if negated else None

    def put(self, i, j, value):
        part = slice((j - i + 1) * BS, (j - i + 2) * BS)
        high = value.astype(bf16)
        low = (value - high.astype(f32)).astype(bf16)
        self.high[i, :, part] = high
        self.low[i, :, part] = low
        if self.minus is not None:
            self.minus.high[i, :, part] = -high
            self.minus.low[i, :, part] = -low

    def left(self, i, first, last):
        part = slice((first - i + 1) * BS, (last - i + 2) * BS)
        high, low = self.high[i, :, part], self.low[i, :, part]
        return [high, high, low]

    def right(self, first, last, j, j_last):
        highs, lows = [], []
        for k in range(first, last + 1):
            part = slice((j - k + 1) * BS, (j_last - k + 2) * BS)
            highs.append(self.high[k, :, part])
            lows.append(self.low[k, :, part])
        return highs + lows + highs


def piece(h, x, rows, mids, cols):
    after_h = jnp.concatenate(x.right(*mids, *cols), axis=0)
    after_x = jnp.concatenate(h.minus.right(*mids, *cols), axis=0)

    def product(left, right):
        return jnp.dot(jnp.concatenate(left, axis=1), right, preferred_element_type=f32)

    return [product(h.left(i, *mids), after_h) + product(x.left(i, *mids), after_x) for i in rows]


def one_side(a, b, row, mids, col):
    left = jnp.concatenate(a.left(row, *mids), axis=1)
    right = jnp.concatenate(b.right(*mids, col, col), axis=0)
    return jnp.dot(left, right, preferred_element_type=f32)


def tile(h, x, i):
    upper, lower = piece(h, x, (i, i + 1), (i, i + 1), (i, i + 1))
    return upper[:, :BS], upper[:, BS:], lower[:, :BS], lower[:, BS:]


def part(h, x, i, k, j):
    return piece(h, x, (i,), (k, k), (j, j))[0]


def half_places():
    shape = (BS // 2, BS)
    return lax.broadcasted_iota(jnp.int32, shape, 0), lax.broadcasted_iota(jnp.int32, shape, 1)


def swap_halves(rows):
    return jnp.concatenate([rows[:, BS // 2 :], rows[:, : BS // 2]], axis=1)


def put_symmetric(payload, block):
    r, c = half_places()
    turned = swap_halves(block[BS // 2 :])
    first = 3 * BS
    payload[first : first + BS // 2, :] = jnp.where(c < r, turned, block[: BS // 2])
    payload[first + BS // 2 : first + BS // 2 + 1, :] = jnp.sum(jnp.where(c == r, turned, 0.0), axis=0, keepdims=True)


def get_symmetric(payload):
    r, c = half_places()
    first = 3 * BS
    rows = payload[first : first + BS // 2, :]
    turned = jnp.concatenate([rows, rows], axis=0).T
    upper = jnp.where(c < r, turned[: BS // 2], rows)
    quarter = jnp.where(c < r, rows, turned[: BS // 2])
    quarter = jnp.where(c == r, line(payload, first + BS // 2), quarter)
    lower = jnp.where(c < BS // 2, turned[BS // 2 :], swap_halves(quarter))
    return jnp.concatenate([upper, lower], axis=0)


def coefficient(term):
    return time_step / (term + 1)


SUMS = ((1, 2, 1), (1, 1, 2), (1, 3, 4), (1, 4, 3), (2, 2, 2), (2, 3, 3), (3, 2, 2), (3, 3, 3), (3, 2, 3), (3, 3, 2))
OWN = (((0, -1), (2, 1)), ((0, 0), (2, 2)), ((0, 1), (2, 3)), ((1, -1), (3, 2)), ((1, 0), (3, 3)), ((1, 1), (3, 4)))
EARLY = ((1, 2, 2), (1, 3, 3), (1, 2, 3), (1, 3, 2))
LATE = ((1, 2, 1), (1, 1, 2), (2, 2, 1), (2, 1, 2), (3, 2, 1), (3, 1, 2), (2, 2, 2), (3, 2, 2), (3, 2, 3), (3, 3, 2))
DONE_EARLY = {(2, 2): (1,), (2, 3): (1, 2), (3, 2): (1, 2), (3, 3): (1,)}
DONE_NEAR = {(3, 3): (2, 3), (3, 4): (1, 2, 3)}
DONE_FAR = {(2, 1): (1, 2, 3), (2, 2): (2, 3), (2, 3): (3,), (3, 2): (3,)}


def weighted(terms_of, signs):
    total = None
    for sign, value in zip(signs, terms_of):
        total = (value if sign > 0 else -value) if total is None else (total + value if sign > 0 else total - value)
    return total


def parts_of(values, i, j, terms):
    re_signs, im_signs = [SIGN_RE[term] for term in terms], [SIGN_IM[term] for term in terms]
    here = [values[(term, i, j)] for term in terms]
    there = here if i == j else [values[(term, j, i)] for term in terms]
    real = 0.5 * (weighted(here, re_signs) + weighted(there, re_signs).T)
    imag = 0.5 * (weighted(here, im_signs) - weighted(there, im_signs).T)
    return real, imag


def add_terms(base, values, done, phase):
    for index, (_, (i, j)) in enumerate(OWN):
        terms = [level - 1 + 3 * phase for level in done.get((i, j), ())]
        if terms:
            real, imag = parts_of(values, i, j, terms)
            base[index, 0] = base[index, 0] + real
            base[index, 1] = base[index, 1] + imag


def views(h_ref, x_ref):
    return Band(h_ref, True), [Band(x_ref.at[level]) for level in range(3)]


def before_far(h, xs, phase, table, sums, early, far, carry):
    x0, x1, _ = xs
    term = 3 * phase
    t = tile(h, x0, 2)
    scale = line(table, 6 + term)
    inner = {
        (2, 2): (t[0] + part(h, x0, 2, 1, 2)) * coefficient(term),
        (2, 3): t[1] * scale,
        (3, 2): t[2] * scale,
    }
    for (i, j), value in inner.items():
        x1.put(i, j, value)
        early[EARLY.index((1, i, j))] = value
    carry[...] = t[3]
    first = 1 - phase
    far[first * BS : (first + 1) * BS, :] = inner[(2, 2)]
    value = part(h, x1, 2, 3, 2)
    far[(first + 1) * BS : (first + 2) * BS, :] = value
    sums[SUMS.index((2, 2, 2))] = value


def before_near_first(carry, h_ref, near_in, x_in, sums_in, early_in, near, x_ref, sums, early):
    before_near(carry, h_ref, x_ref, sums, early, near, 0)


def before_near_second(carry, h_ref, x_in, sums_in, early_in, near, x_ref, sums, early):
    before_near(carry, h_ref, x_ref, sums, early, near, 1)


def before_near(carry, h_ref, x_ref, sums, early, near, phase):
    h, (x0, x1, _) = views(h_ref, x_ref)
    first = 1 - phase
    value = (carry[...] + part(h, x0, 3, 4, 3)) * coefficient(3 * phase)
    x1.put(3, 3, value)
    early[EARLY.index((1, 3, 3))] = value
    near[first * BS : (first + 1) * BS, :] = value
    value = part(h, x1, 3, 2, 3)
    near[(first + 1) * BS : (first + 2) * BS, :] = value
    sums[SUMS.index((2, 3, 3))] = value


def own_first(
    re, im, ham, dip, pattern_in, field,
    far, near, table, h_ref, x_ref, sums, early, carry, re_in, im_in,
    ham_in, dip_in, pattern, sems,
):
    copies = [
        pltpu.make_async_copy(source, target, sems.at[n])
        for n, (source, target) in enumerate(
            ((pattern_in, pattern), (ham, ham_in), (dip, dip_in), (re, re_in), (im, im_in))
        )
    ]
    for copy in copies:
        copy.start()
    copies[0].wait()
    for n, (row, offset) in enumerate(((0, -1), (0, 1), (1, 1))):
        r, e = own_index(row, offset)
        for term in range(TERMS):
            table[6 * n + term : 6 * n + term + 1, :] = jnp.full(
                (1, BS), pattern[e, r, term].astype(f32) * coefficient(term), f32
            )
    h, xs = views(h_ref, x_ref)
    for copy in copies[1:3]:
        copy.wait()
    for (row, offset), (i, j) in OWN:
        value = own(ham_in, row, offset) + field[0] * own(dip_in, row, offset)
        h.put(i, j, value)
        if j in (1, 4):
            h.put(j, i, value.T)
        if i == j:
            put_symmetric(far if i == 2 else near, value)
    for copy in copies[3:]:
        copy.wait()
    for (row, offset), (i, j) in OWN:
        real, imag = own(re_in, row, offset), own(im_in, row, offset)
        xs[0].put(i, j, real + imag)
        if j in (1, 4):
            xs[0].put(j, i, (real - imag).T)
        if i == j:
            (far if i == 2 else near)[0:BS, :] = real + imag
    before_far(h, xs, 0, table, sums, early, far, carry)


def own_rest(h, xs, phase, table, early, base, sums):
    x0, x1, x2 = xs
    term = 3 * phase
    values = {(term, i, j): early[index] for index, (_, i, j) in enumerate(EARLY)}
    t = tile(h, x1, 2)
    scale = line(table, 6 + term + 1)
    for (i, j), value in (((2, 3), t[1] * scale), ((3, 2), t[2] * scale)):
        x2.put(i, j, value)
        values[(term + 1, i, j)] = value
    for a, b in ((3, 4), (2, 1)):
        sums[SUMS.index((1, a, b))] = part(h, x0, a, a, b)
        sums[SUMS.index((1, b, a))] = part(h, x0, b, a, a)
    sums[SUMS.index((3, 2, 2))] = part(h, x2, 2, 3, 2)
    sums[SUMS.index((3, 3, 3))] = part(h, x2, 3, 2, 3)
    add_terms(base, values, DONE_EARLY, phase)


def side(h, xs, a, b, start, payload, phase, scales, sums, record):
    x0, x1, x2 = xs
    c = [coefficient(3 * phase + n) for n in range(3)]
    low = min(a, b)
    at_a, at_b = (0, 3) if a == low else (3, 0)
    up, down = (low, low + 1), (low + 1, low)

    def known(level, i, j):
        return sums[SUMS.index((level, i, j))]

    def put(level, i, j, value):
        record(level, i, j, value)
        if level < 3:
            xs[level].put(i, j, value)

    first = 1 - phase
    x0.put(b, b, start)
    x1.put(b, b, slot(payload, first))
    put(1, a, b, (part(h, x0, a, b, b) + known(1, a, b)) * scales[0])
    put(1, b, a, (part(h, x0, b, b, a) + known(1, b, a)) * scales[0])
    t = tile(h, x1, low)
    put(2, a, a, (t[at_a] + known(2, a, a)) * c[1])
    put(2, b, b, (t[at_b] + slot(payload, first + 1)) * c[1])
    put(2, *up, t[1] * scales[1])
    put(2, *down, t[2] * scales[1])

    def last():
        row = piece(h, x2, (a,), (low, low + 1), (low, low + 1))[0]
        here, there = (row[:, :BS], row[:, BS:]) if a == low else (row[:, BS:], row[:, :BS])
        put(3, a, b, there * scales[2])
        put(3, a, a, (here + known(3, a, a)) * c[2])
        if phase:
            put(3, b, a, piece(h, x2, (b,), (low, low + 1), (a, a))[0] * scales[2])
            return None
        row = piece(h, x2, (b,), (low, low + 1), (low, low + 1))[0]
        here, there = (row[:, :BS], row[:, BS:]) if b == low else (row[:, BS:], row[:, :BS])
        put(3, b, a, there * scales[2])
        return here

    return last


def near_side(h, xs, start, near, phase, table, base, sums):
    term = 3 * phase
    values = {}

    def record(level, i, j, value):
        values[(term + level - 1, i, j)] = value

    scales = [line(table, 12 + term + n) for n in range(3)]
    own_part = side(h, xs, 3, 4, start, near, phase, scales, sums, record)()
    x2 = xs[2]
    sums[SUMS.index((3, 2, 3))] = one_side(h, x2, 2, (2, 3), 3) + one_side(x2, h.minus, 2, (3, 3), 3)
    sums[SUMS.index((3, 3, 2))] = one_side(h, x2, 3, (3, 3), 2) + one_side(x2, h.minus, 3, (2, 3), 2)
    add_terms(base, values, DONE_NEAR, phase)
    return values, own_part


def far_side(h, xs, start, far, phase, table, sums, record, between=lambda: None):
    term = 3 * phase
    scales = [line(table, term + n) for n in range(3)]
    last = side(h, xs, 2, 1, start, far, phase, scales, sums, record)
    x2 = xs[2]
    scale = line(table, 6 + term + 2)
    record(3, 2, 3, (one_side(x2, h.minus, 2, (2, 2), 3) + sums[SUMS.index((3, 2, 3))]) * scale)
    record(3, 3, 2, (one_side(h, x2, 3, (2, 2), 2) + sums[SUMS.index((3, 3, 2))]) * scale)
    between()
    return last()


def rest_first(re_in, im_in, table, early, h_ref, x_in, sums_in, x_ref, sums, base):
    h, xs = views(h_ref, x_ref)
    for index, ((row, offset), _) in enumerate(OWN):
        base[index, 0], base[index, 1] = own(re_in, row, offset), own(im_in, row, offset)
    own_rest(h, xs, 0, table, early, base, sums)


def near_first(
    near, table, h_in, x_in, sums_in, base_in, h_ref, x_ref, sums, base, own_part, part_far, part_near
):
    h, xs = views(h_ref, x_ref)
    h.put(4, 4, get_symmetric(near))
    values, own_part[...] = near_side(h, xs, slot(near, 0), near, 0, table, base, sums)
    for i, j in ((3, 3), (3, 4), (4, 3)):
        xs[0].put(i, j, values[(2, i, j)])
    part_far[0:BS, :] = sums[SUMS.index((3, 2, 2))]
    part_far[BS:, :] = jnp.zeros((FAR_PART_ROWS - BS, BS), f32)
    part_near[0:BS, :] = sums[SUMS.index((3, 3, 3))]
    part_near[BS:, :] = jnp.zeros((PART_ROWS - BS, BS), f32)


def far_first(far, table, h_in, x_in, sums_in, h_ref, x_ref, sums, late, early, far_next, own_part, carry):
    h, xs = views(h_ref, x_ref)
    h.put(1, 1, get_symmetric(far))
    state = {}

    def record(level, i, j, value):
        if (level, i, j) in LATE:
            late[LATE.index((level, i, j))] = value
        if level == 3:
            state[(i, j)] = value

    own_part[...] = far_side(h, xs, slot(far, 0), far, 0, table, sums, record)
    for (i, j), value in state.items():
        xs[0].put(i, j, value)
    before_far(h, xs, 1, table, sums, early, far_next, carry)


def rest_second(late, early, table, h_ref, x_in, sums_in, base_in, x_ref, sums, base):
    h, xs = views(h_ref, x_ref)
    values = {(level - 1, i, j): late[index] for index, (level, i, j) in enumerate(LATE)}
    add_terms(base, values, DONE_FAR, 0)
    own_rest(h, xs, 1, table, early, base, sums)


def near_second(near, own_part, part_near, table, h_ref, x_in, sums_in, base_in, x_ref, sums, base):
    h, xs = views(h_ref, x_ref)
    start = (own_part[...] + part_near[0:BS, :]) * coefficient(2)
    near_side(h, xs, start, near, 1, table, base, sums)


def far_second(far, own_part, part_far, table, sums, base, h_ref, x_in, x_ref, out_re, out_im, stage, sems):
    h, xs = views(h_ref, x_ref)
    copies = []
    for index, ((row, offset), _) in enumerate(OWN):
        r, e = own_index(row, offset)
        source = stage if index < 4 else base
        for a, out in enumerate((out_re, out_im)):
            copies.append(pltpu.make_async_copy(source.at[index, a], out.at[r, e], sems.at[len(copies)]))

    def send(first):
        for copy in copies[2 * first : 2 * first + 4]:
            copy.start()

    def apart(first):
        pl.when(lax.axis_index("col") >= 0)(lambda: send(first))

    apart(4)
    values = {}

    def record(level, i, j, value):
        values[(level + 2, i, j)] = value

    def finish(index):
        i, j = OWN[index][1]
        real, imag = parts_of(values, i, j, [level + 2 for level in DONE_FAR[(i, j)]])
        stage[index, 0], stage[index, 1] = base[index, 0] + real, base[index, 1] + imag

    def between():
        finish(2)
        finish(3)
        apart(2)

    start = (own_part[...] + part_far[0:BS, :]) * coefficient(2)
    far_side(h, xs, start, far, 1, table, sums, record, between)
    finish(0)
    finish(1)
    send(0)
    for copy in copies:
        copy.wait()


VECTOR = pl.BlockSpec(memory_space=pltpu.VMEM)
SCALAR = pl.BlockSpec(memory_space=pltpu.SMEM)
BIG = pl.BlockSpec(memory_space=pltpu.HBM)


def call(kernel, ins, outs, scratch=(), aliases=None):
    return pl.pallas_call(
        kernel,
        out_shape=[shape for shape, _ in outs],
        in_specs=ins,
        out_specs=[spec for _, spec in outs],
        scratch_shapes=list(scratch),
        input_output_aliases=aliases or {},
        compiler_params=pltpu.CompilerParams(vmem_limit_bytes=24 * 2**20),
        cost_estimate=pl.CostEstimate(flops=0, bytes_accessed=0, transcendentals=0),
    )


def vector(*shape, dtype=f32):
    return jax.ShapeDtypeStruct(shape, dtype), VECTOR


def body(density_real, density_imag, hamiltonian, dipole, field, pattern):
    count = lax.axis_size(RING)
    pair = [(i, i ^ 1) for i in range(count)]
    cross = [(i, (i + 1) % count if i % 2 else (i - 1) % count) for i in range(count)]
    pattern = jnp.transpose(pattern, (2, 1, 0))
    whole = density_real.shape
    inputs = [
        pltpu.with_memory_space_constraint(x, pltpu.HBM)
        for x in (density_real, density_imag, hamiltonian, dipole, pattern)
    ]
    dma = pltpu.SemaphoreType.DMA
    h_out, x_out = vector(4, ROWS, BS, 3 * BS, dtype=bf16), vector(3, 2, ROWS, BS, 3 * BS, dtype=bf16)
    base_out, sums_out = vector(len(OWN), 2, BS, BS), vector(len(SUMS), BS, BS)
    carry_out, early_out, late_out = vector(BS, BS), vector(len(EARLY), BS, BS), vector(len(LATE), BS, BS)
    out = (jax.ShapeDtypeStruct(whole, f32), BIG)

    far, near, table, h, x, sums, early, carry, re_in, im_in = call(
        own_first,
        [BIG] * 5 + [SCALAR],
        [
            vector(FIRST_ROWS + 2 * MORE, BS),
            vector(FIRST_ROWS, BS),
            vector(TABLE_ROWS, BS),
            h_out,
            x_out,
            sums_out,
            early_out,
            carry_out,
            vector(*whole),
            vector(*whole),
        ],
        [pltpu.VMEM(whole, f32)] * 2 + [pltpu.SMEM(pattern.shape, jnp.int32), dma((5,))],
    )(*inputs, field)
    far = lax.ppermute(far, RING, cross)
    near, x, sums, early = call(
        before_near_first,
        [VECTOR] * 6,
        [vector(FIRST_ROWS, BS), x_out, sums_out, early_out],
        aliases={2: 0, 3: 1, 4: 2, 5: 3},
    )(carry, h, near, x, sums, early)
    near = lax.ppermute(near, RING, pair)
    x, sums, base = call(
        rest_first,
        [VECTOR] * 7,
        [x_out, sums_out, base_out],
        aliases={5: 0, 6: 1},
    )(re_in, im_in, table, early, h, x, sums)
    h, x, sums, base, own_near, part_far, part_near = call(
        near_first,
        [VECTOR] * 6,
        [h_out, x_out, sums_out, base_out, carry_out, vector(FAR_PART_ROWS, BS), vector(PART_ROWS, BS)],
        aliases={2: 0, 3: 1, 4: 2, 5: 3},
    )(near, table, h, x, sums, base)
    part_far = lax.ppermute(part_far, RING, cross)
    part_near = lax.ppermute(part_near, RING, pair)
    h, x, sums, late, early, far, own_far, carry = call(
        far_first,
        [VECTOR] * 5,
        [
            h_out,
            x_out,
            sums_out,
            late_out,
            early_out,
            vector(SECOND_ROWS + MORE, BS),
            carry_out,
            carry_out,
        ],
        aliases={2: 0, 3: 1, 4: 2},
    )(far, table, h, x, sums)
    far = lax.ppermute(far, RING, cross)
    near, x, sums, early = call(
        before_near_second,
        [VECTOR] * 5,
        [vector(SECOND_ROWS, BS), x_out, sums_out, early_out],
        aliases={2: 1, 3: 2, 4: 3},
    )(carry, h, x, sums, early)
    near = lax.ppermute(near, RING, pair)
    x, sums, base = call(
        rest_second,
        [VECTOR] * 7,
        [x_out, sums_out, base_out],
        aliases={4: 0, 5: 1, 6: 2},
    )(late, early, table, h, x, sums, base)
    x, sums, base = call(
        near_second,
        [VECTOR] * 8,
        [x_out, sums_out, base_out],
        aliases={5: 0, 6: 1, 7: 2},
    )(near, own_near, part_near, table, h, x, sums, base)
    _, out_re, out_im = call(
        far_second,
        [VECTOR] * 8,
        [x_out, out, out],
        [pltpu.VMEM((4, 2, BS, BS), f32), dma((12,))],
        aliases={7: 0},
    )(far, own_far, part_far, table, sums, base, h, x)
    return out_re, out_im


def solution(mesh):
    in_specs = (
        P(("row", "col"), None, None, None),
        P(("row", "col"), None, None, None),
        P(("row", "col"), None, None, None),
        P(("parts", "row", "col"), None, None, None),
        P("parts"),
        P(None, ("row", "col"), None),
    )
    out_specs = (
        P(("parts", "row", "col"), None, None, None),
        P(("parts", "row", "col"), None, None, None),
    )
    return jax.shard_map(body, mesh=mesh, in_specs=in_specs, out_specs=out_specs, check_vma=False)
```

```python
import functools

import jax
import jax.numpy as jnp
from jax import lax
from jax.experimental import pallas as pl
from jax.experimental.pallas import tpu as pltpu
from jax.sharding import PartitionSpec as P

TERMS = 6
BS = 128
time_step = 0.5
RING = ("row", "col")
f32, bf16 = jnp.float32, jnp.bfloat16

ROWS = 6
SIGN_RE = (1.0, -1.0, -1.0, 1.0, 1.0, -1.0)
SIGN_IM = (-1.0, -1.0, 1.0, 1.0, -1.0, -1.0)
FIRST_ROWS = 3 * BS + BS // 2 + 8
SECOND_ROWS = 2 * BS
MORE = 1
PART_ROWS = SECOND_ROWS + 2
FAR_PART_ROWS = SECOND_ROWS + 2
TABLE_ROWS = 24


def own_index(row, offset):
    core = lax.axis_index("col")
    return jnp.where(core == 0, row, 1 - row), jnp.where(core == 0, 1 + offset, 1 - offset)


def own(ref, row, offset):
    r, e = own_index(row, offset)
    return ref[r, e]


def slot(ref, index):
    return ref[index * BS : (index + 1) * BS, :]


def line(ref, index):
    return ref[index : index + 1, :]


class Band:
    def __init__(self, ref, negated=False):
        self.high, self.low = ref.at[0], ref.at[1]
        self.minus = Band(ref.at[pl.ds(2, 2)]) if negated else None

    def put(self, i, j, value):
        part = slice((j - i + 1) * BS, (j - i + 2) * BS)
        high = value.astype(bf16)
        low = (value - high.astype(f32)).astype(bf16)
        self.high[i, :, part] = high
        self.low[i, :, part] = low
        if self.minus is not None:
            self.minus.high[i, :, part] = -high
            self.minus.low[i, :, part] = -low

    def left(self, i, first, last):
        part = slice((first - i + 1) * BS, (last - i + 2) * BS)
        high, low = self.high[i, :, part], self.low[i, :, part]
        return [high, high, low]

    def right(self, first, last, j, j_last):
        highs, lows = [], []
        for k in range(first, last + 1):
            part = slice((j - k + 1) * BS, (j_last - k + 2) * BS)
            highs.append(self.high[k, :, part])
            lows.append(self.low[k, :, part])
        return highs + lows + highs


def piece(h, x, rows, mids, cols):
    after_h = jnp.concatenate(x.right(*mids, *cols), axis=0)
    after_x = jnp.concatenate(h.minus.right(*mids, *cols), axis=0)

    def product(left, right):
        return jnp.dot(jnp.concatenate(left, axis=1), right, preferred_element_type=f32)

    return [product(h.left(i, *mids), after_h) + product(x.left(i, *mids), after_x) for i in rows]


def one_side(a, b, row, mids, col):
    left = jnp.concatenate(a.left(row, *mids), axis=1)
    right = jnp.concatenate(b.right(*mids, col, col), axis=0)
    return jnp.dot(left, right, preferred_element_type=f32)


def tile(h, x, i):
    upper, lower = piece(h, x, (i, i + 1), (i, i + 1), (i, i + 1))
    return upper[:, :BS], upper[:, BS:], lower[:, :BS], lower[:, BS:]


def part(h, x, i, k, j):
    return piece(h, x, (i,), (k, k), (j, j))[0]


def half_places():
    shape = (BS // 2, BS)
    return lax.broadcasted_iota(jnp.int32, shape, 0), lax.broadcasted_iota(jnp.int32, shape, 1)


def swap_halves(rows):
    return jnp.concatenate([rows[:, BS // 2 :], rows[:, : BS // 2]], axis=1)


def put_symmetric(payload, block):
    r, c = half_places()
    turned = swap_halves(block[BS // 2 :])
    first = 3 * BS
    payload[first : first + BS // 2, :] = jnp.where(c < r, turned, block[: BS // 2])
    payload[first + BS // 2 : first + BS // 2 + 1, :] = jnp.sum(jnp.where(c == r, turned, 0.0), axis=0, keepdims=True)


def get_symmetric(payload):
    r, c = half_places()
    first = 3 * BS
    rows = payload[first : first + BS // 2, :]
    turned = jnp.concatenate([rows, rows], axis=0).T
    upper = jnp.where(c < r, turned[: BS // 2], rows)
    quarter = jnp.where(c < r, rows, turned[: BS // 2])
    quarter = jnp.where(c == r, line(payload, first + BS // 2), quarter)
    lower = jnp.where(c < BS // 2, turned[BS // 2 :], swap_halves(quarter))
    return jnp.concatenate([upper, lower], axis=0)


def coefficient(term):
    return time_step / (term + 1)


SUMS = ((1, 2, 1), (1, 1, 2), (1, 3, 4), (1, 4, 3), (2, 2, 2), (2, 3, 3), (3, 2, 2), (3, 3, 3), (3, 2, 3), (3, 3, 2))
OWN = (((0, -1), (2, 1)), ((0, 0), (2, 2)), ((0, 1), (2, 3)), ((1, -1), (3, 2)), ((1, 0), (3, 3)), ((1, 1), (3, 4)))
EARLY = ((1, 2, 2), (1, 3, 3), (1, 2, 3), (1, 3, 2))
LATE = ((1, 2, 1), (1, 1, 2), (2, 2, 1), (2, 1, 2), (3, 2, 1), (3, 1, 2), (2, 2, 2), (3, 2, 2), (3, 2, 3), (3, 3, 2))
DONE_EARLY = {(2, 2): (1,), (2, 3): (1, 2), (3, 2): (1, 2), (3, 3): (1,)}
DONE_NEAR = {(3, 3): (2, 3), (3, 4): (1, 2, 3)}
DONE_FAR = {(2, 1): (1, 2, 3), (2, 2): (2, 3), (2, 3): (3,), (3, 2): (3,)}


def weighted(terms_of, signs):
    total = None
    for sign, value in zip(signs, terms_of):
        total = (value if sign > 0 else -value) if total is None else (total + value if sign > 0 else total - value)
    return total


def parts_of(values, i, j, terms):
    re_signs, im_signs = [SIGN_RE[term] for term in terms], [SIGN_IM[term] for term in terms]
    here = [values[(term, i, j)] for term in terms]
    there = here if i == j else [values[(term, j, i)] for term in terms]
    real = 0.5 * (weighted(here, re_signs) + weighted(there, re_signs).T)
    imag = 0.5 * (weighted(here, im_signs) - weighted(there, im_signs).T)
    return real, imag


def add_terms(base, values, done, phase):
    for index, (_, (i, j)) in enumerate(OWN):
        terms = [level - 1 + 3 * phase for level in done.get((i, j), ())]
        if terms:
            real, imag = parts_of(values, i, j, terms)
            base[index, 0] = base[index, 0] + real
            base[index, 1] = base[index, 1] + imag


def views(h_ref, x_ref):
    return Band(h_ref, True), [Band(x_ref.at[level]) for level in range(3)]


def before_far(h, xs, phase, table, sums, early, far, carry):
    x0, x1, _ = xs
    term = 3 * phase
    t = tile(h, x0, 2)
    scale = line(table, 6 + term)
    inner = {
        (2, 2): (t[0] + part(h, x0, 2, 1, 2)) * coefficient(term),
        (2, 3): t[1] * scale,
        (3, 2): t[2] * scale,
    }
    for (i, j), value in inner.items():
        x1.put(i, j, value)
        early[EARLY.index((1, i, j))] = value
    carry[...] = t[3]
    first = 1 - phase
    far[first * BS : (first + 1) * BS, :] = inner[(2, 2)]
    value = part(h, x1, 2, 3, 2)
    far[(first + 1) * BS : (first + 2) * BS, :] = value
    sums[SUMS.index((2, 2, 2))] = value


def before_near_first(carry, h_ref, near_in, x_in, sums_in, early_in, near, x_ref, sums, early):
    before_near(carry, h_ref, x_ref, sums, early, near, 0)


def before_near_second(carry, h_ref, x_in, sums_in, early_in, near, x_ref, sums, early):
    before_near(carry, h_ref, x_ref, sums, early, near, 1)


def before_near(carry, h_ref, x_ref, sums, early, near, phase):
    h, (x0, x1, _) = views(h_ref, x_ref)
    first = 1 - phase
    value = (carry[...] + part(h, x0, 3, 4, 3)) * coefficient(3 * phase)
    x1.put(3, 3, value)
    early[EARLY.index((1, 3, 3))] = value
    near[first * BS : (first + 1) * BS, :] = value
    value = part(h, x1, 3, 2, 3)
    near[(first + 1) * BS : (first + 2) * BS, :] = value
    sums[SUMS.index((2, 3, 3))] = value


def own_first(
    re, im, ham, dip, pattern_in, field,
    far, near, table, h_ref, x_ref, sums, early, carry, re_in, im_in,
    ham_in, dip_in, pattern, sems,
):
    copies = [
        pltpu.make_async_copy(source, target, sems.at[n])
        for n, (source, target) in enumerate(
            ((pattern_in, pattern), (ham, ham_in), (dip, dip_in), (re, re_in), (im, im_in))
        )
    ]
    for copy in copies:
        copy.start()
    copies[0].wait()
    for n, (row, offset) in enumerate(((0, -1), (0, 1), (1, 1))):
        r, e = own_index(row, offset)
        for term in range(TERMS):
            table[6 * n + term : 6 * n + term + 1, :] = jnp.full(
                (1, BS), pattern[e, r, term].astype(f32) * coefficient(term), f32
            )
    h, xs = views(h_ref, x_ref)
    for copy in copies[1:3]:
        copy.wait()
    for (row, offset), (i, j) in OWN:
        value = own(ham_in, row, offset) + field[0] * own(dip_in, row, offset)
        h.put(i, j, value)
        if j in (1, 4):
            h.put(j, i, value.T)
        if i == j:
            put_symmetric(far if i == 2 else near, value)
    for copy in copies[3:]:
        copy.wait()
    for (row, offset), (i, j) in OWN:
        real, imag = own(re_in, row, offset), own(im_in, row, offset)
        xs[0].put(i, j, real + imag)
        if j in (1, 4):
            xs[0].put(j, i, (real - imag).T)
        if i == j:
            (far if i == 2 else near)[0:BS, :] = real + imag
    before_far(h, xs, 0, table, sums, early, far, carry)


def own_rest(h, xs, phase, table, early, base, sums):
    x0, x1, x2 = xs
    term = 3 * phase
    values = {(term, i, j): early[index] for index, (_, i, j) in enumerate(EARLY)}
    t = tile(h, x1, 2)
    scale = line(table, 6 + term + 1)
    for (i, j), value in (((2, 3), t[1] * scale), ((3, 2), t[2] * scale)):
        x2.put(i, j, value)
        values[(term + 1, i, j)] = value
    for a, b in ((3, 4), (2, 1)):
        sums[SUMS.index((1, a, b))] = part(h, x0, a, a, b)
        sums[SUMS.index((1, b, a))] = part(h, x0, b, a, a)
    sums[SUMS.index((3, 2, 2))] = part(h, x2, 2, 3, 2)
    sums[SUMS.index((3, 3, 3))] = part(h, x2, 3, 2, 3)
    add_terms(base, values, DONE_EARLY, phase)


def side(h, xs, a, b, start, payload, phase, scales, sums, record):
    x0, x1, x2 = xs
    c = [coefficient(3 * phase + n) for n in range(3)]
    low = min(a, b)
    at_a, at_b = (0, 3) if a == low else (3, 0)
    up, down = (low, low + 1), (low + 1, low)

    def known(level, i, j):
        return sums[SUMS.index((level, i, j))]

    def put(level, i, j, value):
        record(level, i, j, value)
        if level < 3:
            xs[level].put(i, j, value)

    first = 1 - phase
    x0.put(b, b, start)
    x1.put(b, b, slot(payload, first))
    put(1, a, b, (part(h, x0, a, b, b) + known(1, a, b)) * scales[0])
    put(1, b, a, (part(h, x0, b, b, a) + known(1, b, a)) * scales[0])
    t = tile(h, x1, low)
    put(2, a, a, (t[at_a] + known(2, a, a)) * c[1])
    put(2, b, b, (t[at_b] + slot(payload, first + 1)) * c[1])
    put(2, *up, t[1] * scales[1])
    put(2, *down, t[2] * scales[1])

    def last():
        row = piece(h, x2, (a,), (low, low + 1), (low, low + 1))[0]
        here, there = (row[:, :BS], row[:, BS:]) if a == low else (row[:, BS:], row[:, :BS])
        put(3, a, b, there * scales[2])
        put(3, a, a, (here + known(3, a, a)) * c[2])
        if phase:
            put(3, b, a, piece(h, x2, (b,), (low, low + 1), (a, a))[0] * scales[2])
            return None
        row = piece(h, x2, (b,), (low, low + 1), (low, low + 1))[0]
        here, there = (row[:, :BS], row[:, BS:]) if b == low else (row[:, BS:], row[:, :BS])
        put(3, b, a, there * scales[2])
        return here

    return last


def near_side(h, xs, start, near, phase, table, base, sums):
    term = 3 * phase
    values = {}

    def record(level, i, j, value):
        values[(term + level - 1, i, j)] = value

    scales = [line(table, 12 + term + n) for n in range(3)]
    own_part = side(h, xs, 3, 4, start, near, phase, scales, sums, record)()
    x2 = xs[2]
    sums[SUMS.index((3, 2, 3))] = one_side(h, x2, 2, (2, 3), 3) + one_side(x2, h.minus, 2, (3, 3), 3)
    sums[SUMS.index((3, 3, 2))] = one_side(h, x2, 3, (3, 3), 2) + one_side(x2, h.minus, 3, (2, 3), 2)
    add_terms(base, values, DONE_NEAR, phase)
    return values, own_part


def far_side(h, xs, start, far, phase, table, sums, record, between=lambda: None):
    term = 3 * phase
    scales = [line(table, term + n) for n in range(3)]
    last = side(h, xs, 2, 1, start, far, phase, scales, sums, record)
    x2 = xs[2]
    scale = line(table, 6 + term + 2)
    record(3, 2, 3, (one_side(x2, h.minus, 2, (2, 2), 3) + sums[SUMS.index((3, 2, 3))]) * scale)
    record(3, 3, 2, (one_side(h, x2, 3, (2, 2), 2) + sums[SUMS.index((3, 3, 2))]) * scale)
    between()
    return last()


def rest_first(re_in, im_in, table, early, h_ref, x_in, sums_in, x_ref, sums, base):
    h, xs = views(h_ref, x_ref)
    for index, ((row, offset), _) in enumerate(OWN):
        base[index, 0], base[index, 1] = own(re_in, row, offset), own(im_in, row, offset)
    own_rest(h, xs, 0, table, early, base, sums)


def near_first(
    near, table, h_in, x_in, sums_in, base_in, h_ref, x_ref, sums, base, own_part, part_far, part_near
):
    h, xs = views(h_ref, x_ref)
    h.put(4, 4, get_symmetric(near))
    values, own_part[...] = near_side(h, xs, slot(near, 0), near, 0, table, base, sums)
    for i, j in ((3, 3), (3, 4), (4, 3)):
        xs[0].put(i, j, values[(2, i, j)])
    part_far[0:BS, :] = sums[SUMS.index((3, 2, 2))]
    part_far[BS:, :] = jnp.zeros((FAR_PART_ROWS - BS, BS), f32)
    part_near[0:BS, :] = sums[SUMS.index((3, 3, 3))]
    part_near[BS:, :] = jnp.zeros((PART_ROWS - BS, BS), f32)


def far_first(far, table, h_in, x_in, sums_in, h_ref, x_ref, sums, late, early, far_next, own_part, carry):
    h, xs = views(h_ref, x_ref)
    h.put(1, 1, get_symmetric(far))
    state = {}

    def record(level, i, j, value):
        if (level, i, j) in LATE:
            late[LATE.index((level, i, j))] = value
        if level == 3:
            state[(i, j)] = value

    own_part[...] = far_side(h, xs, slot(far, 0), far, 0, table, sums, record)
    for (i, j), value in state.items():
        xs[0].put(i, j, value)
    before_far(h, xs, 1, table, sums, early, far_next, carry)


def rest_second(late, early, table, h_ref, x_in, sums_in, base_in, x_ref, sums, base):
    h, xs = views(h_ref, x_ref)
    values = {(level - 1, i, j): late[index] for index, (level, i, j) in enumerate(LATE)}
    add_terms(base, values, DONE_FAR, 0)
    own_rest(h, xs, 1, table, early, base, sums)


def near_second(near, own_part, part_near, table, h_ref, x_in, sums_in, base_in, x_ref, sums, base):
    h, xs = views(h_ref, x_ref)
    start = (own_part[...] + part_near[0:BS, :]) * coefficient(2)
    near_side(h, xs, start, near, 1, table, base, sums)


def far_second(far, own_part, part_far, table, sums, base, h_ref, x_in, x_ref, out_re, out_im, stage, sems):
    h, xs = views(h_ref, x_ref)
    copies = []
    for index, ((row, offset), _) in enumerate(OWN):
        r, e = own_index(row, offset)
        source = stage if index < 4 else base
        for a, out in enumerate((out_re, out_im)):
            copies.append(pltpu.make_async_copy(source.at[index, a], out.at[r, e], sems.at[len(copies)]))

    def send(first):
        for copy in copies[2 * first : 2 * first + (4 if first > 1 else 2)]:
            copy.start()

    def apart(first):
        pl.when(lax.axis_index("col") >= 0)(lambda: send(first))

    apart(4)
    values = {}

    def record(level, i, j, value):
        values[(level + 2, i, j)] = value

    def finish(index):
        i, j = OWN[index][1]
        real, imag = parts_of(values, i, j, [level + 2 for level in DONE_FAR[(i, j)]])
        stage[index, 0], stage[index, 1] = base[index, 0] + real, base[index, 1] + imag

    def between():
        finish(2)
        finish(3)
        apart(2)

    start = (own_part[...] + part_far[0:BS, :]) * coefficient(2)
    far_side(h, xs, start, far, 1, table, sums, record, between)
    finish(1)
    send(1)
    finish(0)
    send(0)
    for copy in copies:
        copy.wait()


VECTOR = pl.BlockSpec(memory_space=pltpu.VMEM)
SCALAR = pl.BlockSpec(memory_space=pltpu.SMEM)
BIG = pl.BlockSpec(memory_space=pltpu.HBM)


def call(kernel, ins, outs, scratch=(), aliases=None):
    return pl.pallas_call(
        kernel,
        out_shape=[shape for shape, _ in outs],
        in_specs=ins,
        out_specs=[spec for _, spec in outs],
        scratch_shapes=list(scratch),
        input_output_aliases=aliases or {},
        compiler_params=pltpu.CompilerParams(vmem_limit_bytes=24 * 2**20),
        cost_estimate=pl.CostEstimate(flops=0, bytes_accessed=0, transcendentals=0),
    )


def vector(*shape, dtype=f32):
    return jax.ShapeDtypeStruct(shape, dtype), VECTOR


def body(density_real, density_imag, hamiltonian, dipole, field, pattern):
    count = lax.axis_size(RING)
    pair = [(i, i ^ 1) for i in range(count)]
    cross = [(i, (i + 1) % count if i % 2 else (i - 1) % count) for i in range(count)]
    pattern = jnp.transpose(pattern, (2, 1, 0))
    whole = density_real.shape
    inputs = [
        pltpu.with_memory_space_constraint(x, pltpu.HBM)
        for x in (density_real, density_imag, hamiltonian, dipole, pattern)
    ]
    dma = pltpu.SemaphoreType.DMA
    h_out, x_out = vector(4, ROWS, BS, 3 * BS, dtype=bf16), vector(3, 2, ROWS, BS, 3 * BS, dtype=bf16)
    base_out, sums_out = vector(len(OWN), 2, BS, BS), vector(len(SUMS), BS, BS)
    carry_out, early_out, late_out = vector(BS, BS), vector(len(EARLY), BS, BS), vector(len(LATE), BS, BS)
    out = (jax.ShapeDtypeStruct(whole, f32), BIG)

    far, near, table, h, x, sums, early, carry, re_in, im_in = call(
        own_first,
        [BIG] * 5 + [SCALAR],
        [
            vector(FIRST_ROWS + 2 * MORE, BS),
            vector(FIRST_ROWS, BS),
            vector(TABLE_ROWS, BS),
            h_out,
            x_out,
            sums_out,
            early_out,
            carry_out,
            vector(*whole),
            vector(*whole),
        ],
        [pltpu.VMEM(whole, f32)] * 2 + [pltpu.SMEM(pattern.shape, jnp.int32), dma((5,))],
    )(*inputs, field)
    far = lax.ppermute(far, RING, cross)
    near, x, sums, early = call(
        before_near_first,
        [VECTOR] * 6,
        [vector(FIRST_ROWS, BS), x_out, sums_out, early_out],
        aliases={2: 0, 3: 1, 4: 2, 5: 3},
    )(carry, h, near, x, sums, early)
    near = lax.ppermute(near, RING, pair)
    x, sums, base = call(
        rest_first,
        [VECTOR] * 7,
        [x_out, sums_out, base_out],
        aliases={5: 0, 6: 1},
    )(re_in, im_in, table, early, h, x, sums)
    h, x, sums, base, own_near, part_far, part_near = call(
        near_first,
        [VECTOR] * 6,
        [h_out, x_out, sums_out, base_out, carry_out, vector(FAR_PART_ROWS, BS), vector(PART_ROWS, BS)],
        aliases={2: 0, 3: 1, 4: 2, 5: 3},
    )(near, table, h, x, sums, base)
    part_far = lax.ppermute(part_far, RING, cross)
    part_near = lax.ppermute(part_near, RING, pair)
    h, x, sums, late, early, far, own_far, carry = call(
        far_first,
        [VECTOR] * 5,
        [
            h_out,
            x_out,
            sums_out,
            late_out,
            early_out,
            vector(SECOND_ROWS + MORE, BS),
            carry_out,
            carry_out,
        ],
        aliases={2: 0, 3: 1, 4: 2},
    )(far, table, h, x, sums)
    far = lax.ppermute(far, RING, cross)
    near, x, sums, early = call(
        before_near_second,
        [VECTOR] * 5,
        [vector(SECOND_ROWS, BS), x_out, sums_out, early_out],
        aliases={2: 1, 3: 2, 4: 3},
    )(carry, h, x, sums, early)
    near = lax.ppermute(near, RING, pair)
    x, sums, base = call(
        rest_second,
        [VECTOR] * 7,
        [x_out, sums_out, base_out],
        aliases={4: 0, 5: 1, 6: 2},
    )(late, early, table, h, x, sums, base)
    x, sums, base = call(
        near_second,
        [VECTOR] * 8,
        [x_out, sums_out, base_out],
        aliases={5: 0, 6: 1, 7: 2},
    )(near, own_near, part_near, table, h, x, sums, base)
    _, out_re, out_im = call(
        far_second,
        [VECTOR] * 8,
        [x_out, out, out],
        [pltpu.VMEM((4, 2, BS, BS), f32), dma((12,))],
        aliases={7: 0},
    )(far, own_far, part_far, table, sums, base, h, x)
    return out_re, out_im


def solution(mesh):
    in_specs = (
        P(("row", "col"), None, None, None),
        P(("row", "col"), None, None, None),
        P(("row", "col"), None, None, None),
        P(("parts", "row", "col"), None, None, None),
        P("parts"),
        P(None, ("row", "col"), None),
    )
    out_specs = (
        P(("parts", "row", "col"), None, None, None),
        P(("parts", "row", "col"), None, None, None),
    )
    return jax.shard_map(body, mesh=mesh, in_specs=in_specs, out_specs=out_specs, check_vma=False)
```
